512 devices in a mesh: fx: 16 (over x, y_lo), fy: 16 (over z, core), sec: 2 (over y_hi).
Axes of the slice: x: 4, y: 8 (y_hi: 2, y_lo: 4; y = y_hi * 4 + y_lo), z: 8, core: 2. Of those that a mesh axis runs over, the one named last changes fastest.
Arguments:
- state: float32 [5, 32, 512, 256], P(None, 'fx', 'fy', 'sec'), may hold values from -6 to 6
- mixing: float32 [5, 5], replicated, may hold values from -2.5 to 2.5
- wall_weight: float32 [32, 16, 256], P('fx', 'fy', 'sec'), may hold values from 0.05 to 0.4
- patch_map: int32 [32, 16, 2, 1], P('fx', 'fy', 'sec'), may hold values from 0 to 15
- block_map: int32 [32, 16, 2, 1], P('fx', 'fy', 'sec'), may hold values from 0 to 31
- shell_disp: float32 [16, 4096], P('fx'), may hold values from -6 to 6
- shell_vel: float32 [16, 4096], P('fx'), may hold values from -6 to 6
- connect: int32 [16, 64, 2], P('fx'), may hold values from 0 to 31
- stiffness: float32 [16, 64, 128], P('fx'), may hold values from 0.25 to 1
Outputs:
- new_state: float32 [5, 32, 512, 256], P(None, 'fx', 'fy', 'sec')
- new_disp: float32 [16, 4096], P('fx')
- new_vel: float32 [16, 4096], P('fx')
The draws below stay inside these ranges and needn't reach their ends.
Inputs may be any that keep to these rules, and one draw needn't show every extreme that they name: `patch_map`: every patch is named by some tile; some patches are named far more often than others. `connect`: block indices within one patch.
All inputs are finite; a program needn't handle non-finite values.
Results may differ from the reference program's by a relative error of at most 0.0001.
Values sent between devices are 32-bit elements; how exact they have to be, the bound alone decides.
No kernel may reach another device: no remote copies, remote signals or barrier semaphores. Data moves between devices by JAX's collectives and lax.ppermute only.
A program may use at most 64 MiB of HBM per device.

```python
import math
import jax
import jax.numpy as jnp
from jax import lax

NVAR = 5
CY = 32
CZ = 128
NB = 32
SUBCYCLES = 4
NP = 16
SD = 4096
NE = 64
NX = 32
NY = 512
NZ = 256
N_FY = 16
N_SEC = 2


def with_ends(drawn, stream_key, low, high):
    longest = drawn.shape.index(max(drawn.shape))
    spots = []
    for shift in (0, 1):
        where = [jax.random.randint(jax.random.fold_in(stream_key, axis), (), 0, length) for axis, length in enumerate(drawn.shape)]
        where[longest] = (where[longest] + shift) % drawn.shape[longest]
        spots.append(tuple(where))
    return drawn.at[spots[0]].set(low).at[spots[1]].set(high)


def level_of(stream_key, dims, pieces, low, high):
    loudness, own = 1.0, jax.random.fold_in(stream_key, 6)
    for position, blocks in pieces:
        steps = jnp.exp(jax.random.uniform(jax.random.fold_in(own, position), (blocks,), jnp.float32, low / len(pieces), high / len(pieces)))
        loudness = loudness * jnp.repeat(steps, dims[position] // blocks).reshape([-1 if axis == position else 1 for axis in range(len(dims))])
    return loudness


def different_ones(rng, rows, count, top, lift):
    ranking = jax.random.permutation(jax.random.fold_in(rng, 1), count)
    favour = ranking
    for power in range(3):
        favour = favour * favour // count
    favour = favour * lift // count
    lots = jax.random.randint(jax.random.fold_in(rng, 2), (rows, count), 0, 4096) + favour
    sure = jax.random.permutation(jax.random.fold_in(rng, 3), rows)[jnp.arange(count) % rows]
    lots = jnp.where(jnp.arange(rows)[:, None] == sure[None, :], 1 << 14, lots)
    priority = lots * count + jnp.arange(count)
    return lax.top_k(priority.astype(jnp.int32), top)[1].astype(jnp.int32)


def normal_values(stream_key, dims, spread, most, split=(), dtype=jnp.bfloat16):
    entries = jax.random.normal(stream_key, dims, jnp.float32) * spread
    if len(split) > 0:
        entries = level_of(stream_key, dims, split, -0.22, 0.18) * entries
    return jnp.clip(entries, min=-most, max=most).astype(dtype)


def setup_inputs(seed: int = 0) -> dict:
    key_of = jax.random.split(jax.random.key(seed), 10)
    state = normal_values(key_of[0], (NVAR, NX, NY, NZ), 1.0, 6.0, ((1, 16), (2, 16), (3, 2)), jnp.float32)
    mixing = normal_values(key_of[1], (NVAR, NVAR), NVAR ** -0.5, 2.5, (), jnp.float32)
    wall_weight = jnp.clip(0.05 + 0.35 * jax.random.uniform(key_of[2], (NX, N_FY, NZ), jnp.float32) ** level_of(key_of[2], (NX, N_FY, NZ), ((0, 16), (1, 16), (2, 2)), -0.2, 0.2), 0.05, 0.4)
    patch_map = different_ones(key_of[3], NX * N_FY * N_SEC, NP, 1, 1024).reshape((NX, N_FY, N_SEC, 1))
    block_map = with_ends(jax.random.randint(key_of[4], (NX, N_FY, N_SEC, 1), 0, NB), jax.random.fold_in(key_of[4], 1), 0, NB - 1).astype(jnp.int32)
    shell_disp = normal_values(key_of[5], (NP, SD), 0.5, 6.0, ((0, 16),), jnp.float32)
    shell_vel = normal_values(key_of[6], (NP, SD), 0.5, 6.0, ((0, 16),), jnp.float32)
    connect = with_ends(jax.random.randint(key_of[7], (NP, NE, 2), 0, NB), jax.random.fold_in(key_of[7], 1), 0, NB - 1).astype(jnp.int32)
    stiffness = jnp.clip(jnp.exp(math.log(1.0) - 1.3862944 * jax.random.uniform(key_of[8], (NP, NE, CZ), jnp.float32) ** level_of(key_of[8], (NP, NE, CZ), ((0, 16),), -0.2, 0.2)), 0.25, 1.0)
    return dict(state=state, mixing=mixing, wall_weight=wall_weight, patch_map=patch_map, block_map=block_map, shell_disp=shell_disp, shell_vel=shell_vel, connect=connect, stiffness=stiffness)


DIFFUSION = 0.25
TRANSPORT = 0.5
TIME_STEP = 0.2
SHELL_STEP = 0.25
DAMPING = 0.1


def rate_of(padded, mixing):
    center = padded[:, 1:-1, 1:-1, 1:-1]
    ahead = padded[:, 2:, 1:-1, 1:-1]
    behind = padded[:, :-2, 1:-1, 1:-1]
    beside = ahead + behind + padded[:, 1:-1, 2:, 1:-1] + padded[:, 1:-1, :-2, 1:-1]
    beside = beside + padded[:, 1:-1, 1:-1, 2:] + padded[:, 1:-1, 1:-1, :-2]
    mixed = jnp.einsum("vw,wxyz->vxyz", mixing, center, precision=lax.Precision.HIGHEST)
    return DIFFUSION * (beside - 6.0 * center) - TRANSPORT * 0.5 * (ahead - behind) + mixed


def fluid_rate(field, mixing):
    return rate_of(jnp.pad(field, ((0, 0), (1, 1), (1, 1), (1, 1))), mixing)


def shell_cycles(load, disp, vel, pairs, stiff):
    first = pairs[:, 0]
    second = pairs[:, 1]
    width = stiff.shape[1]
    count = disp.shape[0] // width
    load = load.reshape(count, width)
    disp = disp.reshape(count, width)
    vel = vel.reshape(count, width)
    samples = []
    for cycle in range(SUBCYCLES):
        stretch = stiff * (disp[first] - disp[second])
        inner = jax.ops.segment_sum(stretch, first, num_segments=count) - jax.ops.segment_sum(stretch, second, num_segments=count)
        vel = vel + SHELL_STEP * (load - inner - DAMPING * vel)
        disp = disp + SHELL_STEP * vel
        samples.append(disp.reshape(-1))
    return disp.reshape(-1), vel.reshape(-1), jnp.stack(samples)


def reference(state, mixing, wall_weight, patch_map, block_map, shell_disp, shell_vel, connect, stiffness):
    pressure = state[4, :, ::CY, :]
    tile_load = (wall_weight * pressure).reshape(NX * N_FY * N_SEC, CZ)
    target = (patch_map.reshape(-1) * NB + block_map.reshape(-1)).astype(jnp.int32)
    loads = jax.ops.segment_sum(tile_load, target, num_segments=NP * NB).reshape(NP, NB * CZ)
    new_disp, new_vel, samples = jax.vmap(shell_cycles)(loads, shell_disp, shell_vel, connect, stiffness)
    wall = jnp.mean(samples, 1).reshape(NP * NB, CZ)
    wall_tiles = wall[target].reshape(NX, N_FY, NZ)
    first_rate = fluid_rate(state, mixing)
    section = state + TIME_STEP * first_rate
    second_rate = fluid_rate(section, mixing)
    new_state = state + 0.5 * TIME_STEP * (first_rate + second_rate)
    new_state = new_state.at[2, :, ::CY, :].add(wall_weight * wall_tiles)
    return new_state, new_disp, new_vel
```

```python
import jax
import jax.numpy as jnp
from jax import lax
from jax.experimental import pallas as pl
from jax.experimental.pallas import tpu as pltpu
from jax.sharding import PartitionSpec as P

NV = 5
NB = 32
SUBCYCLES = 4
LANES = 128

DIFFUSION = 0.25
TRANSPORT = 0.5
TIME_STEP = 0.2
SHELL_STEP = 0.25
DAMPING = 0.1

TOP = 8
ROWS = 48

VM = pl.BlockSpec(memory_space=pltpu.VMEM)
SM = pl.BlockSpec(memory_space=pltpu.SMEM)


def kernel_call(body, outs, ins, scratch=(), cost=20000):
    return pl.pallas_call(
        body,
        out_shape=outs,
        in_specs=ins,
        out_specs=jax.tree.map(lambda _: VM, outs),
        scratch_shapes=scratch,
        cost_estimate=pl.CostEstimate(flops=cost, bytes_accessed=cost, transcendentals=0),
    )


def f32(*shape):
    return jax.ShapeDtypeStruct(shape, jnp.float32)


def offer_body(patch_ref, block_ref, weight_ref, state_ref, out_ref):
    rows = []
    for tile in range(2):
        rows.append(weight_ref[tile] * state_ref[0, tile, 0:1, :])
    for tile in range(2):
        target = patch_ref[tile, 0, 0, 0] * NB + block_ref[tile, 0, 0, 0]
        rows.append(jnp.full((1, LANES), target.astype(jnp.float32)))
    rows = jnp.concatenate(rows, axis=0)
    for receiver in range(out_ref.shape[0]):
        out_ref[receiver] = rows


def offer(patch_map, block_map, weight, state, receivers):
    return pl.pallas_call(
        offer_body,
        grid=(1,),
        out_shape=f32(receivers, 4, LANES),
        in_specs=[
            SM,
            SM,
            pl.BlockSpec((2, 1, LANES), lambda i: (0, 0, 0)),
            pl.BlockSpec((1, 2, 8, LANES), lambda i: (4, 0, 0, 0)),
        ],
        out_specs=pl.BlockSpec((receivers, 4, LANES), lambda i: (0, 0, 0)),
        cost_estimate=pl.CostEstimate(flops=4096, bytes_accessed=65536, transcendentals=0),
    )(patch_map, block_map, weight, state)


def collect_body(tiles_ref, out_ref):
    base = (lax.axis_index("fx") * NB).astype(jnp.float32)
    block = lax.broadcasted_iota(jnp.int32, (NB, LANES), 0).astype(jnp.float32) + base
    sums = [jnp.zeros((NB, LANES), jnp.float32) for _ in range(4)]
    for sender in range(tiles_ref.shape[0]):
        for tile in range(2):
            load = tiles_ref[sender, tile : tile + 1, :]
            target = tiles_ref[sender, 2 + tile : 3 + tile, :]
            slot = (2 * sender + tile) % 4
            sums[slot] = sums[slot] + jnp.where(block == target, load, 0.0)
    total = (sums[0] + sums[1]) + (sums[2] + sums[3])
    for receiver in range(out_ref.shape[0]):
        out_ref[receiver] = total


def pieces(x):
    high = x.astype(jnp.bfloat16)
    rest = x - high.astype(jnp.float32)
    middle = rest.astype(jnp.bfloat16)
    low = (rest - middle.astype(jnp.float32)).astype(jnp.bfloat16)
    return jnp.concatenate([high, middle, low], axis=0)


def thrice(select):
    select = select.astype(jnp.bfloat16)
    return jnp.concatenate([select, select, select], axis=1)


def picked(select3, x):
    return jnp.dot(select3, pieces(x), preferred_element_type=jnp.float32)


def shell_body(
    loads_ref, tiles_ref, disp_ref, vel_ref, connect_ref, stiff_ref, disp_out, vel_out, wall_out
):
    elements = stiff_ref.shape[0]
    lane = lax.broadcasted_iota(jnp.int32, (elements, LANES), 1)
    first = connect_ref[:, 0:1]
    second = connect_ref[:, 1:2]
    ends = (lane == first).astype(jnp.float32) - (lane == second).astype(jnp.float32)
    gather = thrice(ends[:, :NB])
    scatter = thrice(ends.T[:NB, :])

    base = (lax.axis_index("fx") * NB).astype(jnp.float32)
    sec = lax.axis_index("sec")
    peers = wall_out.shape[0]
    targets = [
        tiles_ref[2 * peer + sec, 2 + tile : 3 + tile, :]
        for peer in range(peers)
        for tile in range(2)
    ]
    targets = jnp.concatenate(targets, axis=0)[:, :NB]
    block = lax.broadcasted_iota(jnp.int32, (2 * peers, NB), 1).astype(jnp.float32) + base
    wanted = thrice((block == targets).astype(jnp.float32))

    stiff = stiff_ref[...]
    disp = disp_ref[...]
    vel = vel_ref[...]
    load = loads_ref[0]
    for sender in range(1, loads_ref.shape[0]):
        load = load + loads_ref[sender]
    total = jnp.zeros_like(disp)
    for _ in range(SUBCYCLES):
        stretch = stiff * picked(gather, disp)
        inner = picked(scatter, stretch)
        vel = vel + SHELL_STEP * (load - inner - DAMPING * vel)
        disp = disp + SHELL_STEP * vel
        total = total + disp
    disp_out[...] = disp
    vel_out[...] = vel
    wall = picked(wanted, total * (1.0 / SUBCYCLES))
    for peer in range(peers):
        wall_out[peer] = wall[2 * peer : 2 * peer + 2, :]


def finish_body(walls_ref, weight_ref, state_ref, out_ref):
    wall = walls_ref[0]
    for owner in range(1, walls_ref.shape[0]):
        wall = wall + walls_ref[owner]
    row = lax.broadcasted_iota(jnp.int32, (8, LANES), 0)
    for tile in range(2):
        gain = weight_ref[tile] * wall[tile : tile + 1, :]
        out_ref[0, tile] = state_ref[0, tile] + jnp.where(row == 0, gain, 0.0)


def finish(walls, weight, state):
    owners = walls.shape[0]
    part = pl.BlockSpec((1, 2, 8, LANES), lambda i: (2, 0, 0, 0))
    return pl.pallas_call(
        finish_body,
        grid=(1,),
        out_shape=f32(*state.shape),
        in_specs=[
            pl.BlockSpec((owners, 2, LANES), lambda i: (0, 0, 0)),
            pl.BlockSpec((2, 1, LANES), lambda i: (0, 0, 0)),
            part,
        ],
        out_specs=part,
        input_output_aliases={2: 0},
        cost_estimate=pl.CostEstimate(flops=4096, bytes_accessed=65536, transcendentals=0),
    )(walls, weight, state)


def slab(low_ref, state_ref, high_ref, v, xi):
    if xi == 0:
        return low_ref.at[v, 1]
    if xi == 3:
        return high_ref.at[v, 0]
    return state_ref.at[v, xi - 1]


def pack_sec_body(low_ref, state_ref, high_ref, out_ref):
    sec = lax.axis_index("sec")
    lane = lax.broadcasted_iota(jnp.int32, (32, LANES), 1)
    packed = jnp.zeros((32, LANES), jnp.float32)
    for v in range(NV):
        for xi in range(4):
            first = 8 * v + 2 * xi
            moved = pltpu.roll(
                slab(low_ref, state_ref, high_ref, v, xi)[...], first + 2 * (1 - sec), axis=1
            )
            packed = jnp.where((lane == first) | (lane == first + 1), moved, packed)
    out_ref[...] = packed


def pack_span_body(low_ref, state_ref, high_ref, beyond_ref, top_ref, bottom_ref):
    last = state_ref.shape[2] - 1
    for out, rows in ((top_ref, (0, 1)), (bottom_ref, (last, last - 1))):
        for place, y in enumerate(rows):
            for v in range(NV):
                for xi in range(4):
                    spot = 8 * v + 4 * place + xi
                    out[spot : spot + 1, :] = slab(low_ref, state_ref, high_ref, v, xi)[
                        y : y + 1, :
                    ]
            out[8 * NV + place : 8 * NV + place + 1, :] = beyond_ref[y : y + 1, :]
        out[8 * NV + 2 :, :] = jnp.zeros((6, LANES), jnp.float32)


def stencil(center, ahead, behind, others, mixed):
    beside = ahead + behind + others
    return DIFFUSION * (beside - 6.0 * center) - TRANSPORT * 0.5 * (ahead - behind) + mixed


def fluid_body(
    mixing_ref,
    low_ref,
    state_ref,
    high_ref,
    edge_ref,
    beyond_ref,
    top_ref,
    bottom_ref,
    before_ref,
    after_ref,
    out_ref,
    field,
    section,
    packed,
):
    size = state_ref.shape[2]
    end = TOP + size
    sec = lax.axis_index("sec")
    fx = lax.axis_index("fx")
    fy = lax.axis_index("fy")
    inside_low = (fx > 0).astype(jnp.float32)
    inside_high = (fx < lax.axis_size("fx") - 1).astype(jnp.float32)
    inside_before = (fy > 0).astype(jnp.float32)
    inside_after = (fy < lax.axis_size("fy") - 1).astype(jnp.float32)
    mix = [[mixing_ref[v, w] for w in range(NV)] for v in range(NV)]

    lane = lax.broadcasted_iota(jnp.int32, (1, LANES), 1)
    open_lane = (LANES - 1) * (1 - sec)
    keep_low = (lane != 0).astype(jnp.float32)
    keep_high = (lane != LANES - 1).astype(jnp.float32)
    at_open = (lane == open_lane).astype(jnp.float32)

    def along_z(cells, columns, v, xi):
        moved = pltpu.roll(columns, LANES - 1 - (8 * v + 2 * xi), axis=1)
        return (
            keep_low * pltpu.roll(cells, 1, axis=1)
            + keep_high * pltpu.roll(cells, LANES - 1, axis=1)
            + at_open * moved
        )

    def mixed(cells, v):
        total = mix[v][0] * cells[0]
        for w in range(1, NV):
            total = total + mix[v][w] * cells[w]
        return total

    packed[TOP:end, :] = beyond_ref[...]
    packed[TOP - 1 : TOP, :] = before_ref[8 * NV : 8 * NV + 1, :]
    packed[end : end + 1, :] = after_ref[8 * NV : 8 * NV + 1, :]
    beyond = beyond_ref[...]
    group = lane // 8
    mixed_columns = jnp.zeros((size, LANES), jnp.float32)
    for shift in range(1 - NV, NV):
        factor = jnp.zeros((1, LANES), jnp.float32)
        for v in range(NV):
            if 0 <= v - shift < NV:
                factor = jnp.where(group == v, mix[v][v - shift], factor)
        source = beyond if shift == 0 else pltpu.roll(beyond, (8 * shift) % LANES, axis=1)
        mixed_columns = mixed_columns + factor * source
    column_rate = stencil(
        beyond,
        pltpu.roll(beyond, LANES - 2, axis=1),
        pltpu.roll(beyond, 2, axis=1),
        packed[TOP - 1 : end - 1, :]
        + packed[TOP + 1 : end + 1, :]
        + pltpu.roll(beyond + edge_ref[...], 1 + (LANES - 2) * (1 - sec), axis=1),
        mixed_columns,
    )
    column_section = beyond + TIME_STEP * column_rate

    row = lax.broadcasted_iota(jnp.int32, (8, LANES), 0)
    inside_rows = jnp.where(row < 4, inside_before, inside_after)
    row_cells = []
    row_others = []
    row_columns = jnp.where(
        row < 4, before_ref[8 * NV : 8 * NV + 1, :], after_ref[8 * NV : 8 * NV + 1, :]
    )
    for v in range(NV):
        cells = jnp.concatenate(
            [before_ref[8 * v : 8 * v + 4, :], after_ref[8 * v : 8 * v + 4, :]], axis=0
        )
        outer = jnp.concatenate(
            [before_ref[8 * v + 4 : 8 * v + 8, :], after_ref[8 * v + 4 : 8 * v + 8, :]], axis=0
        )
        inner = jnp.concatenate(
            [top_ref[8 * v : 8 * v + 4, :], bottom_ref[8 * v : 8 * v + 4, :]], axis=0
        )
        columns = jnp.zeros((8, LANES), jnp.float32)
        for xi in (1, 2):
            moved = pltpu.roll(row_columns, LANES - 1 - (8 * v + 2 * xi), axis=1)
            columns = jnp.where((row == xi) | (row == 4 + xi), moved, columns)
        across = (
            keep_low * pltpu.roll(cells, 1, axis=1)
            + keep_high * pltpu.roll(cells, LANES - 1, axis=1)
            + at_open * columns
        )
        row_cells.append(cells)
        row_others.append(outer + inner + across)
    for v in range(NV):
        cells = row_cells[v]
        rate = stencil(
            cells,
            pltpu.roll(cells, 7, axis=0),
            pltpu.roll(cells, 1, axis=0),
            row_others[v],
            mixed(row_cells, v),
        )
        after = inside_rows * (cells + TIME_STEP * rate)
        for xi in (1, 2):
            section[v, xi, TOP - 1 : TOP, :] = after[xi : xi + 1, :]
            section[v, xi, end : end + 1, :] = after[4 + xi : 5 + xi, :]

    for v in range(NV):
        for xi in range(4):
            field[v, xi, TOP:end, :] = slab(low_ref, state_ref, high_ref, v, xi)[...]
            field[v, xi, TOP - 1 : TOP, :] = before_ref[8 * v + xi : 8 * v + xi + 1, :]
            field[v, xi, end : end + 1, :] = after_ref[8 * v + xi : 8 * v + xi + 1, :]

    def center(v, x):
        if x < 0:
            return low_ref[v, 0]
        if x > 3:
            return high_ref[v, 1]
        return field[v, x, TOP:end, :]

    for xi in range(4):
        cells = [center(w, xi) for w in range(NV)]
        for v in range(NV):
            others = (
                field[v, xi, TOP - 1 : end - 1, :]
                + field[v, xi, TOP + 1 : end + 1, :]
                + along_z(cells[v], beyond, v, xi)
            )
            rate = stencil(
                cells[v], center(v, xi + 1), center(v, xi - 1), others, mixed(cells, v)
            )
            after = cells[v] + TIME_STEP * rate
            if xi == 0:
                after = inside_low * after
            if xi == 3:
                after = inside_high * after
            section[v, xi, TOP:end, :] = after
            if xi in (1, 2):
                out_ref[v, xi - 1] = cells[v] + 0.5 * TIME_STEP * rate

    for xi in (1, 2):
        cells = [section[w, xi, TOP:end, :] for w in range(NV)]
        for v in range(NV):
            others = (
                section[v, xi, TOP - 1 : end - 1, :]
                + section[v, xi, TOP + 1 : end + 1, :]
                + along_z(cells[v], column_section, v, xi)
            )
            rate = stencil(
                cells[v],
                section[v, xi + 1, TOP:end, :],
                section[v, xi - 1, TOP:end, :],
                others,
                mixed(cells, v),
            )
            out_ref[v, xi - 1] = out_ref[v, xi - 1] + 0.5 * TIME_STEP * rate


def shards(
    state, mixing, wall_weight, patch_map, block_map, shell_disp, shell_vel, connect, stiffness
):
    nfx, nfy, nsec = (lax.axis_size(axis) for axis in ("fx", "fy", "sec"))
    up_x = [(i, i + 1) for i in range(nfx - 1)]
    down_x = [(i + 1, i) for i in range(nfx - 1)]
    up_y = [(i, i + 1) for i in range(nfy - 1)]
    down_y = [(i + 1, i) for i in range(nfy - 1)]

    offered = offer(patch_map, block_map, wall_weight, state, nfx * nsec)
    tiles = lax.all_to_all(offered, ("fx", "sec"), 0, 0, tiled=True)

    low = lax.ppermute(state, "fx", up_x)
    high = lax.ppermute(state, "fx", down_x)

    partial = kernel_call(collect_body, f32(nfy, NB, LANES), [VM])(tiles)
    loads = lax.all_to_all(partial, "fy", 0, 0, tiled=True)

    edge = kernel_call(pack_sec_body, f32(32, LANES), [VM] * 3)(low, state, high)
    beyond = lax.ppermute(edge, "sec", [(0, 1), (1, 0)])
    span = f32(8 * NV + 8, LANES)
    top, bottom = kernel_call(pack_span_body, (span, span), [VM] * 4)(low, state, high, beyond)
    before = lax.ppermute(bottom, "fy", up_y)
    after = lax.ppermute(top, "fy", down_y)

    new_disp, new_vel, walls = kernel_call(
        shell_body, (f32(NB, LANES), f32(NB, LANES), f32(nfx, 2, LANES)), [VM] * 6
    )(
        loads,
        tiles,
        shell_disp.reshape(NB, LANES),
        shell_vel.reshape(NB, LANES),
        connect[0],
        stiffness[0],
    )
    walls = lax.all_to_all(walls, "fx", 0, 0, tiled=True)

    fluid = kernel_call(
        fluid_body,
        f32(*state.shape),
        [SM] + [VM] * 9,
        scratch=[
            pltpu.VMEM((NV, 4, ROWS, LANES), jnp.float32),
            pltpu.VMEM((NV, 4, ROWS, LANES), jnp.float32),
            pltpu.VMEM((ROWS, LANES), jnp.float32),
        ],
    )(mixing, low, state, high, edge, beyond, top, bottom, before, after)
    new_state = finish(walls, wall_weight, fluid)
    return (new_state, new_disp.reshape(1, -1), new_vel.reshape(1, -1))


def solution(mesh):
    return jax.shard_map(
        shards,
        mesh=mesh,
        in_specs=(
            P(None, "fx", "fy", "sec"),
            P(),
            P("fx", "fy", "sec"),
            P("fx", "fy", "sec", None),
            P("fx", "fy", "sec", None),
            P("fx", None),
            P("fx", None),
            P("fx", None, None),
            P("fx", None, None),
        ),
        out_specs=(P(None, "fx", "fy", "sec"), P("fx", None), P("fx", None)),
        check_vma=False,
    )
```

```python
import jax
import jax.numpy as jnp
from jax import lax
from jax.experimental import pallas as pl
from jax.experimental.pallas import tpu as pltpu
from jax.sharding import PartitionSpec as P

NV = 5
NB = 32
SUBCYCLES = 4
LANES = 128

DIFFUSION = 0.25
TRANSPORT = 0.5
TIME_STEP = 0.2
SHELL_STEP = 0.25
DAMPING = 0.1

TOP = 8
ROWS = 48

VM = pl.BlockSpec(memory_space=pltpu.VMEM)
SM = pl.BlockSpec(memory_space=pltpu.SMEM)
ANY = pl.BlockSpec(memory_space=pl.ANY)
SMALL = pltpu.CompilerParams(vmem_limit_bytes=8 * 1024 * 1024)


def kernel_call(body, outs, ins, scratch=(), cost=20000):
    return pl.pallas_call(
        body,
        out_shape=outs,
        in_specs=ins,
        out_specs=jax.tree.map(lambda _: VM, outs),
        scratch_shapes=scratch,
        compiler_params=SMALL,
        cost_estimate=pl.CostEstimate(flops=cost, bytes_accessed=cost, transcendentals=0),
    )


def f32(*shape):
    return jax.ShapeDtypeStruct(shape, jnp.float32)


def offer_body(patch_ref, block_ref, weight_ref, state_ref, out_ref):
    rows = []
    for tile in range(2):
        rows.append(weight_ref[tile] * state_ref[0, tile, 0:1, :])
    for tile in range(2):
        target = patch_ref[tile] * NB + block_ref[tile]
        rows.append(jnp.full((1, LANES), target.astype(jnp.float32)))
    rows = jnp.concatenate(rows, axis=0)
    for receiver in range(out_ref.shape[0]):
        out_ref[receiver] = rows


def offer(patch_map, block_map, weight, state, receivers):
    return pl.pallas_call(
        offer_body,
        grid=(1,),
        out_shape=f32(receivers, 4, LANES),
        in_specs=[
            SM,
            SM,
            VM,
            pl.BlockSpec((1, 2, 8, LANES), lambda i: (4, 0, 0, 0)),
        ],
        out_specs=VM,
        compiler_params=SMALL,
        cost_estimate=pl.CostEstimate(flops=4096, bytes_accessed=65536, transcendentals=0),
    )(patch_map, block_map, weight, state)


def collect_body(tiles_ref, _, out_ref):
    base = (lax.axis_index("fx") * NB).astype(jnp.float32)
    block = lax.broadcasted_iota(jnp.int32, (NB, LANES), 0).astype(jnp.float32) + base
    sums = [jnp.zeros((NB, LANES), jnp.float32) for _ in range(4)]
    for sender in range(tiles_ref.shape[0]):
        for tile in range(2):
            load = tiles_ref[sender, tile : tile + 1, :]
            target = tiles_ref[sender, 2 + tile : 3 + tile, :]
            slot = (2 * sender + tile) % 4
            sums[slot] = sums[slot] + jnp.where(block == target, load, 0.0)
    total = (sums[0] + sums[1]) + (sums[2] + sums[3])
    for receiver in range(out_ref.shape[0]):
        out_ref[receiver] = total


def couple_body(connect_ref, stiff_ref, out_ref):
    elements = stiff_ref.shape[0]
    block = lax.broadcasted_iota(jnp.int32, (NB, elements), 0)
    first = connect_ref[0:1, :]
    second = connect_ref[1:2, :]
    ends = (block == first).astype(jnp.float32) - (block == second).astype(jnp.float32)
    pairs = [(ends * ends[a : a + 1, :]).astype(jnp.bfloat16) for a in range(NB)]
    pairs = jnp.concatenate(pairs, axis=0)
    rest = stiff_ref[...]
    total = None
    for _ in range(3):
        term = rest.astype(jnp.bfloat16)
        rest = rest - term.astype(jnp.float32)
        product = jnp.dot(pairs, term, preferred_element_type=jnp.float32)
        total = product if total is None else total + product
    out_ref[...] = total.reshape(NB, NB, LANES)


def shell_body(
    loads_ref, tiles_ref, couple_ref, disp_ref, vel_ref, _, disp_out, vel_out, wall_out
):
    base = (lax.axis_index("fx") * NB).astype(jnp.float32)
    sec = lax.axis_index("sec")
    disp = disp_ref[...]
    vel = vel_ref[...]
    load = loads_ref[0]
    for sender in range(1, loads_ref.shape[0]):
        load = load + loads_ref[sender]
    total = jnp.zeros_like(disp)
    for _ in range(SUBCYCLES):
        inner = [jnp.zeros_like(disp) for _ in range(4)]
        for a in range(NB):
            inner[a % 4] = inner[a % 4] + couple_ref[a] * disp[a : a + 1, :]
        inner = (inner[0] + inner[1]) + (inner[2] + inner[3])
        vel = vel + SHELL_STEP * (load - inner - DAMPING * vel)
        disp = disp + SHELL_STEP * vel
        total = total + disp
    wall = total * (1.0 / SUBCYCLES)
    block = lax.broadcasted_iota(jnp.int32, (NB, LANES), 0).astype(jnp.float32) + base
    for peer in range(wall_out.shape[0]):
        for tile in range(2):
            target = tiles_ref[2 * peer + sec, 2 + tile : 3 + tile, :]
            wanted = jnp.where(block == target, wall, 0.0)
            wall_out[peer, tile : tile + 1, :] = jnp.sum(wanted, axis=0, keepdims=True)
    disp_out[...] = disp
    vel_out[...] = vel


def finish_body(walls_ref, weight_ref, part_ref, _, out_ref):
    wall = walls_ref[0]
    for owner in range(1, walls_ref.shape[0]):
        wall = wall + walls_ref[owner]
    row = lax.broadcasted_iota(jnp.int32, (8, LANES), 0)
    for tile in range(2):
        gain = weight_ref[tile] * wall[tile : tile + 1, :]
        out_ref[0, tile] = part_ref[tile] + jnp.where(row == 0, gain, 0.0)


def finish(walls, weight, part, state):
    return pl.pallas_call(
        finish_body,
        grid=(1,),
        out_shape=f32(*state.shape),
        in_specs=[VM, VM, VM, ANY],
        out_specs=pl.BlockSpec((1, 2, 8, LANES), lambda i: (2, 0, 0, 0)),
        input_output_aliases={3: 0},
        compiler_params=SMALL,
        cost_estimate=pl.CostEstimate(flops=4096, bytes_accessed=65536, transcendentals=0),
    )(walls, weight, part, state)


def slab(low_ref, state_ref, high_ref, v, xi):
    if xi == 0:
        return low_ref.at[v, 1]
    if xi == 3:
        return high_ref.at[v, 0]
    return state_ref.at[v, xi - 1]


def pack_sec_body(low_ref, state_ref, high_ref, out_ref):
    sec = lax.axis_index("sec")
    lane = lax.broadcasted_iota(jnp.int32, (32, LANES), 1)

    def pack(shift):
        packed = jnp.zeros((32, LANES), jnp.float32)
        for v in range(NV):
            for xi in range(4):
                first = 8 * v + 2 * xi
                cells = slab(low_ref, state_ref, high_ref, v, xi)[...]
                moved = pltpu.roll(cells, first + shift, axis=1) if first + shift else cells
                packed = jnp.where((lane == first) | (lane == first + 1), moved, packed)
        out_ref[...] = packed

    pl.when(sec == 0)(lambda: pack(2))
    pl.when(sec == 1)(lambda: pack(0))


def pack_span_body(low_ref, state_ref, high_ref, beyond_ref, top_ref, bottom_ref):
    last = state_ref.shape[2] - 1
    for out, rows in ((top_ref, (0, 1)), (bottom_ref, (last, last - 1))):
        for place, y in enumerate(rows):
            for v in range(NV):
                for xi in range(4):
                    spot = 8 * v + 4 * place + xi
                    out[spot : spot + 1, :] = slab(low_ref, state_ref, high_ref, v, xi)[
                        y : y + 1, :
                    ]
            out[8 * NV + place : 8 * NV + place + 1, :] = beyond_ref[y : y + 1, :]
        out[8 * NV + 2 :, :] = jnp.zeros((6, LANES), jnp.float32)


def stencil(center, ahead, behind, others, mixed):
    beside = ahead + behind + others
    return DIFFUSION * (beside - 6.0 * center) - TRANSPORT * 0.5 * (ahead - behind) + mixed


def fluid_body(
    mixing_ref,
    low_ref,
    state_ref,
    high_ref,
    edge_ref,
    beyond_ref,
    top_ref,
    bottom_ref,
    before_ref,
    after_ref,
    out_ref,
    part_ref,
    field,
    section,
    packed,
):
    size = state_ref.shape[2]
    end = TOP + size
    sec = lax.axis_index("sec")
    fx = lax.axis_index("fx")
    fy = lax.axis_index("fy")
    inside_low = (fx > 0).astype(jnp.float32)
    inside_high = (fx < lax.axis_size("fx") - 1).astype(jnp.float32)
    inside_before = (fy > 0).astype(jnp.float32)
    inside_after = (fy < lax.axis_size("fy") - 1).astype(jnp.float32)
    mix = [[mixing_ref[v, w] for w in range(NV)] for v in range(NV)]

    lane = lax.broadcasted_iota(jnp.int32, (1, LANES), 1)
    open_lane = (LANES - 1) * (1 - sec)
    keep_low = (lane != 0).astype(jnp.float32)
    keep_high = (lane != LANES - 1).astype(jnp.float32)
    at_open = (lane == open_lane).astype(jnp.float32)

    def along_z(cells, columns, v, xi):
        moved = pltpu.roll(columns, LANES - 1 - (8 * v + 2 * xi), axis=1)
        return (
            keep_low * pltpu.roll(cells, 1, axis=1)
            + keep_high * pltpu.roll(cells, LANES - 1, axis=1)
            + at_open * moved
        )

    def mixed(cells, v):
        total = mix[v][0] * cells[0]
        for w in range(1, NV):
            total = total + mix[v][w] * cells[w]
        return total

    packed[TOP:end, :] = beyond_ref[...]
    packed[TOP - 1 : TOP, :] = before_ref[8 * NV : 8 * NV + 1, :]
    packed[end : end + 1, :] = after_ref[8 * NV : 8 * NV + 1, :]
    beyond = beyond_ref[...]
    group = lane // 8
    mixed_columns = jnp.zeros((size, LANES), jnp.float32)
    for shift in range(1 - NV, NV):
        factor = jnp.zeros((1, LANES), jnp.float32)
        for v in range(NV):
            if 0 <= v - shift < NV:
                factor = jnp.where(group == v, mix[v][v - shift], factor)
        source = beyond if shift == 0 else pltpu.roll(beyond, (8 * shift) % LANES, axis=1)
        mixed_columns = mixed_columns + factor * source
    column_rate = stencil(
        beyond,
        pltpu.roll(beyond, LANES - 2, axis=1),
        pltpu.roll(beyond, 2, axis=1),
        packed[TOP - 1 : end - 1, :]
        + packed[TOP + 1 : end + 1, :]
        + pltpu.roll(beyond + edge_ref[...], 1 + (LANES - 2) * (1 - sec), axis=1),
        mixed_columns,
    )
    column_section = beyond + TIME_STEP * column_rate

    row = lax.broadcasted_iota(jnp.int32, (8, LANES), 0)
    inside_rows = jnp.where(row < 4, inside_before, inside_after)
    row_cells = []
    row_others = []
    row_columns = jnp.where(
        row < 4, before_ref[8 * NV : 8 * NV + 1, :], after_ref[8 * NV : 8 * NV + 1, :]
    )
    for v in range(NV):
        cells = jnp.concatenate(
            [before_ref[8 * v : 8 * v + 4, :], after_ref[8 * v : 8 * v + 4, :]], axis=0
        )
        outer = jnp.concatenate(
            [before_ref[8 * v + 4 : 8 * v + 8, :], after_ref[8 * v + 4 : 8 * v + 8, :]], axis=0
        )
        inner = jnp.concatenate(
            [top_ref[8 * v : 8 * v + 4, :], bottom_ref[8 * v : 8 * v + 4, :]], axis=0
        )
        columns = jnp.zeros((8, LANES), jnp.float32)
        for xi in (1, 2):
            moved = pltpu.roll(row_columns, LANES - 1 - (8 * v + 2 * xi), axis=1)
            columns = jnp.where((row == xi) | (row == 4 + xi), moved, columns)
        across = (
            keep_low * pltpu.roll(cells, 1, axis=1)
            + keep_high * pltpu.roll(cells, LANES - 1, axis=1)
            + at_open * columns
        )
        row_cells.append(cells)
        row_others.append(outer + inner + across)
    for v in range(NV):
        cells = row_cells[v]
        rate = stencil(
            cells,
            pltpu.roll(cells, 7, axis=0),
            pltpu.roll(cells, 1, axis=0),
            row_others[v],
            mixed(row_cells, v),
        )
        after = inside_rows * (cells + TIME_STEP * rate)
        for xi in (1, 2):
            section[v, xi, TOP - 1 : TOP, :] = after[xi : xi + 1, :]
            section[v, xi, end : end + 1, :] = after[4 + xi : 5 + xi, :]

    for v in range(NV):
        for xi in range(4):
            field[v, xi, TOP:end, :] = slab(low_ref, state_ref, high_ref, v, xi)[...]
            field[v, xi, TOP - 1 : TOP, :] = before_ref[8 * v + xi : 8 * v + xi + 1, :]
            field[v, xi, end : end + 1, :] = after_ref[8 * v + xi : 8 * v + xi + 1, :]

    def center(v, x):
        if x < 0:
            return low_ref[v, 0]
        if x > 3:
            return high_ref[v, 1]
        return field[v, x, TOP:end, :]

    for xi in range(4):
        cells = [center(w, xi) for w in range(NV)]
        for v in range(NV):
            others = (
                field[v, xi, TOP - 1 : end - 1, :]
                + field[v, xi, TOP + 1 : end + 1, :]
                + along_z(cells[v], beyond, v, xi)
            )
            rate = stencil(
                cells[v], center(v, xi + 1), center(v, xi - 1), others, mixed(cells, v)
            )
            after = cells[v] + TIME_STEP * rate
            if xi == 0:
                after = inside_low * after
            if xi == 3:
                after = inside_high * after
            section[v, xi, TOP:end, :] = after
            if xi in (1, 2):
                out_ref[v, xi - 1] = cells[v] + 0.5 * TIME_STEP * rate

    for xi in (1, 2):
        cells = [section[w, xi, TOP:end, :] for w in range(NV)]
        for v in range(NV):
            others = (
                section[v, xi, TOP - 1 : end - 1, :]
                + section[v, xi, TOP + 1 : end + 1, :]
                + along_z(cells[v], column_section, v, xi)
            )
            rate = stencil(
                cells[v],
                section[v, xi + 1, TOP:end, :],
                section[v, xi - 1, TOP:end, :],
                others,
                mixed(cells, v),
            )
            final = out_ref[v, xi - 1] + 0.5 * TIME_STEP * rate
            out_ref[v, xi - 1] = final
            if v == 2:
                part_ref[xi - 1] = final[:8, :]


def shards(
    state, mixing, wall_weight, patch_map, block_map, shell_disp, shell_vel, connect, stiffness
):
    nfx, nfy, nsec = (lax.axis_size(axis) for axis in ("fx", "fy", "sec"))
    up_x = [(i, i + 1) for i in range(nfx - 1)]
    down_x = [(i + 1, i) for i in range(nfx - 1)]
    up_y = [(i, i + 1) for i in range(nfy - 1)]
    down_y = [(i + 1, i) for i in range(nfy - 1)]

    low = lax.ppermute(state, "fx", up_x)
    high = lax.ppermute(state, "fx", down_x)

    offered = offer(
        patch_map.reshape(2), block_map.reshape(2), wall_weight, state, nfx * nsec
    )
    tiles = lax.all_to_all(offered, ("fx", "sec"), 0, 0, tiled=True)

    edge = kernel_call(pack_sec_body, f32(32, LANES), [VM] * 3)(low, state, high)
    beyond = lax.ppermute(edge, "sec", [(0, 1), (1, 0)])
    couple = kernel_call(couple_body, f32(NB, NB, LANES), [VM] * 2)(
        connect[0].T, stiffness[0]
    )

    partial = kernel_call(collect_body, f32(nfy, NB, LANES), [VM, ANY])(tiles, edge)
    loads = lax.all_to_all(partial, "fy", 0, 0, tiled=True)

    span = f32(8 * NV + 8, LANES)
    top, bottom = kernel_call(pack_span_body, (span, span), [VM] * 4)(low, state, high, beyond)
    before = lax.ppermute(bottom, "fy", up_y)
    after = lax.ppermute(top, "fy", down_y)

    new_disp, new_vel, walls = kernel_call(
        shell_body, (f32(NB, LANES), f32(NB, LANES), f32(nfx, 2, LANES)), [VM] * 5 + [ANY]
    )(loads, tiles, couple, shell_disp.reshape(NB, LANES), shell_vel.reshape(NB, LANES), top)
    walls = lax.all_to_all(walls, "fx", 0, 0, tiled=True)

    fluid, part = kernel_call(
        fluid_body,
        (f32(*state.shape), f32(2, 8, LANES)),
        [SM] + [VM] * 9,
        scratch=[
            pltpu.VMEM((NV, 4, ROWS, LANES), jnp.float32),
            pltpu.VMEM((NV, 4, ROWS, LANES), jnp.float32),
            pltpu.VMEM((ROWS, LANES), jnp.float32),
        ],
    )(mixing, low, state, high, edge, beyond, top, bottom, before, after)
    new_state = finish(walls, wall_weight, part, fluid)
    return (new_state, new_disp.reshape(1, -1), new_vel.reshape(1, -1))


def solution(mesh):
    return jax.shard_map(
        shards,
        mesh=mesh,
        in_specs=(
            P(None, "fx", "fy", "sec"),
            P(),
            P("fx", "fy", "sec"),
            P("fx", "fy", "sec", None),
            P("fx", "fy", "sec", None),
            P("fx", None),
            P("fx", None),
            P("fx", None, None),
            P("fx", None, None),
        ),
        out_specs=(P(None, "fx", "fy", "sec"), P("fx", None), P("fx", None)),
        check_vma=False,
    )
```

```python
import jax
import jax.numpy as jnp
from jax import lax
from jax.experimental import pallas as pl
from jax.experimental.pallas import tpu as pltpu
from jax.sharding import PartitionSpec as P

NV = 5
NB = 32
SUBCYCLES = 4
LANES = 128

DIFFUSION = 0.25
TRANSPORT = 0.5
TIME_STEP = 0.2
SHELL_STEP = 0.25
DAMPING = 0.1

TOP = 8
ROWS = 48

LONG = 3_800_000_000
LONG_SEC = 1_300_000_000

VM = pl.BlockSpec(memory_space=pltpu.VMEM)
SM = pl.BlockSpec(memory_space=pltpu.SMEM)
ANY = pl.BlockSpec(memory_space=pl.ANY)
HBM = pl.BlockSpec(memory_space=pltpu.HBM)
SMALL = pltpu.CompilerParams(vmem_limit_bytes=8 * 1024 * 1024)


def kernel_call(body, outs, ins, scratch=(), cost=20000, params=SMALL):
    return pl.pallas_call(
        body,
        out_shape=outs,
        in_specs=ins,
        out_specs=jax.tree.map(lambda _: VM, outs),
        scratch_shapes=scratch,
        compiler_params=params,
        cost_estimate=pl.CostEstimate(flops=cost, bytes_accessed=cost, transcendentals=0),
    )


def f32(*shape):
    return jax.ShapeDtypeStruct(shape, jnp.float32)


def offer_body(
    patch_hbm, block_hbm, weight_hbm, state_hbm, out_ref, patch_ref, block_ref, weight_ref, wall_ref, arrived
):
    copies = [
        pltpu.make_async_copy(source, target, arrived.at[place])
        for place, (source, target) in enumerate(
            (
                (patch_hbm, patch_ref),
                (block_hbm, block_ref),
                (weight_hbm, weight_ref),
                (state_hbm.at[NV - 1, :, 0:8, :], wall_ref),
            )
        )
    ]
    for copy in copies:
        copy.start()
    for copy in copies:
        copy.wait()
    rows = []
    for tile in range(2):
        rows.append(weight_ref[tile] * wall_ref[tile, 0:1, :])
    for tile in range(2):
        target = patch_ref[tile] * NB + block_ref[tile]
        rows.append(jnp.full((1, LANES), target.astype(jnp.float32)))
    rows = jnp.concatenate(rows, axis=0)
    for receiver in range(out_ref.shape[0]):
        out_ref[receiver] = rows


def offer(patch_map, block_map, weight, state, receivers):
    return kernel_call(
        offer_body,
        f32(receivers, 4, LANES),
        [HBM] * 4,
        scratch=[
            pltpu.SMEM((2,), jnp.int32),
            pltpu.SMEM((2,), jnp.int32),
            pltpu.VMEM((2, 1, LANES), jnp.float32),
            pltpu.VMEM((2, 8, LANES), jnp.float32),
            pltpu.SemaphoreType.DMA((4,)),
        ],
        params=None,
    )(patch_map, block_map, weight, state)


def collect_body(tiles_ref, out_ref):
    base = (lax.axis_index("fx") * NB).astype(jnp.float32)
    block = lax.broadcasted_iota(jnp.int32, (NB, LANES), 0).astype(jnp.float32) + base
    sums = [jnp.zeros((NB, LANES), jnp.float32) for _ in range(4)]
    for sender in range(tiles_ref.shape[0]):
        for tile in range(2):
            load = tiles_ref[sender, tile : tile + 1, :]
            target = tiles_ref[sender, 2 + tile : 3 + tile, :]
            slot = (2 * sender + tile) % 4
            sums[slot] = sums[slot] + jnp.where(block == target, load, 0.0)
    total = (sums[0] + sums[1]) + (sums[2] + sums[3])
    for receiver in range(out_ref.shape[0]):
        out_ref[receiver] = total


def couple_body(connect_ref, stiff_ref, out_ref):
    elements = stiff_ref.shape[0]
    block = lax.broadcasted_iota(jnp.int32, (NB, elements), 0)
    first = connect_ref[0:1, :]
    second = connect_ref[1:2, :]
    ends = (block == first).astype(jnp.float32) - (block == second).astype(jnp.float32)
    pairs = [(ends * ends[a : a + 1, :]).astype(jnp.bfloat16) for a in range(NB)]
    pairs = jnp.concatenate(pairs, axis=0)
    rest = stiff_ref[...]
    total = None
    for _ in range(3):
        term = rest.astype(jnp.bfloat16)
        rest = rest - term.astype(jnp.float32)
        product = jnp.dot(pairs, term, preferred_element_type=jnp.float32)
        total = product if total is None else total + product
    out_ref[...] = total.reshape(NB, NB, LANES)


def shell_body(
    loads_ref, tiles_ref, couple_ref, disp_ref, vel_ref, _, disp_out, vel_out, wall_out
):
    base = (lax.axis_index("fx") * NB).astype(jnp.float32)
    sec = lax.axis_index("sec")
    disp = disp_ref[...]
    vel = vel_ref[...]
    load = loads_ref[0]
    for sender in range(1, loads_ref.shape[0]):
        load = load + loads_ref[sender]
    total = jnp.zeros_like(disp)
    for _ in range(SUBCYCLES):
        inner = [jnp.zeros_like(disp) for _ in range(4)]
        for a in range(NB):
            inner[a % 4] = inner[a % 4] + couple_ref[a] * disp[a : a + 1, :]
        inner = (inner[0] + inner[1]) + (inner[2] + inner[3])
        vel = vel + SHELL_STEP * (load - inner - DAMPING * vel)
        disp = disp + SHELL_STEP * vel
        total = total + disp
    wall = total * (1.0 / SUBCYCLES)
    block = lax.broadcasted_iota(jnp.int32, (NB, LANES), 0).astype(jnp.float32) + base
    for peer in range(wall_out.shape[0]):
        for tile in range(2):
            target = tiles_ref[2 * peer + sec, 2 + tile : 3 + tile, :]
            wanted = jnp.where(block == target, wall, 0.0)
            wall_out[peer, tile : tile + 1, :] = jnp.sum(wanted, axis=0, keepdims=True)
    disp_out[...] = disp
    vel_out[...] = vel


def finish_body(walls_ref, weight_ref, part_ref, _, out_ref):
    wall = walls_ref[0]
    for owner in range(1, walls_ref.shape[0]):
        wall = wall + walls_ref[owner]
    row = lax.broadcasted_iota(jnp.int32, (8, LANES), 0)
    for tile in range(2):
        gain = weight_ref[tile] * wall[tile : tile + 1, :]
        out_ref[0, tile] = part_ref[tile] + jnp.where(row == 0, gain, 0.0)


def finish(walls, weight, part, state):
    return pl.pallas_call(
        finish_body,
        grid=(1,),
        out_shape=f32(*state.shape),
        in_specs=[VM, VM, VM, ANY],
        out_specs=pl.BlockSpec((1, 2, 8, LANES), lambda i: (2, 0, 0, 0)),
        input_output_aliases={3: 0},
        compiler_params=SMALL,
        cost_estimate=pl.CostEstimate(flops=4096, bytes_accessed=65536, transcendentals=0),
    )(walls, weight, part, state)


def slab(low_ref, state_ref, high_ref, v, xi):
    if xi == 0:
        return low_ref.at[v, 1]
    if xi == 3:
        return high_ref.at[v, 0]
    return state_ref.at[v, xi - 1]


def pack_columns(slabs, out_ref):
    lane = lax.broadcasted_iota(jnp.int32, (32, LANES), 1)

    def pack(shift):
        packed = jnp.zeros((32, LANES), jnp.float32)
        for (v, xi), cells_ref in slabs.items():
            first = 8 * v + 2 * xi
            cells = cells_ref[...]
            moved = pltpu.roll(cells, first + shift, axis=1) if first + shift else cells
            packed = jnp.where((lane == first) | (lane == first + 1), moved, packed)
        out_ref[...] = packed

    sec = lax.axis_index("sec")
    pl.when(sec == 0)(lambda: pack(2))
    pl.when(sec == 1)(lambda: pack(0))


def first_round_body(state_ref, _, copy_ref, edge_ref):
    copy_ref[...] = state_ref[...]
    pack_columns({(v, xi): state_ref.at[v, xi - 1] for v in range(NV) for xi in (1, 2)}, edge_ref)


def corner_body(beyond_ref, out_ref):
    last = beyond_ref.shape[0] - 1
    for place, y in enumerate((0, 1, last, last - 1)):
        out_ref[place : place + 1, :] = beyond_ref[y : y + 1, :]
    out_ref[4:8, :] = jnp.zeros((4, LANES), jnp.float32)


def second_round_body(
    low_ref, state_ref, high_ref, corner_ref, top_ref, bottom_ref, edge_ref
):
    last = state_ref.shape[2] - 1
    for end, (out, rows) in enumerate(((top_ref, (0, 1)), (bottom_ref, (last, last - 1)))):
        for place, y in enumerate(rows):
            for v in range(NV):
                for xi in range(4):
                    spot = 8 * v + 4 * place + xi
                    out[spot : spot + 1, :] = slab(low_ref, state_ref, high_ref, v, xi)[
                        y : y + 1, :
                    ]
        out[8 * NV : 8 * NV + 2, :] = corner_ref[2 * end : 2 * end + 2, :]
        out[8 * NV + 2 :, :] = jnp.zeros((6, LANES), jnp.float32)
    outer = {(v, 0): low_ref.at[v, 1] for v in range(NV)}
    outer |= {(v, 3): high_ref.at[v, 0] for v in range(NV)}
    pack_columns(outer, edge_ref)


def stencil(center, ahead, behind, others, mixed):
    beside = ahead + behind + others
    return DIFFUSION * (beside - 6.0 * center) - TRANSPORT * 0.5 * (ahead - behind) + mixed


def fluid_body(
    mixing_ref,
    low_ref,
    state_ref,
    high_ref,
    edge_ref,
    own_beyond_ref,
    outer_beyond_ref,
    top_ref,
    bottom_ref,
    before_ref,
    after_ref,
    out_ref,
    part_ref,
    field,
    section,
    packed,
):
    beyond = own_beyond_ref[...] + outer_beyond_ref[...]
    size = state_ref.shape[2]
    end = TOP + size
    sec = lax.axis_index("sec")
    fx = lax.axis_index("fx")
    fy = lax.axis_index("fy")
    inside_low = (fx > 0).astype(jnp.float32)
    inside_high = (fx < lax.axis_size("fx") - 1).astype(jnp.float32)
    inside_before = (fy > 0).astype(jnp.float32)
    inside_after = (fy < lax.axis_size("fy") - 1).astype(jnp.float32)
    mix = [[mixing_ref[v, w] for w in range(NV)] for v in range(NV)]

    lane = lax.broadcasted_iota(jnp.int32, (1, LANES), 1)
    open_lane = (LANES - 1) * (1 - sec)
    keep_low = (lane != 0).astype(jnp.float32)
    keep_high = (lane != LANES - 1).astype(jnp.float32)
    at_open = (lane == open_lane).astype(jnp.float32)

    def along_z(cells, columns, v, xi):
        moved = pltpu.roll(columns, LANES - 1 - (8 * v + 2 * xi), axis=1)
        return (
            keep_low * pltpu.roll(cells, 1, axis=1)
            + keep_high * pltpu.roll(cells, LANES - 1, axis=1)
            + at_open * moved
        )

    def mixed(cells, v):
        total = mix[v][0] * cells[0]
        for w in range(1, NV):
            total = total + mix[v][w] * cells[w]
        return total

    packed[TOP:end, :] = beyond
    packed[TOP - 1 : TOP, :] = before_ref[8 * NV : 8 * NV + 1, :]
    packed[end : end + 1, :] = after_ref[8 * NV : 8 * NV + 1, :]
    group = lane // 8
    mixed_columns = jnp.zeros((size, LANES), jnp.float32)
    for shift in range(1 - NV, NV):
        factor = jnp.zeros((1, LANES), jnp.float32)
        for v in range(NV):
            if 0 <= v - shift < NV:
                factor = jnp.where(group == v, mix[v][v - shift], factor)
        source = beyond if shift == 0 else pltpu.roll(beyond, (8 * shift) % LANES, axis=1)
        mixed_columns = mixed_columns + factor * source
    column_rate = stencil(
        beyond,
        pltpu.roll(beyond, LANES - 2, axis=1),
        pltpu.roll(beyond, 2, axis=1),
        packed[TOP - 1 : end - 1, :]
        + packed[TOP + 1 : end + 1, :]
        + pltpu.roll(beyond + edge_ref[...], 1 + (LANES - 2) * (1 - sec), axis=1),
        mixed_columns,
    )
    column_section = beyond + TIME_STEP * column_rate

    row = lax.broadcasted_iota(jnp.int32, (8, LANES), 0)
    inside_rows = jnp.where(row < 4, inside_before, inside_after)
    row_cells = []
    row_others = []
    row_columns = jnp.where(
        row < 4, before_ref[8 * NV : 8 * NV + 1, :], after_ref[8 * NV : 8 * NV + 1, :]
    )
    for v in range(NV):
        cells = jnp.concatenate(
            [before_ref[8 * v : 8 * v + 4, :], after_ref[8 * v : 8 * v + 4, :]], axis=0
        )
        outer = jnp.concatenate(
            [before_ref[8 * v + 4 : 8 * v + 8, :], after_ref[8 * v + 4 : 8 * v + 8, :]], axis=0
        )
        inner = jnp.concatenate(
            [top_ref[8 * v : 8 * v + 4, :], bottom_ref[8 * v : 8 * v + 4, :]], axis=0
        )
        columns = jnp.zeros((8, LANES), jnp.float32)
        for xi in (1, 2):
            moved = pltpu.roll(row_columns, LANES - 1 - (8 * v + 2 * xi), axis=1)
            columns = jnp.where((row == xi) | (row == 4 + xi), moved, columns)
        across = (
            keep_low * pltpu.roll(cells, 1, axis=1)
            + keep_high * pltpu.roll(cells, LANES - 1, axis=1)
            + at_open * columns
        )
        row_cells.append(cells)
        row_others.append(outer + inner + across)
    for v in range(NV):
        cells = row_cells[v]
        rate = stencil(
            cells,
            pltpu.roll(cells, 7, axis=0),
            pltpu.roll(cells, 1, axis=0),
            row_others[v],
            mixed(row_cells, v),
        )
        after = inside_rows * (cells + TIME_STEP * rate)
        for xi in (1, 2):
            section[v, xi, TOP - 1 : TOP, :] = after[xi : xi + 1, :]
            section[v, xi, end : end + 1, :] = after[4 + xi : 5 + xi, :]

    for v in range(NV):
        for xi in range(4):
            field[v, xi, TOP:end, :] = slab(low_ref, state_ref, high_ref, v, xi)[...]
            field[v, xi, TOP - 1 : TOP, :] = before_ref[8 * v + xi : 8 * v + xi + 1, :]
            field[v, xi, end : end + 1, :] = after_ref[8 * v + xi : 8 * v + xi + 1, :]

    def center(v, x):
        if x < 0:
            return low_ref[v, 0]
        if x > 3:
            return high_ref[v, 1]
        return field[v, x, TOP:end, :]

    for xi in range(4):
        cells = [center(w, xi) for w in range(NV)]
        for v in range(NV):
            others = (
                field[v, xi, TOP - 1 : end - 1, :]
                + field[v, xi, TOP + 1 : end + 1, :]
                + along_z(cells[v], beyond, v, xi)
            )
            rate = stencil(
                cells[v], center(v, xi + 1), center(v, xi - 1), others, mixed(cells, v)
            )
            after = cells[v] + TIME_STEP * rate
            if xi == 0:
                after = inside_low * after
            if xi == 3:
                after = inside_high * after
            section[v, xi, TOP:end, :] = after
            if xi in (1, 2):
                out_ref[v, xi - 1] = cells[v] + 0.5 * TIME_STEP * rate

    for xi in (1, 2):
        cells = [section[w, xi, TOP:end, :] for w in range(NV)]
        for v in range(NV):
            others = (
                section[v, xi, TOP - 1 : end - 1, :]
                + section[v, xi, TOP + 1 : end + 1, :]
                + along_z(cells[v], column_section, v, xi)
            )
            rate = stencil(
                cells[v],
                section[v, xi + 1, TOP:end, :],
                section[v, xi - 1, TOP:end, :],
                others,
                mixed(cells, v),
            )
            final = out_ref[v, xi - 1] + 0.5 * TIME_STEP * rate
            out_ref[v, xi - 1] = final
            if v == 2:
                part_ref[xi - 1] = final[:8, :]


def shards(
    state, mixing, wall_weight, patch_map, block_map, shell_disp, shell_vel, connect, stiffness
):
    nfx, nfy, nsec = (lax.axis_size(axis) for axis in ("fx", "fy", "sec"))
    up_x = [(i, i + 1) for i in range(nfx - 1)]
    down_x = [(i + 1, i) for i in range(nfx - 1)]
    up_y = [(i, i + 1) for i in range(nfy - 1)]
    down_y = [(i + 1, i) for i in range(nfy - 1)]

    offered = offer(
        patch_map.reshape(2), block_map.reshape(2), wall_weight, state, nfx * nsec
    )
    tiles = lax.all_to_all(offered, ("fx", "sec"), 0, 0, tiled=True)

    columns = f32(32, LANES)
    sent, edge = kernel_call(first_round_body, (f32(*state.shape), columns), [VM, ANY])(
        state, offered
    )
    low = lax.ppermute(sent, "fx", up_x)
    high = lax.ppermute(sent, "fx", down_x)
    beyond = lax.ppermute(edge, "sec", [(0, 1), (1, 0)])

    partial = kernel_call(collect_body, f32(nfy, NB, LANES), [VM])(tiles)
    loads = lax.all_to_all(partial, "fy", 0, 0, tiled=True)

    couple = kernel_call(couple_body, f32(NB, NB, LANES), [VM] * 2)(
        connect[0].T, stiffness[0]
    )
    corner = kernel_call(corner_body, f32(8, LANES), [VM], cost=LONG_SEC)(beyond)
    span = f32(8 * NV + 8, LANES)
    top, bottom, outer_edge = kernel_call(
        second_round_body, (span, span, columns), [VM] * 4, cost=LONG
    )(low, sent, high, corner)
    before = lax.ppermute(bottom, "fy", up_y)
    after = lax.ppermute(top, "fy", down_y)
    outer_beyond = lax.ppermute(outer_edge, "sec", [(0, 1), (1, 0)])

    new_disp, new_vel, walls = kernel_call(
        shell_body, (f32(NB, LANES), f32(NB, LANES), f32(nfx, 2, LANES)), [VM] * 5 + [ANY]
    )(loads, tiles, couple, shell_disp.reshape(NB, LANES), shell_vel.reshape(NB, LANES), top)
    walls = lax.all_to_all(walls, "fx", 0, 0, tiled=True)

    fluid, part = kernel_call(
        fluid_body,
        (f32(*state.shape), f32(2, 8, LANES)),
        [SM] + [VM] * 10,
        scratch=[
            pltpu.VMEM((NV, 4, ROWS, LANES), jnp.float32),
            pltpu.VMEM((NV, 4, ROWS, LANES), jnp.float32),
            pltpu.VMEM((ROWS, LANES), jnp.float32),
        ],
        cost=LONG,
    )(mixing, low, sent, high, edge, beyond, outer_beyond, top, bottom, before, after)
    new_state = finish(walls, wall_weight, part, fluid)
    return (new_state, new_disp.reshape(1, -1), new_vel.reshape(1, -1))


def solution(mesh):
    return jax.shard_map(
        shards,
        mesh=mesh,
        in_specs=(
            P(None, "fx", "fy", "sec"),
            P(),
            P("fx", "fy", "sec"),
            P("fx", "fy", "sec", None),
            P("fx", "fy", "sec", None),
            P("fx", None),
            P("fx", None),
            P("fx", None, None),
            P("fx", None, None),
        ),
        out_specs=(P(None, "fx", "fy", "sec"), P("fx", None), P("fx", None)),
        check_vma=False,
    )
```

```python
import jax
import jax.numpy as jnp
from jax import lax
from jax.experimental import pallas as pl
from jax.experimental.pallas import tpu as pltpu
from jax.sharding import PartitionSpec as P

NV = 5
NB = 32
SUBCYCLES = 4
LANES = 128

DIFFUSION = 0.25
TRANSPORT = 0.5
TIME_STEP = 0.2
SHELL_STEP = 0.25
DAMPING = 0.1

TOP = 8
ROWS = 48

LONG = 3_800_000_000

VM = pl.BlockSpec(memory_space=pltpu.VMEM)
SM = pl.BlockSpec(memory_space=pltpu.SMEM)
ANY = pl.BlockSpec(memory_space=pl.ANY)
HBM = pl.BlockSpec(memory_space=pltpu.HBM)
SMALL = pltpu.CompilerParams(vmem_limit_bytes=8 * 1024 * 1024)


def kernel_call(body, outs, ins, scratch=(), cost=20000, params=SMALL):
    return pl.pallas_call(
        body,
        out_shape=outs,
        in_specs=ins,
        out_specs=jax.tree.map(lambda _: VM, outs),
        scratch_shapes=scratch,
        compiler_params=params,
        cost_estimate=pl.CostEstimate(flops=cost, bytes_accessed=cost, transcendentals=0),
    )


def f32(*shape):
    return jax.ShapeDtypeStruct(shape, jnp.float32)


def terms(x):
    found = []
    for _ in range(3):
        term = x.astype(jnp.bfloat16)
        x = x - term.astype(jnp.float32)
        found.append(term)
    return found


def product(select, x, axis=0):
    select = select.astype(jnp.bfloat16)
    total = None
    for term in terms(x):
        part = lax.dot_general(
            select, term, (((1,), (axis,)), ((), ())), preferred_element_type=jnp.float32
        )
        total = part if total is None else total + part
    return total


def offer_body(
    patch_hbm, block_hbm, weight_hbm, state_hbm, out_ref, sent_ref, weight_ref, patch_ref, block_ref, arrived
):
    copies = [
        pltpu.make_async_copy(source, target, arrived.at[place])
        for place, (source, target) in enumerate(
            (
                (state_hbm, sent_ref),
                (patch_hbm, patch_ref),
                (block_hbm, block_ref),
                (weight_hbm, weight_ref),
            )
        )
    ]
    for copy in copies:
        copy.start()
    for copy in copies:
        copy.wait()
    sec = lax.axis_index("sec")
    column = lax.broadcasted_iota(jnp.int32, (8, LANES), 0)
    lane = lax.broadcasted_iota(jnp.int32, (8, LANES), 1)
    wanted = (lane == column + (LANES - 2) * (1 - sec)).astype(jnp.float32)
    columns = product(wanted, sent_ref[...].reshape(-1, LANES), axis=1)
    rows = [weight_ref[tile] * sent_ref[NV - 1, tile, 0:1, :] for tile in range(2)]
    for tile in range(2):
        target = patch_ref[tile] * NB + block_ref[tile]
        target = jnp.full((1, LANES // 2), target.astype(jnp.float32))
        values = columns[tile : tile + 1, :]
        rows += [values[:, :LANES], values[:, LANES : 2 * LANES]]
        rows.append(jnp.concatenate([values[:, 2 * LANES :], target], axis=1))
    rows = jnp.concatenate(rows, axis=0)
    for receiver in range(out_ref.shape[0]):
        out_ref[receiver] = rows


def offer(patch_map, block_map, weight, state, receivers):
    return kernel_call(
        offer_body,
        (f32(receivers, 8, LANES), f32(*state.shape), f32(*weight.shape)),
        [HBM] * 4,
        scratch=[
            pltpu.SMEM((2,), jnp.int32),
            pltpu.SMEM((2,), jnp.int32),
            pltpu.SemaphoreType.DMA((4,)),
        ],
        params=None,
    )(patch_map, block_map, weight, state)


def targets_of(rows):
    lane = lax.broadcasted_iota(jnp.int32, (8, LANES), 1)
    return jnp.where(lane < LANES // 2, pltpu.roll(rows, LANES // 2, axis=1), rows)


def collect_body(offered_ref, out_ref):
    base = (lax.axis_index("fx") * NB).astype(jnp.float32)
    block = lax.broadcasted_iota(jnp.int32, (NB, LANES), 0).astype(jnp.float32) + base
    sums = [jnp.zeros((NB, LANES), jnp.float32) for _ in range(4)]
    for sender in range(offered_ref.shape[0]):
        rows = offered_ref[sender]
        targets = targets_of(rows)
        for tile in range(2):
            load = rows[tile : tile + 1, :]
            target = targets[4 + 3 * tile : 5 + 3 * tile, :]
            slot = (2 * sender + tile) % 4
            sums[slot] = sums[slot] + jnp.where(block == target, load, 0.0)
    total = (sums[0] + sums[1]) + (sums[2] + sums[3])
    for receiver in range(out_ref.shape[0]):
        out_ref[receiver] = total


def couple_body(connect_ref, stiff_ref, disp_ref, vel_ref, out_ref, disp_out, vel_out):
    elements = stiff_ref.shape[0]
    block = lax.broadcasted_iota(jnp.int32, (NB, elements), 0)
    first = connect_ref[0:1, :]
    second = connect_ref[1:2, :]
    ends = (block == first).astype(jnp.float32) - (block == second).astype(jnp.float32)
    pairs = [(ends * ends[a : a + 1, :]).astype(jnp.bfloat16) for a in range(NB)]
    pairs = jnp.concatenate(pairs, axis=0)
    out_ref[...] = product(pairs, stiff_ref[...]).reshape(NB, NB, LANES)
    disp_out[...] = disp_ref[...]
    vel_out[...] = vel_ref[...]


def shell_body(
    loads_ref, offered_ref, couple_ref, disp_ref, vel_ref, _, disp_out, vel_out, wall_out
):
    base = (lax.axis_index("fx") * NB).astype(jnp.float32)
    sec = lax.axis_index("sec")
    disp = disp_ref[...]
    vel = vel_ref[...]
    load = loads_ref[0]
    for sender in range(1, loads_ref.shape[0]):
        load = load + loads_ref[sender]
    total = jnp.zeros_like(disp)
    for _ in range(SUBCYCLES):
        inner = [jnp.zeros_like(disp) for _ in range(4)]
        for a in range(NB):
            inner[a % 4] = inner[a % 4] + couple_ref[a] * disp[a : a + 1, :]
        inner = (inner[0] + inner[1]) + (inner[2] + inner[3])
        vel = vel + SHELL_STEP * (load - inner - DAMPING * vel)
        disp = disp + SHELL_STEP * vel
        total = total + disp
    wall = total * (1.0 / SUBCYCLES)
    block = lax.broadcasted_iota(jnp.int32, (NB, LANES), 0).astype(jnp.float32) + base
    for peer in range(wall_out.shape[0]):
        targets = targets_of(offered_ref[2 * peer + sec])
        for tile in range(2):
            target = targets[4 + 3 * tile : 5 + 3 * tile, :]
            wanted = jnp.where(block == target, wall, 0.0)
            wall_out[peer, tile : tile + 1, :] = jnp.sum(wanted, axis=0, keepdims=True)
    disp_out[...] = disp
    vel_out[...] = vel


def finish_body(walls_ref, weight_ref, part_ref, _, out_ref):
    wall = walls_ref[0]
    for owner in range(1, walls_ref.shape[0]):
        wall = wall + walls_ref[owner]
    row = lax.broadcasted_iota(jnp.int32, (8, LANES), 0)
    for tile in range(2):
        gain = weight_ref[tile] * wall[tile : tile + 1, :]
        out_ref[0, tile] = part_ref[tile] + jnp.where(row == 0, gain, 0.0)


def finish(walls, weight, part, state):
    return pl.pallas_call(
        finish_body,
        grid=(1,),
        out_shape=f32(*state.shape),
        in_specs=[VM, VM, VM, ANY],
        out_specs=pl.BlockSpec((1, 2, 8, LANES), lambda i: (2, 0, 0, 0)),
        input_output_aliases={3: 0},
        compiler_params=SMALL,
        cost_estimate=pl.CostEstimate(flops=4096, bytes_accessed=65536, transcendentals=0),
    )(walls, weight, part, state)


def slab(low_ref, state_ref, high_ref, v, xi):
    if xi == 0:
        return low_ref.at[v, 1]
    if xi == 3:
        return high_ref.at[v, 0]
    return state_ref.at[v, xi - 1]


def pack_columns(slabs, out_ref):
    lane = lax.broadcasted_iota(jnp.int32, (32, LANES), 1)

    def pack(shift):
        packed = jnp.zeros((32, LANES), jnp.float32)
        for (v, xi), cells_ref in slabs.items():
            first = 8 * v + 2 * xi
            cells = cells_ref[...]
            moved = pltpu.roll(cells, first + shift, axis=1) if first + shift else cells
            packed = jnp.where((lane == first) | (lane == first + 1), moved, packed)
        out_ref[...] = packed

    sec = lax.axis_index("sec")
    pl.when(sec == 0)(lambda: pack(2))
    pl.when(sec == 1)(lambda: pack(0))


def unpack_columns(offered_ref):
    sec = lax.axis_index("sec")
    fx = lax.axis_index("fx")
    last = lax.axis_size("fx") - 1
    rows = [
        offered_ref[2 * jnp.maximum(fx - 1, 0) + 1 - sec] * (fx > 0).astype(jnp.float32),
        offered_ref[2 * fx + 1 - sec],
        offered_ref[2 * jnp.minimum(fx + 1, last) + 1 - sec] * (fx < last).astype(jnp.float32),
        jnp.zeros((8, LANES), jnp.float32),
    ]
    rows = jnp.concatenate(rows, axis=0)

    def place(shape):
        l = lax.broadcasted_iota(jnp.int32, shape, 0)
        xi = (l & 7) >> 1
        neighbour = jnp.where(xi == 0, 0, jnp.where(xi == 3, 2, 1))
        return neighbour, l & 1, 2 * (l >> 3) + 1 - (xi & 1)

    neighbour, column, source = place((LANES, 32))
    row = 8 * neighbour + 2 + 3 * column + (source >> 2)
    here = lax.broadcasted_iota(jnp.int32, (LANES, 32), 1) == row
    here &= lax.broadcasted_iota(jnp.int32, (LANES, 32), 0) < 8 * NV
    lines = product(here.astype(jnp.float32), rows)
    _, _, source = place((LANES, LANES))
    position = lax.broadcasted_iota(jnp.int32, (LANES, LANES), 1)
    lines = jnp.where((position >> 5) == (source & 3), lines, 0.0)
    position = lax.broadcasted_iota(jnp.int32, (32, LANES), 1)
    y = lax.broadcasted_iota(jnp.int32, (32, LANES), 0)
    return product(((position & 31) == y).astype(jnp.float32), lines, axis=1)


def second_round_body(
    low_ref, state_ref, high_ref, offered_ref, top_ref, bottom_ref, beyond_ref
):
    beyond_ref[...] = unpack_columns(offered_ref)
    last = state_ref.shape[2] - 1
    for out, rows in ((top_ref, (0, 1)), (bottom_ref, (last, last - 1))):
        for place, y in enumerate(rows):
            for v in range(NV):
                for xi in range(4):
                    spot = 8 * v + 4 * place + xi
                    out[spot : spot + 1, :] = slab(low_ref, state_ref, high_ref, v, xi)[
                        y : y + 1, :
                    ]
            out[8 * NV + place : 8 * NV + place + 1, :] = beyond_ref[y : y + 1, :]
        out[8 * NV + 2 :, :] = jnp.zeros((6, LANES), jnp.float32)


def stencil(center, ahead, behind, others, mixed):
    beside = ahead + behind + others
    return DIFFUSION * (beside - 6.0 * center) - TRANSPORT * 0.5 * (ahead - behind) + mixed


def fluid_body(
    mixing_ref,
    low_ref,
    state_ref,
    high_ref,
    beyond_ref,
    top_ref,
    bottom_ref,
    before_ref,
    after_ref,
    out_ref,
    part_ref,
    field,
    section,
    packed,
    edge_ref,
):
    beyond = beyond_ref[...]
    pack_columns({(v, xi): state_ref.at[v, xi - 1] for v in range(NV) for xi in (1, 2)}, edge_ref)
    size = state_ref.shape[2]
    end = TOP + size
    sec = lax.axis_index("sec")
    fx = lax.axis_index("fx")
    fy = lax.axis_index("fy")
    inside_low = (fx > 0).astype(jnp.float32)
    inside_high = (fx < lax.axis_size("fx") - 1).astype(jnp.float32)
    inside_before = (fy > 0).astype(jnp.float32)
    inside_after = (fy < lax.axis_size("fy") - 1).astype(jnp.float32)
    mix = [[mixing_ref[v, w] for w in range(NV)] for v in range(NV)]

    lane = lax.broadcasted_iota(jnp.int32, (1, LANES), 1)
    open_lane = (LANES - 1) * (1 - sec)
    keep_low = (lane != 0).astype(jnp.float32)
    keep_high = (lane != LANES - 1).astype(jnp.float32)
    at_open = (lane == open_lane).astype(jnp.float32)

    def along_z(cells, columns, v, xi):
        moved = pltpu.roll(columns, LANES - 1 - (8 * v + 2 * xi), axis=1)
        return (
            keep_low * pltpu.roll(cells, 1, axis=1)
            + keep_high * pltpu.roll(cells, LANES - 1, axis=1)
            + at_open * moved
        )

    def mixed(cells, v):
        total = mix[v][0] * cells[0]
        for w in range(1, NV):
            total = total + mix[v][w] * cells[w]
        return total

    packed[TOP:end, :] = beyond
    packed[TOP - 1 : TOP, :] = before_ref[8 * NV : 8 * NV + 1, :]
    packed[end : end + 1, :] = after_ref[8 * NV : 8 * NV + 1, :]
    group = lane // 8
    mixed_columns = jnp.zeros((size, LANES), jnp.float32)
    for shift in range(1 - NV, NV):
        factor = jnp.zeros((1, LANES), jnp.float32)
        for v in range(NV):
            if 0 <= v - shift < NV:
                factor = jnp.where(group == v, mix[v][v - shift], factor)
        source = beyond if shift == 0 else pltpu.roll(beyond, (8 * shift) % LANES, axis=1)
        mixed_columns = mixed_columns + factor * source
    column_rate = stencil(
        beyond,
        pltpu.roll(beyond, LANES - 2, axis=1),
        pltpu.roll(beyond, 2, axis=1),
        packed[TOP - 1 : end - 1, :]
        + packed[TOP + 1 : end + 1, :]
        + pltpu.roll(beyond + edge_ref[...], 1 + (LANES - 2) * (1 - sec), axis=1),
        mixed_columns,
    )
    column_section = beyond + TIME_STEP * column_rate

    row = lax.broadcasted_iota(jnp.int32, (8, LANES), 0)
    inside_rows = jnp.where(row < 4, inside_before, inside_after)
    row_cells = []
    row_others = []
    row_columns = jnp.where(
        row < 4, before_ref[8 * NV : 8 * NV + 1, :], after_ref[8 * NV : 8 * NV + 1, :]
    )
    for v in range(NV):
        cells = jnp.concatenate(
            [before_ref[8 * v : 8 * v + 4, :], after_ref[8 * v : 8 * v + 4, :]], axis=0
        )
        outer = jnp.concatenate(
            [before_ref[8 * v + 4 : 8 * v + 8, :], after_ref[8 * v + 4 : 8 * v + 8, :]], axis=0
        )
        inner = jnp.concatenate(
            [top_ref[8 * v : 8 * v + 4, :], bottom_ref[8 * v : 8 * v + 4, :]], axis=0
        )
        columns = jnp.zeros((8, LANES), jnp.float32)
        for xi in (1, 2):
            moved = pltpu.roll(row_columns, LANES - 1 - (8 * v + 2 * xi), axis=1)
            columns = jnp.where((row == xi) | (row == 4 + xi), moved, columns)
        across = (
            keep_low * pltpu.roll(cells, 1, axis=1)
            + keep_high * pltpu.roll(cells, LANES - 1, axis=1)
            + at_open * columns
        )
        row_cells.append(cells)
        row_others.append(outer + inner + across)
    for v in range(NV):
        cells = row_cells[v]
        rate = stencil(
            cells,
            pltpu.roll(cells, 7, axis=0),
            pltpu.roll(cells, 1, axis=0),
            row_others[v],
            mixed(row_cells, v),
        )
        after = inside_rows * (cells + TIME_STEP * rate)
        for xi in (1, 2):
            section[v, xi, TOP - 1 : TOP, :] = after[xi : xi + 1, :]
            section[v, xi, end : end + 1, :] = after[4 + xi : 5 + xi, :]

    for v in range(NV):
        for xi in range(4):
            field[v, xi, TOP:end, :] = slab(low_ref, state_ref, high_ref, v, xi)[...]
            field[v, xi, TOP - 1 : TOP, :] = before_ref[8 * v + xi : 8 * v + xi + 1, :]
            field[v, xi, end : end + 1, :] = after_ref[8 * v + xi : 8 * v + xi + 1, :]

    def center(v, x):
        if x < 0:
            return low_ref[v, 0]
        if x > 3:
            return high_ref[v, 1]
        return field[v, x, TOP:end, :]

    for xi in range(4):
        cells = [center(w, xi) for w in range(NV)]
        for v in range(NV):
            others = (
                field[v, xi, TOP - 1 : end - 1, :]
                + field[v, xi, TOP + 1 : end + 1, :]
                + along_z(cells[v], beyond, v, xi)
            )
            rate = stencil(
                cells[v], center(v, xi + 1), center(v, xi - 1), others, mixed(cells, v)
            )
            after = cells[v] + TIME_STEP * rate
            if xi == 0:
                after = inside_low * after
            if xi == 3:
                after = inside_high * after
            section[v, xi, TOP:end, :] = after
            if xi in (1, 2):
                out_ref[v, xi - 1] = cells[v] + 0.5 * TIME_STEP * rate

    for xi in (1, 2):
        cells = [section[w, xi, TOP:end, :] for w in range(NV)]
        for v in range(NV):
            others = (
                section[v, xi, TOP - 1 : end - 1, :]
                + section[v, xi, TOP + 1 : end + 1, :]
                + along_z(cells[v], column_section, v, xi)
            )
            rate = stencil(
                cells[v],
                section[v, xi + 1, TOP:end, :],
                section[v, xi - 1, TOP:end, :],
                others,
                mixed(cells, v),
            )
            final = out_ref[v, xi - 1] + 0.5 * TIME_STEP * rate
            out_ref[v, xi - 1] = final
            if v == 2:
                part_ref[xi - 1] = final[:8, :]


def shards(
    state, mixing, wall_weight, patch_map, block_map, shell_disp, shell_vel, connect, stiffness
):
    nfx, nfy, nsec = (lax.axis_size(axis) for axis in ("fx", "fy", "sec"))
    up_x = [(i, i + 1) for i in range(nfx - 1)]
    down_x = [(i + 1, i) for i in range(nfx - 1)]
    up_y = [(i, i + 1) for i in range(nfy - 1)]
    down_y = [(i + 1, i) for i in range(nfy - 1)]

    offered, sent, weight = offer(
        patch_map.reshape(2), block_map.reshape(2), wall_weight, state, nfx * nsec
    )
    offered = lax.all_to_all(offered, ("fx", "sec"), 0, 0, tiled=True)
    low = lax.ppermute(sent, "fx", up_x)
    high = lax.ppermute(sent, "fx", down_x)

    partial = kernel_call(collect_body, f32(nfy, NB, LANES), [VM])(offered)
    loads = lax.all_to_all(partial, "fy", 0, 0, tiled=True)

    block = f32(NB, LANES)
    couple, disp, vel = kernel_call(
        couple_body, (f32(NB, NB, LANES), block, block), [VM] * 4
    )(
        connect[0].T,
        stiffness[0],
        shell_disp.reshape(NB, LANES),
        shell_vel.reshape(NB, LANES),
    )
    span = f32(8 * NV + 8, LANES)
    top, bottom, beyond = kernel_call(
        second_round_body, (span, span, f32(32, LANES)), [VM] * 4, cost=LONG
    )(low, sent, high, offered)
    before = lax.ppermute(bottom, "fy", up_y)
    after = lax.ppermute(top, "fy", down_y)

    new_disp, new_vel, walls = kernel_call(
        shell_body, (block, block, f32(nfx, 2, LANES)), [VM] * 5 + [ANY]
    )(loads, offered, couple, disp, vel, top)
    walls = lax.all_to_all(walls, "fx", 0, 0, tiled=True)

    fluid, part = kernel_call(
        fluid_body,
        (f32(*state.shape), f32(2, 8, LANES)),
        [SM] + [VM] * 8,
        scratch=[
            pltpu.VMEM((NV, 4, ROWS, LANES), jnp.float32),
            pltpu.VMEM((NV, 4, ROWS, LANES), jnp.float32),
            pltpu.VMEM((ROWS, LANES), jnp.float32),
            pltpu.VMEM((32, LANES), jnp.float32),
        ],
        cost=LONG,
    )(mixing, low, sent, high, beyond, top, bottom, before, after)
    new_state = finish(walls, weight, part, fluid)
    return (new_state, new_disp.reshape(1, -1), new_vel.reshape(1, -1))


def solution(mesh):
    return jax.shard_map(
        shards,
        mesh=mesh,
        in_specs=(
            P(None, "fx", "fy", "sec"),
            P(),
            P("fx", "fy", "sec"),
            P("fx", "fy", "sec", None),
            P("fx", "fy", "sec", None),
            P("fx", None),
            P("fx", None),
            P("fx", None, None),
            P("fx", None, None),
        ),
        out_specs=(P(None, "fx", "fy", "sec"), P("fx", None), P("fx", None)),
        check_vma=False,
    )
```

```python
import jax
import jax.numpy as jnp
from jax import lax
from jax.experimental import pallas as pl
from jax.experimental.pallas import tpu as pltpu
from jax.sharding import PartitionSpec as P

NV = 5
NB = 32
SUBCYCLES = 4
LANES = 128

DIFFUSION = 0.25
TRANSPORT = 0.5
TIME_STEP = 0.2
SHELL_STEP = 0.25
DAMPING = 0.1

TOP = 8
ROWS = 48

LONG = 3_800_000_000

VM = pl.BlockSpec(memory_space=pltpu.VMEM)
SM = pl.BlockSpec(memory_space=pltpu.SMEM)
ANY = pl.BlockSpec(memory_space=pl.ANY)
HBM = pl.BlockSpec(memory_space=pltpu.HBM)
SMALL = pltpu.CompilerParams(vmem_limit_bytes=8 * 1024 * 1024)


def kernel_call(body, outs, ins, scratch=(), cost=20000, params=SMALL):
    return pl.pallas_call(
        body,
        out_shape=outs,
        in_specs=ins,
        out_specs=jax.tree.map(lambda _: VM, outs),
        scratch_shapes=scratch,
        compiler_params=params,
        cost_estimate=pl.CostEstimate(flops=cost, bytes_accessed=cost, transcendentals=0),
    )


def f32(*shape):
    return jax.ShapeDtypeStruct(shape, jnp.float32)


def terms(x):
    found = []
    for _ in range(3):
        term = x.astype(jnp.bfloat16)
        x = x - term.astype(jnp.float32)
        found.append(term)
    return found


def product(select, x, axis=0):
    select = select.astype(jnp.bfloat16)
    total = None
    for term in terms(x):
        part = lax.dot_general(
            select, term, (((1,), (axis,)), ((), ())), preferred_element_type=jnp.float32
        )
        total = part if total is None else total + part
    return total


def offer_body(
    patch_hbm,
    block_hbm,
    weight_hbm,
    state_hbm,
    out_ref,
    patch_ref,
    block_ref,
    weight_ref,
    state_ref,
    arrived,
):
    copies = [
        pltpu.make_async_copy(source, target, arrived.at[place])
        for place, (source, target) in enumerate(
            (
                (state_hbm, state_ref),
                (patch_hbm, patch_ref),
                (block_hbm, block_ref),
                (weight_hbm, weight_ref),
            )
        )
    ]
    for copy in copies:
        copy.start()
    for copy in copies:
        copy.wait()
    sec = lax.axis_index("sec")
    column = lax.broadcasted_iota(jnp.int32, (8, LANES), 0)
    lane = lax.broadcasted_iota(jnp.int32, (8, LANES), 1)
    wanted = (lane == column + (LANES - 2) * (1 - sec)).astype(jnp.float32)
    columns = product(wanted, state_ref[...].reshape(-1, LANES), axis=1)
    rows = [weight_ref[tile] * state_ref[NV - 1, tile, 0:1, :] for tile in range(2)]
    for tile in range(2):
        target = patch_ref[tile] * NB + block_ref[tile]
        target = jnp.full((1, LANES // 2), target.astype(jnp.float32))
        values = columns[tile : tile + 1, :]
        rows += [values[:, :LANES], values[:, LANES : 2 * LANES]]
        rows.append(jnp.concatenate([values[:, 2 * LANES :], target], axis=1))
    rows = jnp.concatenate(rows, axis=0)
    for receiver in range(out_ref.shape[0]):
        out_ref[receiver] = rows


def offer(patch_map, block_map, weight, state, receivers):
    return kernel_call(
        offer_body,
        f32(receivers, 8, LANES),
        [HBM] * 4,
        scratch=[
            pltpu.SMEM((2,), jnp.int32),
            pltpu.SMEM((2,), jnp.int32),
            pltpu.VMEM(weight.shape, jnp.float32),
            pltpu.VMEM(state.shape, jnp.float32),
            pltpu.SemaphoreType.DMA((4,)),
        ],
        params=None,
    )(patch_map, block_map, weight, state)


def targets_of(rows):
    lane = lax.broadcasted_iota(jnp.int32, (8, LANES), 1)
    return jnp.where(lane < LANES // 2, pltpu.roll(rows, LANES // 2, axis=1), rows)


def collect_body(offered_ref, out_ref):
    base = (lax.axis_index("fx") * NB).astype(jnp.float32)
    block = lax.broadcasted_iota(jnp.int32, (NB, LANES), 0).astype(jnp.float32) + base
    sums = [jnp.zeros((NB, LANES), jnp.float32) for _ in range(4)]
    for sender in range(offered_ref.shape[0]):
        rows = offered_ref[sender]
        targets = targets_of(rows)
        for tile in range(2):
            load = rows[tile : tile + 1, :]
            target = targets[4 + 3 * tile : 5 + 3 * tile, :]
            slot = (2 * sender + tile) % 4
            sums[slot] = sums[slot] + jnp.where(block == target, load, 0.0)
    total = (sums[0] + sums[1]) + (sums[2] + sums[3])
    for receiver in range(out_ref.shape[0]):
        out_ref[receiver] = total


def couple_body(
    connect_ref, stiff_ref, disp_ref, vel_ref, weight_ref, out_ref, disp_out, vel_out, weight_out
):
    elements = stiff_ref.shape[0]
    block = lax.broadcasted_iota(jnp.int32, (NB, elements), 0)
    first = connect_ref[0:1, :]
    second = connect_ref[1:2, :]
    ends = (block == first).astype(jnp.float32) - (block == second).astype(jnp.float32)
    pairs = [(ends * ends[a : a + 1, :]).astype(jnp.bfloat16) for a in range(NB)]
    pairs = jnp.concatenate(pairs, axis=0)
    out_ref[...] = product(pairs, stiff_ref[...]).reshape(NB, NB, LANES)
    disp_out[...] = disp_ref[...]
    vel_out[...] = vel_ref[...]
    weight_out[...] = weight_ref[...]


def shell_body(
    loads_ref, offered_ref, couple_ref, disp_ref, vel_ref, _, disp_out, vel_out, wall_out
):
    base = (lax.axis_index("fx") * NB).astype(jnp.float32)
    sec = lax.axis_index("sec")
    disp = disp_ref[...]
    vel = vel_ref[...]
    load = loads_ref[0]
    for sender in range(1, loads_ref.shape[0]):
        load = load + loads_ref[sender]
    total = jnp.zeros_like(disp)
    for _ in range(SUBCYCLES):
        inner = [jnp.zeros_like(disp) for _ in range(4)]
        for a in range(NB):
            inner[a % 4] = inner[a % 4] + couple_ref[a] * disp[a : a + 1, :]
        inner = (inner[0] + inner[1]) + (inner[2] + inner[3])
        vel = vel + SHELL_STEP * (load - inner - DAMPING * vel)
        disp = disp + SHELL_STEP * vel
        total = total + disp
    wall = total * (1.0 / SUBCYCLES)
    block = lax.broadcasted_iota(jnp.int32, (NB, LANES), 0).astype(jnp.float32) + base
    for peer in range(wall_out.shape[0]):
        targets = targets_of(offered_ref[2 * peer + sec])
        for tile in range(2):
            target = targets[4 + 3 * tile : 5 + 3 * tile, :]
            wanted = jnp.where(block == target, wall, 0.0)
            wall_out[peer, tile : tile + 1, :] = jnp.sum(wanted, axis=0, keepdims=True)
    disp_out[...] = disp
    vel_out[...] = vel


def finish_body(walls_ref, weight_ref, part_ref, _, out_ref):
    wall = walls_ref[0]
    for owner in range(1, walls_ref.shape[0]):
        wall = wall + walls_ref[owner]
    row = lax.broadcasted_iota(jnp.int32, (8, LANES), 0)
    for tile in range(2):
        gain = weight_ref[tile] * wall[tile : tile + 1, :]
        out_ref[0, tile] = part_ref[tile] + jnp.where(row == 0, gain, 0.0)


def finish(walls, weight, part, state):
    return pl.pallas_call(
        finish_body,
        grid=(1,),
        out_shape=f32(*state.shape),
        in_specs=[VM, VM, VM, ANY],
        out_specs=pl.BlockSpec((1, 2, 8, LANES), lambda i: (2, 0, 0, 0)),
        input_output_aliases={3: 0},
        compiler_params=SMALL,
        cost_estimate=pl.CostEstimate(flops=4096, bytes_accessed=65536, transcendentals=0),
    )(walls, weight, part, state)


def sides(axis, near, far):
    even = lax.rem(lax.axis_index(axis), 2) == 0
    return jnp.where(even, far, near), jnp.where(even, near, far)


def slab(near_ref, state_ref, far_ref, v, xi, rows=slice(None)):
    if xi < 1:
        return sides("fx", near_ref[v, 1 + xi, rows, :], far_ref[v, 1 + xi, rows, :])[0]
    if xi > 2:
        return sides("fx", near_ref[v, xi - 3, rows, :], far_ref[v, xi - 3, rows, :])[1]
    return state_ref[v, xi - 1, rows, :]


def pack_columns(slabs, out_ref):
    lane = lax.broadcasted_iota(jnp.int32, (32, LANES), 1)

    def pack(shift):
        packed = jnp.zeros((32, LANES), jnp.float32)
        for (v, xi), cells_ref in slabs.items():
            first = 8 * v + 2 * xi
            cells = cells_ref[...]
            moved = pltpu.roll(cells, first + shift, axis=1) if first + shift else cells
            packed = jnp.where((lane == first) | (lane == first + 1), moved, packed)
        out_ref[...] = packed

    sec = lax.axis_index("sec")
    pl.when(sec == 0)(lambda: pack(2))
    pl.when(sec == 1)(lambda: pack(0))


def unpack_columns(offered_ref):
    sec = lax.axis_index("sec")
    fx = lax.axis_index("fx")
    last = lax.axis_size("fx") - 1
    rows = [
        offered_ref[2 * jnp.maximum(fx - 1, 0) + 1 - sec] * (fx > 0).astype(jnp.float32),
        offered_ref[2 * fx + 1 - sec],
        offered_ref[2 * jnp.minimum(fx + 1, last) + 1 - sec] * (fx < last).astype(jnp.float32),
        jnp.zeros((8, LANES), jnp.float32),
    ]
    rows = jnp.concatenate(rows, axis=0)

    def place(shape):
        l = lax.broadcasted_iota(jnp.int32, shape, 0)
        xi = (l & 7) >> 1
        neighbour = jnp.where(xi == 0, 0, jnp.where(xi == 3, 2, 1))
        return neighbour, l & 1, 2 * (l >> 3) + 1 - (xi & 1)

    neighbour, column, source = place((LANES, 32))
    row = 8 * neighbour + 2 + 3 * column + (source >> 2)
    here = lax.broadcasted_iota(jnp.int32, (LANES, 32), 1) == row
    here &= lax.broadcasted_iota(jnp.int32, (LANES, 32), 0) < 8 * NV
    lines = product(here.astype(jnp.float32), rows)
    _, _, source = place((LANES, LANES))
    position = lax.broadcasted_iota(jnp.int32, (LANES, LANES), 1)
    lines = jnp.where((position >> 5) == (source & 3), lines, 0.0)
    position = lax.broadcasted_iota(jnp.int32, (32, LANES), 1)
    y = lax.broadcasted_iota(jnp.int32, (32, LANES), 0)
    return product(((position & 31) == y).astype(jnp.float32), lines, axis=1)


def second_round_body(
    near_ref, state_ref, far_ref, offered_ref, to_near_ref, to_far_ref, beyond_ref
):
    beyond_ref[...] = unpack_columns(offered_ref)
    last = state_ref.shape[2] - 1

    def put(spot, low, high):
        to_far, to_near = sides("fy", high, low)
        to_near_ref[spot : spot + 1, :] = to_near
        to_far_ref[spot : spot + 1, :] = to_far

    for place in range(2):
        low = slice(place, place + 1)
        high = slice(last - place, last - place + 1)
        for v in range(NV):
            for xi in range(4):
                put(
                    8 * v + 4 * place + xi,
                    slab(near_ref, state_ref, far_ref, v, xi, low),
                    slab(near_ref, state_ref, far_ref, v, xi, high),
                )
        put(8 * NV + place, beyond_ref[low, :], beyond_ref[high, :])
    for out in (to_near_ref, to_far_ref):
        out[8 * NV + 2 :, :] = jnp.zeros((6, LANES), jnp.float32)


def stencil(center, ahead, behind, others, mixed):
    beside = ahead + behind + others
    return DIFFUSION * (beside - 6.0 * center) - TRANSPORT * 0.5 * (ahead - behind) + mixed


def fluid_body(
    mixing_ref,
    near_ref,
    state_ref,
    far_ref,
    beyond_ref,
    to_near_ref,
    to_far_ref,
    from_near_ref,
    from_far_ref,
    out_ref,
    part_ref,
    field,
    section,
    packed,
    edge_ref,
):
    top, bottom = sides("fy", to_near_ref[...], to_far_ref[...])
    before, after = sides("fy", from_near_ref[...], from_far_ref[...])
    beyond = beyond_ref[...]
    pack_columns({(v, xi): state_ref.at[v, xi - 1] for v in range(NV) for xi in (1, 2)}, edge_ref)
    size = state_ref.shape[2]
    end = TOP + size
    sec = lax.axis_index("sec")
    fx = lax.axis_index("fx")
    fy = lax.axis_index("fy")
    inside_low = (fx > 0).astype(jnp.float32)
    inside_high = (fx < lax.axis_size("fx") - 1).astype(jnp.float32)
    inside_before = (fy > 0).astype(jnp.float32)
    inside_after = (fy < lax.axis_size("fy") - 1).astype(jnp.float32)
    mix = [[mixing_ref[v, w] for w in range(NV)] for v in range(NV)]

    lane = lax.broadcasted_iota(jnp.int32, (1, LANES), 1)
    open_lane = (LANES - 1) * (1 - sec)
    keep_low = (lane != 0).astype(jnp.float32)
    keep_high = (lane != LANES - 1).astype(jnp.float32)
    at_open = (lane == open_lane).astype(jnp.float32)

    def along_z(cells, columns, v, xi):
        moved = pltpu.roll(columns, LANES - 1 - (8 * v + 2 * xi), axis=1)
        return (
            keep_low * pltpu.roll(cells, 1, axis=1)
            + keep_high * pltpu.roll(cells, LANES - 1, axis=1)
            + at_open * moved
        )

    def mixed(cells, v):
        total = mix[v][0] * cells[0]
        for w in range(1, NV):
            total = total + mix[v][w] * cells[w]
        return total

    packed[TOP:end, :] = beyond
    packed[TOP - 1 : TOP, :] = before[8 * NV : 8 * NV + 1, :]
    packed[end : end + 1, :] = after[8 * NV : 8 * NV + 1, :]
    group = lane // 8
    mixed_columns = jnp.zeros((size, LANES), jnp.float32)
    for shift in range(1 - NV, NV):
        factor = jnp.zeros((1, LANES), jnp.float32)
        for v in range(NV):
            if 0 <= v - shift < NV:
                factor = jnp.where(group == v, mix[v][v - shift], factor)
        source = beyond if shift == 0 else pltpu.roll(beyond, (8 * shift) % LANES, axis=1)
        mixed_columns = mixed_columns + factor * source
    column_rate = stencil(
        beyond,
        pltpu.roll(beyond, LANES - 2, axis=1),
        pltpu.roll(beyond, 2, axis=1),
        packed[TOP - 1 : end - 1, :]
        + packed[TOP + 1 : end + 1, :]
        + pltpu.roll(beyond + edge_ref[...], 1 + (LANES - 2) * (1 - sec), axis=1),
        mixed_columns,
    )
    column_section = beyond + TIME_STEP * column_rate

    row = lax.broadcasted_iota(jnp.int32, (8, LANES), 0)
    inside_rows = jnp.where(row < 4, inside_before, inside_after)
    row_cells = []
    row_others = []
    row_columns = jnp.where(
        row < 4, before[8 * NV : 8 * NV + 1, :], after[8 * NV : 8 * NV + 1, :]
    )
    for v in range(NV):
        cells = jnp.concatenate(
            [before[8 * v : 8 * v + 4, :], after[8 * v : 8 * v + 4, :]], axis=0
        )
        outer = jnp.concatenate(
            [before[8 * v + 4 : 8 * v + 8, :], after[8 * v + 4 : 8 * v + 8, :]], axis=0
        )
        inner = jnp.concatenate(
            [top[8 * v : 8 * v + 4, :], bottom[8 * v : 8 * v + 4, :]], axis=0
        )
        columns = jnp.zeros((8, LANES), jnp.float32)
        for xi in (1, 2):
            moved = pltpu.roll(row_columns, LANES - 1 - (8 * v + 2 * xi), axis=1)
            columns = jnp.where((row == xi) | (row == 4 + xi), moved, columns)
        across = (
            keep_low * pltpu.roll(cells, 1, axis=1)
            + keep_high * pltpu.roll(cells, LANES - 1, axis=1)
            + at_open * columns
        )
        row_cells.append(cells)
        row_others.append(outer + inner + across)
    for v in range(NV):
        cells = row_cells[v]
        rate = stencil(
            cells,
            pltpu.roll(cells, 7, axis=0),
            pltpu.roll(cells, 1, axis=0),
            row_others[v],
            mixed(row_cells, v),
        )
        later = inside_rows * (cells + TIME_STEP * rate)
        for xi in (1, 2):
            section[v, xi, TOP - 1 : TOP, :] = later[xi : xi + 1, :]
            section[v, xi, end : end + 1, :] = later[4 + xi : 5 + xi, :]

    for v in range(NV):
        for xi in range(4):
            field[v, xi, TOP:end, :] = slab(near_ref, state_ref, far_ref, v, xi)
            field[v, xi, TOP - 1 : TOP, :] = before[8 * v + xi : 8 * v + xi + 1, :]
            field[v, xi, end : end + 1, :] = after[8 * v + xi : 8 * v + xi + 1, :]

    def center(v, x):
        if x < 0 or x > 3:
            return slab(near_ref, state_ref, far_ref, v, x)
        return field[v, x, TOP:end, :]

    for xi in range(4):
        cells = [center(w, xi) for w in range(NV)]
        for v in range(NV):
            others = (
                field[v, xi, TOP - 1 : end - 1, :]
                + field[v, xi, TOP + 1 : end + 1, :]
                + along_z(cells[v], beyond, v, xi)
            )
            rate = stencil(
                cells[v], center(v, xi + 1), center(v, xi - 1), others, mixed(cells, v)
            )
            later = cells[v] + TIME_STEP * rate
            if xi == 0:
                later = inside_low * later
            if xi == 3:
                later = inside_high * later
            section[v, xi, TOP:end, :] = later
            if xi in (1, 2):
                out_ref[v, xi - 1] = cells[v] + 0.5 * TIME_STEP * rate

    for xi in (1, 2):
        cells = [section[w, xi, TOP:end, :] for w in range(NV)]
        for v in range(NV):
            others = (
                section[v, xi, TOP - 1 : end - 1, :]
                + section[v, xi, TOP + 1 : end + 1, :]
                + along_z(cells[v], column_section, v, xi)
            )
            rate = stencil(
                cells[v],
                section[v, xi + 1, TOP:end, :],
                section[v, xi - 1, TOP:end, :],
                others,
                mixed(cells, v),
            )
            final = out_ref[v, xi - 1] + 0.5 * TIME_STEP * rate
            out_ref[v, xi - 1] = final
            if v == 2:
                part_ref[xi - 1] = final[:8, :]


def shards(
    state, mixing, wall_weight, patch_map, block_map, shell_disp, shell_vel, connect, stiffness
):
    nfx, nfy, nsec = (lax.axis_size(axis) for axis in ("fx", "fy", "sec"))
    near_x, far_x, near_y, far_y = (
        [pair for i in range(first, n - 1, 2) for pair in ((i, i + 1), (i + 1, i))]
        for n in (nfx, nfy)
        for first in (0, 1)
    )

    offered = offer(
        patch_map.reshape(2), block_map.reshape(2), wall_weight, state, nfx * nsec
    )
    offered = lax.all_to_all(offered, ("fx", "sec"), 0, 0, tiled=True)
    near = lax.ppermute(state, "fx", near_x)
    far = lax.ppermute(state, "fx", far_x)

    partial = kernel_call(collect_body, f32(nfy, NB, LANES), [VM])(offered)
    loads = lax.all_to_all(partial, "fy", 0, 0, tiled=True)

    block = f32(NB, LANES)
    couple, disp, vel, weight = kernel_call(
        couple_body, (f32(NB, NB, LANES), block, block, f32(*wall_weight.shape)), [VM] * 5
    )(
        connect[0].T,
        stiffness[0],
        shell_disp.reshape(NB, LANES),
        shell_vel.reshape(NB, LANES),
        wall_weight,
    )
    span = f32(8 * NV + 8, LANES)
    to_near, to_far, beyond = kernel_call(
        second_round_body, (span, span, f32(32, LANES)), [VM] * 4, cost=LONG
    )(near, state, far, offered)
    from_near = lax.ppermute(to_near, "fy", near_y)
    from_far = lax.ppermute(to_far, "fy", far_y)

    new_disp, new_vel, walls = kernel_call(
        shell_body, (block, block, f32(nfx, 2, LANES)), [VM] * 5 + [ANY]
    )(loads, offered, couple, disp, vel, to_near)
    walls = lax.all_to_all(walls, "fx", 0, 0, tiled=True)

    fluid, part = kernel_call(
        fluid_body,
        (f32(*state.shape), f32(2, 8, LANES)),
        [SM] + [VM] * 8,
        scratch=[
            pltpu.VMEM((NV, 4, ROWS, LANES), jnp.float32),
            pltpu.VMEM((NV, 4, ROWS, LANES), jnp.float32),
            pltpu.VMEM((ROWS, LANES), jnp.float32),
            pltpu.VMEM((32, LANES), jnp.float32),
        ],
        cost=LONG,
    )(mixing, near, state, far, beyond, to_near, to_far, from_near, from_far)
    new_state = finish(walls, weight, part, fluid)
    return (new_state, new_disp.reshape(1, -1), new_vel.reshape(1, -1))


def solution(mesh):
    return jax.shard_map(
        shards,
        mesh=mesh,
        in_specs=(
            P(None, "fx", "fy", "sec"),
            P(),
            P("fx", "fy", "sec"),
            P("fx", "fy", "sec", None),
            P("fx", "fy", "sec", None),
            P("fx", None),
            P("fx", None),
            P("fx", None, None),
            P("fx", None, None),
        ),
        out_specs=(P(None, "fx", "fy", "sec"), P("fx", None), P("fx", None)),
        check_vma=False,
    )
```

```python
import jax
import jax.numpy as jnp
from jax import lax
from jax.experimental import pallas as pl
from jax.experimental.pallas import tpu as pltpu
from jax.sharding import PartitionSpec as P

NV = 5
NB = 32
SUBCYCLES = 4
LANES = 128
HALF = 64
FY = ("z", "core")

DIFFUSION = 0.25
TRANSPORT = 0.5
TIME_STEP = 0.2
SHELL_STEP = 0.25
DAMPING = 0.1

TOP = 8
ROWS = 48

LONG = 3_800_000_000

VM = pl.BlockSpec(memory_space=pltpu.VMEM)
SM = pl.BlockSpec(memory_space=pltpu.SMEM)
ANY = pl.BlockSpec(memory_space=pl.ANY)
HBM = pl.BlockSpec(memory_space=pltpu.HBM)
SMALL = pltpu.CompilerParams(vmem_limit_bytes=8 * 1024 * 1024)


def kernel_call(body, outs, ins, scratch=(), cost=20000, params=SMALL):
    return pl.pallas_call(
        body,
        out_shape=outs,
        in_specs=ins,
        out_specs=jax.tree.map(lambda _: VM, outs),
        scratch_shapes=scratch,
        compiler_params=params,
        cost_estimate=pl.CostEstimate(flops=cost, bytes_accessed=cost, transcendentals=0),
    )


def f32(*shape):
    return jax.ShapeDtypeStruct(shape, jnp.float32)


def terms(x):
    found = []
    for _ in range(3):
        term = x.astype(jnp.bfloat16)
        x = x - term.astype(jnp.float32)
        found.append(term)
    return found


def product(select, x, axis=0):
    select = select.astype(jnp.bfloat16)
    total = None
    for term in terms(x):
        part = lax.dot_general(
            select, term, (((1,), (axis,)), ((), ())), preferred_element_type=jnp.float32
        )
        total = part if total is None else total + part
    return total


def offer_body(
    patch_hbm,
    block_hbm,
    weight_hbm,
    state_hbm,
    out_ref,
    patch_ref,
    block_ref,
    weight_ref,
    state_ref,
    arrived,
):
    copies = [
        pltpu.make_async_copy(source, target, arrived.at[place])
        for place, (source, target) in enumerate(
            (
                (state_hbm, state_ref),
                (patch_hbm, patch_ref),
                (block_hbm, block_ref),
                (weight_hbm, weight_ref),
            )
        )
    ]
    for copy in copies:
        copy.start()
    for copy in copies:
        copy.wait()
    sec = lax.axis_index("sec")
    column = lax.broadcasted_iota(jnp.int32, (8, LANES), 0)
    lane = lax.broadcasted_iota(jnp.int32, (8, LANES), 1)
    wanted = (lane == column + (LANES - 2) * (1 - sec)).astype(jnp.float32)
    columns = product(wanted, state_ref[...].reshape(-1, LANES), axis=1)
    rows = [weight_ref[tile] * state_ref[NV - 1, tile, 0:1, :] for tile in range(2)]
    for tile in range(2):
        target = patch_ref[tile] * NB + block_ref[tile]
        target = jnp.full((1, LANES // 2), target.astype(jnp.float32))
        values = columns[tile : tile + 1, :]
        rows += [values[:, :LANES], values[:, LANES : 2 * LANES]]
        rows.append(jnp.concatenate([values[:, 2 * LANES :], target], axis=1))
    rows = jnp.concatenate(rows, axis=0)
    for receiver in range(out_ref.shape[0]):
        out_ref[receiver] = rows


def offer(patch_map, block_map, weight, state, receivers):
    return kernel_call(
        offer_body,
        f32(receivers, 8, LANES),
        [HBM] * 4,
        scratch=[
            pltpu.SMEM((2,), jnp.int32),
            pltpu.SMEM((2,), jnp.int32),
            pltpu.VMEM(weight.shape, jnp.float32),
            pltpu.VMEM(state.shape, jnp.float32),
            pltpu.SemaphoreType.DMA((4,)),
        ],
        params=None,
    )(patch_map, block_map, weight, state)


def targets_of(rows):
    lane = lax.broadcasted_iota(jnp.int32, (8, LANES), 1)
    return jnp.where(lane < LANES // 2, pltpu.roll(rows, LANES // 2, axis=1), rows)


def halved(x, core):
    keep = jnp.where(core == 0, x[: NB // 2], x[NB // 2 :])
    move = jnp.where(core == 0, x[NB // 2 :], x[: NB // 2])
    lane = lax.broadcasted_iota(jnp.int32, keep.shape, 1)
    return jnp.where((lane < HALF) == (core == 0), keep, pltpu.roll(move, HALF, axis=1))


def doubled(rows):
    lane = lax.broadcasted_iota(jnp.int32, rows.shape, 1)
    moved = pltpu.roll(rows, HALF, axis=1)
    return jnp.where(lane < HALF, rows, moved), jnp.where(lane < HALF, moved, rows)


def joined(first, second):
    lane = lax.broadcasted_iota(jnp.int32, first.shape, 1)
    low = jnp.where(lane < HALF, first, pltpu.roll(second, HALF, axis=1))
    high = jnp.where(lane < HALF, pltpu.roll(first, HALF, axis=1), second)
    return low, high


def collect_body(offered_ref, out_ref):
    base = (lax.axis_index("fx") * NB).astype(jnp.float32)
    block = lax.broadcasted_iota(jnp.int32, (NB, LANES), 0).astype(jnp.float32) + base
    sums = [jnp.zeros((NB, LANES), jnp.float32) for _ in range(4)]
    for sender in range(offered_ref.shape[0]):
        rows = offered_ref[sender]
        targets = targets_of(rows)
        for tile in range(2):
            load = rows[tile : tile + 1, :]
            target = targets[4 + 3 * tile : 5 + 3 * tile, :]
            slot = (2 * sender + tile) % 4
            sums[slot] = sums[slot] + jnp.where(block == target, load, 0.0)
    total = (sums[0] + sums[1]) + (sums[2] + sums[3])
    halves = [halved(total, core) for core in range(2)]
    for receiver in range(out_ref.shape[0]):
        out_ref[receiver] = halves[receiver % 2]


def couple_body(
    connect_ref, stiff_ref, disp_ref, vel_ref, weight_ref, out_ref, disp_out, vel_out, weight_out
):
    core = lax.axis_index("core")
    elements = stiff_ref.shape[0]
    block = lax.broadcasted_iota(jnp.int32, (NB, elements), 0)
    first = connect_ref[0:1, :]
    second = connect_ref[1:2, :]
    ends = (block == first).astype(jnp.float32) - (block == second).astype(jnp.float32)
    pairs = [(ends * ends[a : a + 1, :]).astype(jnp.bfloat16) for a in range(NB)]
    pairs = jnp.concatenate(pairs, axis=0)
    low, high = doubled(stiff_ref[...])
    force = product(pairs, jnp.where(core == 0, low, high)).reshape(NB, NB, LANES)
    lane = lax.broadcasted_iota(jnp.int32, (NB, NB // 2, LANES), 2)
    out_ref[...] = jnp.where(lane < HALF, force[:, : NB // 2, :], force[:, NB // 2 :, :])
    disp_out[...] = halved(disp_ref[...], core)
    vel_out[...] = halved(vel_ref[...], core)
    weight_out[...] = weight_ref[...]


def shell_body(
    loads_ref, wanted_ref, from_near_ref, couple_ref, disp_ref, vel_ref, last_out, wall_out
):
    disp = disp_ref[...]
    vel = vel_ref[...]
    load = loads_ref[0]
    for sender in range(1, loads_ref.shape[0]):
        load = load + loads_ref[sender]
    total = jnp.zeros_like(disp)
    for _ in range(SUBCYCLES):
        low, high = doubled(disp)
        inner = [jnp.zeros_like(disp) for _ in range(4)]
        for a in range(NB // 2):
            inner[a % 2] = inner[a % 2] + couple_ref[a] * low[a : a + 1, :]
            inner[2 + a % 2] = inner[2 + a % 2] + couple_ref[NB // 2 + a] * high[a : a + 1, :]
        inner = (inner[0] + inner[1]) + (inner[2] + inner[3])
        vel = vel + SHELL_STEP * (load - inner - DAMPING * vel)
        disp = disp + SHELL_STEP * vel
        total = total + disp
    peers = wall_out.shape[0] // 2
    wall = jnp.concatenate(doubled(total * (1.0 / SUBCYCLES)), axis=0)
    wanted = jnp.concatenate([wanted_ref[...], from_near_ref[8 * NV + 8 :, :]], axis=0)
    found = product(wanted[:, :NB], wall)
    lane = lax.broadcasted_iota(jnp.int32, (peers, LANES), 1)
    own = jnp.where(lane < HALF, found[:peers], found[peers : 2 * peers])
    other = jnp.where(lane < HALF, found[2 * peers : 3 * peers], found[3 * peers :])
    core = lax.axis_index("core")
    even = jnp.where(core == 0, own, other)
    odd = jnp.where(core == 0, other, own)
    for peer in range(peers):
        wall_out[2 * peer] = even[peer : peer + 1, :]
        wall_out[2 * peer + 1] = odd[peer : peer + 1, :]
    last_out[: NB // 2, :] = disp
    last_out[NB // 2 :, :] = vel


def finish_body(
    walls_ref, weight_ref, part_ref, own_ref, other_ref, _, out_ref, disp_out, vel_out
):
    halves = []
    for core in range(2):
        wall = walls_ref[core]
        for owner in range(1, walls_ref.shape[0] // 2):
            wall = wall + walls_ref[2 * owner + core]
        halves.append(wall)
    walls = joined(*halves)
    row = lax.broadcasted_iota(jnp.int32, (8, LANES), 0)
    for tile in range(2):
        gain = weight_ref[tile] * walls[tile]
        out_ref[0, tile] = part_ref[tile] + jnp.where(row == 0, gain, 0.0)
    core = lax.axis_index("core")
    first = jnp.where(core == 0, own_ref[...], other_ref[...])
    second = jnp.where(core == 0, other_ref[...], own_ref[...])
    for rows, out in ((slice(0, NB // 2), disp_out), (slice(NB // 2, NB), vel_out)):
        low, high = joined(first[rows], second[rows])
        out[: NB // 2, :] = low
        out[NB // 2 :, :] = high


def finish(walls, weight, part, own, other, state):
    block = pl.BlockSpec((NB, LANES), lambda i: (0, 0))
    return pl.pallas_call(
        finish_body,
        grid=(1,),
        out_shape=(f32(*state.shape), f32(NB, LANES), f32(NB, LANES)),
        in_specs=[VM] * 5 + [ANY],
        out_specs=(pl.BlockSpec((1, 2, 8, LANES), lambda i: (2, 0, 0, 0)), block, block),
        input_output_aliases={5: 0},
        compiler_params=SMALL,
        cost_estimate=pl.CostEstimate(flops=4096, bytes_accessed=65536, transcendentals=0),
    )(walls, weight, part, own, other, state)


def sides(axis, near, far):
    even = lax.rem(lax.axis_index("core" if axis == "fy" else axis), 2) == 0
    return jnp.where(even, far, near), jnp.where(even, near, far)


def slab(near_ref, state_ref, far_ref, v, xi, rows=slice(None)):
    if xi < 1:
        return sides("fx", near_ref[v, 1 + xi, rows, :], far_ref[v, 1 + xi, rows, :])[0]
    if xi > 2:
        return sides("fx", near_ref[v, xi - 3, rows, :], far_ref[v, xi - 3, rows, :])[1]
    return state_ref[v, xi - 1, rows, :]


def pack_columns(slabs, out_ref):
    lane = lax.broadcasted_iota(jnp.int32, (32, LANES), 1)

    def pack(shift):
        packed = jnp.zeros((32, LANES), jnp.float32)
        for (v, xi), cells_ref in slabs.items():
            first = 8 * v + 2 * xi
            cells = cells_ref[...]
            moved = pltpu.roll(cells, first + shift, axis=1) if first + shift else cells
            packed = jnp.where((lane == first) | (lane == first + 1), moved, packed)
        out_ref[...] = packed

    sec = lax.axis_index("sec")
    pl.when(sec == 0)(lambda: pack(2))
    pl.when(sec == 1)(lambda: pack(0))


def unpack_columns(offered_ref):
    sec = lax.axis_index("sec")
    fx = lax.axis_index("fx")
    last = lax.axis_size("fx") - 1
    rows = [
        offered_ref[2 * jnp.maximum(fx - 1, 0) + 1 - sec] * (fx > 0).astype(jnp.float32),
        offered_ref[2 * fx + 1 - sec],
        offered_ref[2 * jnp.minimum(fx + 1, last) + 1 - sec] * (fx < last).astype(jnp.float32),
        jnp.zeros((8, LANES), jnp.float32),
    ]
    rows = jnp.concatenate(rows, axis=0)

    def place(shape):
        l = lax.broadcasted_iota(jnp.int32, shape, 0)
        xi = (l & 7) >> 1
        neighbour = jnp.where(xi == 0, 0, jnp.where(xi == 3, 2, 1))
        return neighbour, l & 1, 2 * (l >> 3) + 1 - (xi & 1)

    neighbour, column, source = place((LANES, 32))
    row = 8 * neighbour + 2 + 3 * column + (source >> 2)
    here = lax.broadcasted_iota(jnp.int32, (LANES, 32), 1) == row
    here &= lax.broadcasted_iota(jnp.int32, (LANES, 32), 0) < 8 * NV
    lines = product(here.astype(jnp.float32), rows)
    _, _, source = place((LANES, LANES))
    position = lax.broadcasted_iota(jnp.int32, (LANES, LANES), 1)
    lines = jnp.where((position >> 5) == (source & 3), lines, 0.0)
    position = lax.broadcasted_iota(jnp.int32, (32, LANES), 1)
    y = lax.broadcasted_iota(jnp.int32, (32, LANES), 0)
    return product(((position & 31) == y).astype(jnp.float32), lines, axis=1)


def wanted_blocks(offered_ref, peers):
    base = (lax.axis_index("fx") * NB).astype(jnp.float32)
    sec = lax.axis_index("sec")
    targets = [targets_of(offered_ref[2 * peer + sec]) for peer in range(peers)]
    rows = [found[4:5, :] for found in targets] + [found[7:8, :] for found in targets]
    rows = jnp.concatenate(rows, axis=0)
    lane = lax.broadcasted_iota(jnp.int32, rows.shape, 1)
    return ((lane.astype(jnp.float32) + base == rows) & (lane < NB)).astype(jnp.float32)


def second_round_body(
    near_ref, state_ref, far_ref, offered_ref, to_near_ref, to_far_ref, beyond_ref, wanted_ref
):
    beyond_ref[...] = unpack_columns(offered_ref)
    wanted = wanted_blocks(offered_ref, wanted_ref.shape[0] // 2)
    wanted_ref[...] = wanted
    to_near_ref[8 * NV + 8 :, :] = wanted
    last = state_ref.shape[2] - 1

    def put(spot, low, high):
        to_far, to_near = sides("fy", high, low)
        to_near_ref[spot : spot + 1, :] = to_near
        to_far_ref[spot : spot + 1, :] = to_far

    for place in range(2):
        low = slice(place, place + 1)
        high = slice(last - place, last - place + 1)
        for v in range(NV):
            for xi in range(4):
                put(
                    8 * v + 4 * place + xi,
                    slab(near_ref, state_ref, far_ref, v, xi, low),
                    slab(near_ref, state_ref, far_ref, v, xi, high),
                )
        put(8 * NV + place, beyond_ref[low, :], beyond_ref[high, :])
    for out in (to_near_ref, to_far_ref):
        out[8 * NV + 2 : 8 * NV + 8, :] = jnp.zeros((6, LANES), jnp.float32)


def stencil(center, ahead, behind, others, mixed):
    beside = ahead + behind + others
    return DIFFUSION * (beside - 6.0 * center) - TRANSPORT * 0.5 * (ahead - behind) + mixed


def fluid_body(
    mixing_ref,
    near_ref,
    state_ref,
    far_ref,
    beyond_ref,
    to_near_ref,
    to_far_ref,
    from_near_ref,
    from_far_ref,
    out_ref,
    part_ref,
    field,
    section,
    packed,
    edge_ref,
):
    rows = 8 * NV + 8
    top, bottom = sides("fy", to_near_ref[:rows, :], to_far_ref[...])
    before, after = sides("fy", from_near_ref[:rows, :], from_far_ref[...])
    beyond = beyond_ref[...]
    pack_columns({(v, xi): state_ref.at[v, xi - 1] for v in range(NV) for xi in (1, 2)}, edge_ref)
    size = state_ref.shape[2]
    end = TOP + size
    sec = lax.axis_index("sec")
    fx = lax.axis_index("fx")
    fy = 2 * lax.axis_index("z") + lax.axis_index("core")
    inside_low = (fx > 0).astype(jnp.float32)
    inside_high = (fx < lax.axis_size("fx") - 1).astype(jnp.float32)
    inside_before = (fy > 0).astype(jnp.float32)
    inside_after = (fy < 2 * lax.axis_size("z") - 1).astype(jnp.float32)
    mix = [[mixing_ref[v, w] for w in range(NV)] for v in range(NV)]

    lane = lax.broadcasted_iota(jnp.int32, (1, LANES), 1)
    open_lane = (LANES - 1) * (1 - sec)
    keep_low = (lane != 0).astype(jnp.float32)
    keep_high = (lane != LANES - 1).astype(jnp.float32)
    at_open = (lane == open_lane).astype(jnp.float32)

    def along_z(cells, columns, v, xi):
        moved = pltpu.roll(columns, LANES - 1 - (8 * v + 2 * xi), axis=1)
        return (
            keep_low * pltpu.roll(cells, 1, axis=1)
            + keep_high * pltpu.roll(cells, LANES - 1, axis=1)
            + at_open * moved
        )

    def mixed(cells, v):
        total = mix[v][0] * cells[0]
        for w in range(1, NV):
            total = total + mix[v][w] * cells[w]
        return total

    packed[TOP:end, :] = beyond
    packed[TOP - 1 : TOP, :] = before[8 * NV : 8 * NV + 1, :]
    packed[end : end + 1, :] = after[8 * NV : 8 * NV + 1, :]
    group = lane // 8
    mixed_columns = jnp.zeros((size, LANES), jnp.float32)
    for shift in range(1 - NV, NV):
        factor = jnp.zeros((1, LANES), jnp.float32)
        for v in range(NV):
            if 0 <= v - shift < NV:
                factor = jnp.where(group == v, mix[v][v - shift], factor)
        source = beyond if shift == 0 else pltpu.roll(beyond, (8 * shift) % LANES, axis=1)
        mixed_columns = mixed_columns + factor * source
    column_rate = stencil(
        beyond,
        pltpu.roll(beyond, LANES - 2, axis=1),
        pltpu.roll(beyond, 2, axis=1),
        packed[TOP - 1 : end - 1, :]
        + packed[TOP + 1 : end + 1, :]
        + pltpu.roll(beyond + edge_ref[...], 1 + (LANES - 2) * (1 - sec), axis=1),
        mixed_columns,
    )
    column_section = beyond + TIME_STEP * column_rate

    row = lax.broadcasted_iota(jnp.int32, (8, LANES), 0)
    inside_rows = jnp.where(row < 4, inside_before, inside_after)
    row_cells = []
    row_others = []
    row_columns = jnp.where(
        row < 4, before[8 * NV : 8 * NV + 1, :], after[8 * NV : 8 * NV + 1, :]
    )
    for v in range(NV):
        cells = jnp.concatenate(
            [before[8 * v : 8 * v + 4, :], after[8 * v : 8 * v + 4, :]], axis=0
        )
        outer = jnp.concatenate(
            [before[8 * v + 4 : 8 * v + 8, :], after[8 * v + 4 : 8 * v + 8, :]], axis=0
        )
        inner = jnp.concatenate(
            [top[8 * v : 8 * v + 4, :], bottom[8 * v : 8 * v + 4, :]], axis=0
        )
        columns = jnp.zeros((8, LANES), jnp.float32)
        for xi in (1, 2):
            moved = pltpu.roll(row_columns, LANES - 1 - (8 * v + 2 * xi), axis=1)
            columns = jnp.where((row == xi) | (row == 4 + xi), moved, columns)
        across = (
            keep_low * pltpu.roll(cells, 1, axis=1)
            + keep_high * pltpu.roll(cells, LANES - 1, axis=1)
            + at_open * columns
        )
        row_cells.append(cells)
        row_others.append(outer + inner + across)
    for v in range(NV):
        cells = row_cells[v]
        rate = stencil(
            cells,
            pltpu.roll(cells, 7, axis=0),
            pltpu.roll(cells, 1, axis=0),
            row_others[v],
            mixed(row_cells, v),
        )
        later = inside_rows * (cells + TIME_STEP * rate)
        for xi in (1, 2):
            section[v, xi, TOP - 1 : TOP, :] = later[xi : xi + 1, :]
            section[v, xi, end : end + 1, :] = later[4 + xi : 5 + xi, :]

    for v in range(NV):
        for xi in range(4):
            field[v, xi, TOP:end, :] = slab(near_ref, state_ref, far_ref, v, xi)
            field[v, xi, TOP - 1 : TOP, :] = before[8 * v + xi : 8 * v + xi + 1, :]
            field[v, xi, end : end + 1, :] = after[8 * v + xi : 8 * v + xi + 1, :]

    def center(v, x):
        if x < 0 or x > 3:
            return slab(near_ref, state_ref, far_ref, v, x)
        return field[v, x, TOP:end, :]

    for xi in range(4):
        cells = [center(w, xi) for w in range(NV)]
        for v in range(NV):
            others = (
                field[v, xi, TOP - 1 : end - 1, :]
                + field[v, xi, TOP + 1 : end + 1, :]
                + along_z(cells[v], beyond, v, xi)
            )
            rate = stencil(
                cells[v], center(v, xi + 1), center(v, xi - 1), others, mixed(cells, v)
            )
            later = cells[v] + TIME_STEP * rate
            if xi == 0:
                later = inside_low * later
            if xi == 3:
                later = inside_high * later
            section[v, xi, TOP:end, :] = later
            if xi in (1, 2):
                out_ref[v, xi - 1] = cells[v] + 0.5 * TIME_STEP * rate

    for xi in (1, 2):
        cells = [section[w, xi, TOP:end, :] for w in range(NV)]
        for v in range(NV):
            others = (
                section[v, xi, TOP - 1 : end - 1, :]
                + section[v, xi, TOP + 1 : end + 1, :]
                + along_z(cells[v], column_section, v, xi)
            )
            rate = stencil(
                cells[v],
                section[v, xi + 1, TOP:end, :],
                section[v, xi - 1, TOP:end, :],
                others,
                mixed(cells, v),
            )
            final = out_ref[v, xi - 1] + 0.5 * TIME_STEP * rate
            out_ref[v, xi - 1] = final
            if v == 2:
                part_ref[xi - 1] = final[:8, :]


def shards(
    state, mixing, wall_weight, patch_map, block_map, shell_disp, shell_vel, connect, stiffness
):
    nfx, nfy, nsec = (lax.axis_size(axis) for axis in ("fx", FY, "sec"))
    near_x, far_x, near_y, far_y = (
        [pair for i in range(first, n - 1, 2) for pair in ((i, i + 1), (i + 1, i))]
        for n in (nfx, nfy)
        for first in (0, 1)
    )

    offered = offer(
        patch_map.reshape(2), block_map.reshape(2), wall_weight, state, nfx * nsec
    )
    offered = lax.all_to_all(offered, ("fx", "sec"), 0, 0, tiled=True)
    near = lax.ppermute(state, "fx", near_x)
    far = lax.ppermute(state, "fx", far_x)

    partial = kernel_call(collect_body, f32(nfy, NB // 2, LANES), [VM])(offered)
    loads = lax.all_to_all(partial, FY, 0, 0, tiled=True)

    half = f32(NB // 2, LANES)
    couple, disp, vel, weight = kernel_call(
        couple_body,
        (f32(NB, NB // 2, LANES), half, half, f32(*wall_weight.shape)),
        [VM] * 5,
    )(
        connect[0].T,
        stiffness[0],
        shell_disp.reshape(NB, LANES),
        shell_vel.reshape(NB, LANES),
        wall_weight,
    )
    span = f32(8 * NV + 8, LANES)
    to_near, to_far, beyond, wanted = kernel_call(
        second_round_body,
        (f32(8 * NV + 8 + 2 * nfx, LANES), span, f32(32, LANES), f32(2 * nfx, LANES)),
        [VM] * 4,
        cost=LONG,
    )(near, state, far, offered)
    from_near = lax.ppermute(to_near, FY, near_y)
    from_far = lax.ppermute(to_far, FY, far_y)

    own, walls = kernel_call(
        shell_body, (f32(NB, LANES), f32(2 * nfx, 1, LANES)), [VM] * 6
    )(loads, wanted, from_near, couple, disp, vel)
    walls = lax.all_to_all(walls, ("fx", "core"), 0, 0, tiled=True)
    other = lax.ppermute(own, FY, near_y)

    fluid, part = kernel_call(
        fluid_body,
        (f32(*state.shape), f32(2, 8, LANES)),
        [SM] + [VM] * 8,
        scratch=[
            pltpu.VMEM((NV, 4, ROWS, LANES), jnp.float32),
            pltpu.VMEM((NV, 4, ROWS, LANES), jnp.float32),
            pltpu.VMEM((ROWS, LANES), jnp.float32),
            pltpu.VMEM((32, LANES), jnp.float32),
        ],
        cost=LONG,
    )(mixing, near, state, far, beyond, to_near, to_far, from_near, from_far)
    new_state, new_disp, new_vel = finish(walls, weight, part, own, other, fluid)
    return (new_state, new_disp.reshape(1, -1), new_vel.reshape(1, -1))


def solution(mesh):
    nfx, nfy, nsec = mesh.devices.shape
    mesh = jax.sharding.Mesh(
        mesh.devices.reshape(nfx, nfy // 2, 2, nsec), ("fx", "z", "core", "sec")
    )
    return jax.shard_map(
        shards,
        mesh=mesh,
        in_specs=(
            P(None, "fx", FY, "sec"),
            P(),
            P("fx", FY, "sec"),
            P("fx", FY, "sec", None),
            P("fx", FY, "sec", None),
            P("fx", None),
            P("fx", None),
            P("fx", None, None),
            P("fx", None, None),
        ),
        out_specs=(P(None, "fx", FY, "sec"), P("fx", None), P("fx", None)),
        check_vma=False,
    )
```

```python
import jax
import jax.numpy as jnp
from jax import lax
from jax.experimental import pallas as pl
from jax.experimental.pallas import tpu as pltpu
from jax.sharding import PartitionSpec as P

NV = 5
NB = 32
SUBCYCLES = 4
LANES = 128
HALF = 64
FY = ("z", "core")

DIFFUSION = 0.25
TRANSPORT = 0.5
TIME_STEP = 0.2
SHELL_STEP = 0.25
DAMPING = 0.1

TOP = 8
ROWS = 48

LONG = 3_800_000_000

VM = pl.BlockSpec(memory_space=pltpu.VMEM)
SM = pl.BlockSpec(memory_space=pltpu.SMEM)
ANY = pl.BlockSpec(memory_space=pl.ANY)
HBM = pl.BlockSpec(memory_space=pltpu.HBM)
SMALL = pltpu.CompilerParams(vmem_limit_bytes=8 * 1024 * 1024)


def kernel_call(body, outs, ins, scratch=(), cost=20000, params=SMALL):
    return pl.pallas_call(
        body,
        out_shape=outs,
        in_specs=ins,
        out_specs=jax.tree.map(lambda _: VM, outs),
        scratch_shapes=scratch,
        compiler_params=params,
        cost_estimate=pl.CostEstimate(flops=cost, bytes_accessed=cost, transcendentals=0),
    )


def f32(*shape):
    return jax.ShapeDtypeStruct(shape, jnp.float32)


def terms(x):
    found = []
    for _ in range(3):
        term = x.astype(jnp.bfloat16)
        x = x - term.astype(jnp.float32)
        found.append(term)
    return found


def product(select, x, axis=0):
    select = select.astype(jnp.bfloat16)
    total = None
    for term in terms(x):
        part = lax.dot_general(
            select, term, (((1,), (axis,)), ((), ())), preferred_element_type=jnp.float32
        )
        total = part if total is None else total + part
    return total


def offer_body(
    patch_hbm,
    block_hbm,
    weight_hbm,
    state_hbm,
    out_ref,
    patch_ref,
    block_ref,
    weight_ref,
    state_ref,
    arrived,
):
    copies = [
        pltpu.make_async_copy(source, target, arrived.at[place])
        for place, (source, target) in enumerate(
            (
                (state_hbm, state_ref),
                (patch_hbm, patch_ref),
                (block_hbm, block_ref),
                (weight_hbm, weight_ref),
            )
        )
    ]
    for copy in copies:
        copy.start()
    for copy in copies:
        copy.wait()
    sec = lax.axis_index("sec")
    column = lax.broadcasted_iota(jnp.int32, (8, LANES), 0)
    lane = lax.broadcasted_iota(jnp.int32, (8, LANES), 1)
    wanted = (lane == column + (LANES - 2) * (1 - sec)).astype(jnp.float32)
    columns = product(wanted, state_ref[...].reshape(-1, LANES), axis=1)
    rows = [weight_ref[tile] * state_ref[NV - 1, tile, 0:1, :] for tile in range(2)]
    for tile in range(2):
        target = patch_ref[tile] * NB + block_ref[tile]
        target = jnp.full((1, LANES // 2), target.astype(jnp.float32))
        values = columns[tile : tile + 1, :]
        rows += [values[:, :LANES], values[:, LANES : 2 * LANES]]
        rows.append(jnp.concatenate([values[:, 2 * LANES :], target], axis=1))
    rows = jnp.concatenate(rows, axis=0)
    for receiver in range(out_ref.shape[0]):
        out_ref[receiver] = rows


def offer(patch_map, block_map, weight, state, receivers):
    return kernel_call(
        offer_body,
        f32(receivers, 8, LANES),
        [HBM] * 4,
        scratch=[
            pltpu.SMEM((2,), jnp.int32),
            pltpu.SMEM((2,), jnp.int32),
            pltpu.VMEM(weight.shape, jnp.float32),
            pltpu.VMEM(state.shape, jnp.float32),
            pltpu.SemaphoreType.DMA((4,)),
        ],
        params=None,
    )(patch_map, block_map, weight, state)


def targets_of(rows):
    lane = lax.broadcasted_iota(jnp.int32, (8, LANES), 1)
    return jnp.where(lane < LANES // 2, pltpu.roll(rows, LANES // 2, axis=1), rows)


def halved(x, core):
    keep = jnp.where(core == 0, x[: NB // 2], x[NB // 2 :])
    move = jnp.where(core == 0, x[NB // 2 :], x[: NB // 2])
    lane = lax.broadcasted_iota(jnp.int32, keep.shape, 1)
    return jnp.where((lane < HALF) == (core == 0), keep, pltpu.roll(move, HALF, axis=1))


def doubled(rows):
    lane = lax.broadcasted_iota(jnp.int32, rows.shape, 1)
    moved = pltpu.roll(rows, HALF, axis=1)
    return jnp.where(lane < HALF, rows, moved), jnp.where(lane < HALF, moved, rows)


def joined(first, second):
    lane = lax.broadcasted_iota(jnp.int32, first.shape, 1)
    low = jnp.where(lane < HALF, first, pltpu.roll(second, HALF, axis=1))
    high = jnp.where(lane < HALF, pltpu.roll(first, HALF, axis=1), second)
    return low, high


def collect_body(offered_ref, out_ref):
    base = (lax.axis_index("fx") * NB).astype(jnp.float32)
    block = lax.broadcasted_iota(jnp.int32, (NB, LANES), 0).astype(jnp.float32) + base
    sums = [jnp.zeros((NB, LANES), jnp.float32) for _ in range(4)]
    for sender in range(offered_ref.shape[0]):
        rows = offered_ref[sender]
        targets = targets_of(rows)
        for tile in range(2):
            load = rows[tile : tile + 1, :]
            target = targets[4 + 3 * tile : 5 + 3 * tile, :]
            slot = (2 * sender + tile) % 4
            sums[slot] = sums[slot] + jnp.where(block == target, load, 0.0)
    total = (sums[0] + sums[1]) + (sums[2] + sums[3])
    halves = [halved(total, core) for core in range(2)]
    for receiver in range(out_ref.shape[0]):
        out_ref[receiver] = halves[receiver % 2]


def couple_body(
    connect_ref, stiff_ref, disp_ref, vel_ref, weight_ref, out_ref, disp_out, vel_out, weight_out
):
    core = lax.axis_index("core")
    elements = stiff_ref.shape[0]
    block = lax.broadcasted_iota(jnp.int32, (NB, elements), 0)
    first = connect_ref[0:1, :]
    second = connect_ref[1:2, :]
    ends = (block == first).astype(jnp.float32) - (block == second).astype(jnp.float32)
    pairs = [(ends * ends[a : a + 1, :]).astype(jnp.bfloat16) for a in range(NB)]
    pairs = jnp.concatenate(pairs, axis=0)
    low, high = doubled(stiff_ref[...])
    out_ref[...] = product(pairs, jnp.where(core == 0, low, high)).reshape(NB, NB, LANES)
    for source, out in ((disp_ref, disp_out), (vel_ref, vel_out)):
        low, high = doubled(source[...])
        out[...] = jnp.where(core == 0, low, high)
    weight_out[...] = weight_ref[...]


def shell_body(
    loads_ref, wanted_ref, from_near_ref, couple_ref, disp_ref, vel_ref, last_out, wall_out
):
    disp = disp_ref[...]
    vel = vel_ref[...]
    load = loads_ref[0]
    for sender in range(1, loads_ref.shape[0]):
        load = load + loads_ref[sender]
    load = jnp.concatenate(doubled(load), axis=0)
    total = jnp.zeros_like(disp)
    for _ in range(SUBCYCLES):
        inner = [jnp.zeros_like(disp) for _ in range(4)]
        for a in range(NB):
            inner[a % 4] = inner[a % 4] + couple_ref[a] * disp[a : a + 1, :]
        inner = (inner[0] + inner[1]) + (inner[2] + inner[3])
        vel = vel + SHELL_STEP * (load - inner - DAMPING * vel)
        disp = disp + SHELL_STEP * vel
        total = total + disp
    slots = wall_out.shape[0]
    wanted = wanted_ref[...] + from_near_ref[8 * NV + 8 :, :]
    found = jnp.dot(
        wanted[:, : 3 * NB].astype(jnp.bfloat16),
        jnp.concatenate(terms(total * (1.0 / SUBCYCLES)), axis=0),
        preferred_element_type=jnp.float32,
    )
    lane = lax.broadcasted_iota(jnp.int32, (slots, LANES), 1)
    wall_out[...] = jnp.where(lane < HALF, found[:slots], found[slots:])
    lane = lax.broadcasted_iota(jnp.int32, (NB // 2, LANES), 1)
    last_out[: NB // 2, :] = jnp.where(lane < HALF, disp[: NB // 2], disp[NB // 2 :])
    last_out[NB // 2 :, :] = jnp.where(lane < HALF, vel[: NB // 2], vel[NB // 2 :])


def finish_body(
    walls_ref, weight_ref, part_ref, own_ref, other_ref, _, out_ref, disp_out, vel_out
):
    wall = walls_ref[0:8, :]
    for first in range(8, walls_ref.shape[0], 8):
        wall = wall + walls_ref[first : first + 8, :]
    wall = wall + pltpu.roll(wall, 4, axis=0)
    wall = wall + pltpu.roll(wall, 2, axis=0)
    walls = joined(wall[0:1, :], wall[1:2, :])
    row = lax.broadcasted_iota(jnp.int32, (8, LANES), 0)
    for tile in range(2):
        gain = weight_ref[tile] * walls[tile]
        out_ref[0, tile] = part_ref[tile] + jnp.where(row == 0, gain, 0.0)
    core = lax.axis_index("core")
    first = jnp.where(core == 0, own_ref[...], other_ref[...])
    second = jnp.where(core == 0, other_ref[...], own_ref[...])
    for rows, out in ((slice(0, NB // 2), disp_out), (slice(NB // 2, NB), vel_out)):
        low, high = joined(first[rows], second[rows])
        out[: NB // 2, :] = low
        out[NB // 2 :, :] = high


def finish(walls, weight, part, own, other, state):
    block = pl.BlockSpec((NB, LANES), lambda i: (0, 0))
    return pl.pallas_call(
        finish_body,
        grid=(1,),
        out_shape=(f32(*state.shape), f32(NB, LANES), f32(NB, LANES)),
        in_specs=[VM] * 5 + [ANY],
        out_specs=(pl.BlockSpec((1, 2, 8, LANES), lambda i: (2, 0, 0, 0)), block, block),
        input_output_aliases={5: 0},
        compiler_params=SMALL,
        cost_estimate=pl.CostEstimate(flops=4096, bytes_accessed=65536, transcendentals=0),
    )(walls, weight, part, own, other, state)


def sides(axis, near, far):
    even = lax.rem(lax.axis_index("core" if axis == "fy" else axis), 2) == 0
    return jnp.where(even, far, near), jnp.where(even, near, far)


def slab(near_ref, state_ref, far_ref, v, xi, rows=slice(None)):
    if xi < 1:
        return sides("fx", near_ref[v, 1 + xi, rows, :], far_ref[v, 1 + xi, rows, :])[0]
    if xi > 2:
        return sides("fx", near_ref[v, xi - 3, rows, :], far_ref[v, xi - 3, rows, :])[1]
    return state_ref[v, xi - 1, rows, :]


def pack_columns(slabs, out_ref):
    lane = lax.broadcasted_iota(jnp.int32, (32, LANES), 1)

    def pack(shift):
        packed = jnp.zeros((32, LANES), jnp.float32)
        for (v, xi), cells_ref in slabs.items():
            first = 8 * v + 2 * xi
            cells = cells_ref[...]
            moved = pltpu.roll(cells, first + shift, axis=1) if first + shift else cells
            packed = jnp.where((lane == first) | (lane == first + 1), moved, packed)
        out_ref[...] = packed

    sec = lax.axis_index("sec")
    pl.when(sec == 0)(lambda: pack(2))
    pl.when(sec == 1)(lambda: pack(0))


def unpack_columns(offered_ref):
    sec = lax.axis_index("sec")
    fx = lax.axis_index("fx")
    last = lax.axis_size("fx") - 1
    rows = [
        offered_ref[2 * jnp.maximum(fx - 1, 0) + 1 - sec] * (fx > 0).astype(jnp.float32),
        offered_ref[2 * fx + 1 - sec],
        offered_ref[2 * jnp.minimum(fx + 1, last) + 1 - sec] * (fx < last).astype(jnp.float32),
        jnp.zeros((8, LANES), jnp.float32),
    ]
    rows = jnp.concatenate(rows, axis=0)

    def place(shape):
        l = lax.broadcasted_iota(jnp.int32, shape, 0)
        xi = (l & 7) >> 1
        neighbour = jnp.where(xi == 0, 0, jnp.where(xi == 3, 2, 1))
        return neighbour, l & 1, 2 * (l >> 3) + 1 - (xi & 1)

    neighbour, column, source = place((LANES, 32))
    row = 8 * neighbour + 2 + 3 * column + (source >> 2)
    here = lax.broadcasted_iota(jnp.int32, (LANES, 32), 1) == row
    here &= lax.broadcasted_iota(jnp.int32, (LANES, 32), 0) < 8 * NV
    lines = product(here.astype(jnp.float32), rows)
    _, _, source = place((LANES, LANES))
    position = lax.broadcasted_iota(jnp.int32, (LANES, LANES), 1)
    lines = jnp.where((position >> 5) == (source & 3), lines, 0.0)
    position = lax.broadcasted_iota(jnp.int32, (32, LANES), 1)
    y = lax.broadcasted_iota(jnp.int32, (32, LANES), 0)
    return product(((position & 31) == y).astype(jnp.float32), lines, axis=1)


def wanted_blocks(offered_ref, peers):
    base = (lax.axis_index("fx") * NB).astype(jnp.float32)
    sec = lax.axis_index("sec")
    targets = [targets_of(offered_ref[2 * peer + sec]) for peer in range(peers)]
    rows = [found[row : row + 1, :] for row in (4, 7) for found in targets for _ in range(2)]
    rows = jnp.concatenate(rows, axis=0)
    lane = lax.broadcasted_iota(jnp.int32, rows.shape, 1)
    here = (lax.broadcasted_iota(jnp.int32, rows.shape, 0) & 1) == lax.axis_index("core")
    asked = (lane & (NB - 1)).astype(jnp.float32) + base == rows
    return (asked & here & (lane < 3 * NB)).astype(jnp.float32)


def second_round_body(
    near_ref, state_ref, far_ref, offered_ref, to_near_ref, to_far_ref, beyond_ref, wanted_ref
):
    beyond_ref[...] = unpack_columns(offered_ref)
    wanted = wanted_blocks(offered_ref, wanted_ref.shape[0] // 4)
    wanted_ref[...] = wanted
    to_near_ref[8 * NV + 8 :, :] = wanted
    last = state_ref.shape[2] - 1

    def put(spot, low, high):
        to_far, to_near = sides("fy", high, low)
        to_near_ref[spot : spot + 1, :] = to_near
        to_far_ref[spot : spot + 1, :] = to_far

    for place in range(2):
        low = slice(place, place + 1)
        high = slice(last - place, last - place + 1)
        for v in range(NV):
            for xi in range(4):
                put(
                    8 * v + 4 * place + xi,
                    slab(near_ref, state_ref, far_ref, v, xi, low),
                    slab(near_ref, state_ref, far_ref, v, xi, high),
                )
        put(8 * NV + place, beyond_ref[low, :], beyond_ref[high, :])
    for out in (to_near_ref, to_far_ref):
        out[8 * NV + 2 : 8 * NV + 8, :] = jnp.zeros((6, LANES), jnp.float32)


def stencil(center, ahead, behind, others, mixed):
    beside = ahead + behind + others
    return DIFFUSION * (beside - 6.0 * center) - TRANSPORT * 0.5 * (ahead - behind) + mixed


def fluid_body(
    mixing_ref,
    near_ref,
    state_ref,
    far_ref,
    beyond_ref,
    to_near_ref,
    to_far_ref,
    from_near_ref,
    from_far_ref,
    out_ref,
    part_ref,
    field,
    section,
    packed,
    edge_ref,
):
    rows = 8 * NV + 8
    top, bottom = sides("fy", to_near_ref[:rows, :], to_far_ref[...])
    before, after = sides("fy", from_near_ref[:rows, :], from_far_ref[...])
    beyond = beyond_ref[...]
    pack_columns({(v, xi): state_ref.at[v, xi - 1] for v in range(NV) for xi in (1, 2)}, edge_ref)
    size = state_ref.shape[2]
    end = TOP + size
    sec = lax.axis_index("sec")
    fx = lax.axis_index("fx")
    fy = 2 * lax.axis_index("z") + lax.axis_index("core")
    inside_low = (fx > 0).astype(jnp.float32)
    inside_high = (fx < lax.axis_size("fx") - 1).astype(jnp.float32)
    inside_before = (fy > 0).astype(jnp.float32)
    inside_after = (fy < 2 * lax.axis_size("z") - 1).astype(jnp.float32)
    mix = [[mixing_ref[v, w] for w in range(NV)] for v in range(NV)]

    lane = lax.broadcasted_iota(jnp.int32, (1, LANES), 1)
    open_lane = (LANES - 1) * (1 - sec)
    keep_low = (lane != 0).astype(jnp.float32)
    keep_high = (lane != LANES - 1).astype(jnp.float32)
    at_open = (lane == open_lane).astype(jnp.float32)

    def along_z(cells, columns, v, xi):
        moved = pltpu.roll(columns, LANES - 1 - (8 * v + 2 * xi), axis=1)
        return (
            keep_low * pltpu.roll(cells, 1, axis=1)
            + keep_high * pltpu.roll(cells, LANES - 1, axis=1)
            + at_open * moved
        )

    def mixed(cells, v):
        total = mix[v][0] * cells[0]
        for w in range(1, NV):
            total = total + mix[v][w] * cells[w]
        return total

    packed[TOP:end, :] = beyond
    packed[TOP - 1 : TOP, :] = before[8 * NV : 8 * NV + 1, :]
    packed[end : end + 1, :] = after[8 * NV : 8 * NV + 1, :]
    group = lane // 8
    mixed_columns = jnp.zeros((size, LANES), jnp.float32)
    for shift in range(1 - NV, NV):
        factor = jnp.zeros((1, LANES), jnp.float32)
        for v in range(NV):
            if 0 <= v - shift < NV:
                factor = jnp.where(group == v, mix[v][v - shift], factor)
        source = beyond if shift == 0 else pltpu.roll(beyond, (8 * shift) % LANES, axis=1)
        mixed_columns = mixed_columns + factor * source
    column_rate = stencil(
        beyond,
        pltpu.roll(beyond, LANES - 2, axis=1),
        pltpu.roll(beyond, 2, axis=1),
        packed[TOP - 1 : end - 1, :]
        + packed[TOP + 1 : end + 1, :]
        + pltpu.roll(beyond + edge_ref[...], 1 + (LANES - 2) * (1 - sec), axis=1),
        mixed_columns,
    )
    column_section = beyond + TIME_STEP * column_rate

    row = lax.broadcasted_iota(jnp.int32, (8, LANES), 0)
    inside_rows = jnp.where(row < 4, inside_before, inside_after)
    row_cells = []
    row_others = []
    row_columns = jnp.where(
        row < 4, before[8 * NV : 8 * NV + 1, :], after[8 * NV : 8 * NV + 1, :]
    )
    for v in range(NV):
        cells = jnp.concatenate(
            [before[8 * v : 8 * v + 4, :], after[8 * v : 8 * v + 4, :]], axis=0
        )
        outer = jnp.concatenate(
            [before[8 * v + 4 : 8 * v + 8, :], after[8 * v + 4 : 8 * v + 8, :]], axis=0
        )
        inner = jnp.concatenate(
            [top[8 * v : 8 * v + 4, :], bottom[8 * v : 8 * v + 4, :]], axis=0
        )
        columns = jnp.zeros((8, LANES), jnp.float32)
        for xi in (1, 2):
            moved = pltpu.roll(row_columns, LANES - 1 - (8 * v + 2 * xi), axis=1)
            columns = jnp.where((row == xi) | (row == 4 + xi), moved, columns)
        across = (
            keep_low * pltpu.roll(cells, 1, axis=1)
            + keep_high * pltpu.roll(cells, LANES - 1, axis=1)
            + at_open * columns
        )
        row_cells.append(cells)
        row_others.append(outer + inner + across)
    for v in range(NV):
        cells = row_cells[v]
        rate = stencil(
            cells,
            pltpu.roll(cells, 7, axis=0),
            pltpu.roll(cells, 1, axis=0),
            row_others[v],
            mixed(row_cells, v),
        )
        later = inside_rows * (cells + TIME_STEP * rate)
        for xi in (1, 2):
            section[v, xi, TOP - 1 : TOP, :] = later[xi : xi + 1, :]
            section[v, xi, end : end + 1, :] = later[4 + xi : 5 + xi, :]

    for v in range(NV):
        for xi in range(4):
            field[v, xi, TOP:end, :] = slab(near_ref, state_ref, far_ref, v, xi)
            field[v, xi, TOP - 1 : TOP, :] = before[8 * v + xi : 8 * v + xi + 1, :]
            field[v, xi, end : end + 1, :] = after[8 * v + xi : 8 * v + xi + 1, :]

    def center(v, x):
        if x < 0 or x > 3:
            return slab(near_ref, state_ref, far_ref, v, x)
        return field[v, x, TOP:end, :]

    for xi in range(4):
        cells = [center(w, xi) for w in range(NV)]
        for v in range(NV):
            others = (
                field[v, xi, TOP - 1 : end - 1, :]
                + field[v, xi, TOP + 1 : end + 1, :]
                + along_z(cells[v], beyond, v, xi)
            )
            rate = stencil(
                cells[v], center(v, xi + 1), center(v, xi - 1), others, mixed(cells, v)
            )
            later = cells[v] + TIME_STEP * rate
            if xi == 0:
                later = inside_low * later
            if xi == 3:
                later = inside_high * later
            section[v, xi, TOP:end, :] = later
            if xi in (1, 2):
                out_ref[v, xi - 1] = cells[v] + 0.5 * TIME_STEP * rate

    for xi in (1, 2):
        cells = [section[w, xi, TOP:end, :] for w in range(NV)]
        for v in range(NV):
            others = (
                section[v, xi, TOP - 1 : end - 1, :]
                + section[v, xi, TOP + 1 : end + 1, :]
                + along_z(cells[v], column_section, v, xi)
            )
            rate = stencil(
                cells[v],
                section[v, xi + 1, TOP:end, :],
                section[v, xi - 1, TOP:end, :],
                others,
                mixed(cells, v),
            )
            final = out_ref[v, xi - 1] + 0.5 * TIME_STEP * rate
            out_ref[v, xi - 1] = final
            if v == 2:
                part_ref[xi - 1] = final[:8, :]


def shards(
    state, mixing, wall_weight, patch_map, block_map, shell_disp, shell_vel, connect, stiffness
):
    nfx, nfy, nsec = (lax.axis_size(axis) for axis in ("fx", FY, "sec"))
    near_x, far_x, near_y, far_y = (
        [pair for i in range(first, n - 1, 2) for pair in ((i, i + 1), (i + 1, i))]
        for n in (nfx, nfy)
        for first in (0, 1)
    )

    offered = offer(
        patch_map.reshape(2), block_map.reshape(2), wall_weight, state, nfx * nsec
    )
    offered = lax.all_to_all(offered, ("fx", "sec"), 0, 0, tiled=True)
    near = lax.ppermute(state, "fx", near_x)
    far = lax.ppermute(state, "fx", far_x)

    partial = kernel_call(collect_body, f32(nfy, NB // 2, LANES), [VM])(offered)
    loads = lax.all_to_all(partial, FY, 0, 0, tiled=True)

    block = f32(NB, LANES)
    couple, disp, vel, weight = kernel_call(
        couple_body,
        (f32(NB, NB, LANES), block, block, f32(*wall_weight.shape)),
        [VM] * 5,
    )(
        connect[0].T,
        stiffness[0],
        shell_disp.reshape(NB, LANES),
        shell_vel.reshape(NB, LANES),
        wall_weight,
    )
    span = f32(8 * NV + 8, LANES)
    to_near, to_far, beyond, wanted = kernel_call(
        second_round_body,
        (f32(8 * NV + 8 + 4 * nfx, LANES), span, f32(32, LANES), f32(4 * nfx, LANES)),
        [VM] * 4,
        cost=LONG,
    )(near, state, far, offered)
    from_near = lax.ppermute(to_near, FY, near_y)
    from_far = lax.ppermute(to_far, FY, far_y)

    own, walls = kernel_call(
        shell_body, (f32(NB, LANES), f32(2 * nfx, LANES)), [VM] * 6
    )(loads, wanted, from_near, couple, disp, vel)
    walls = lax.all_to_all(walls, ("fx", "core"), 0, 0, tiled=True)
    other = lax.ppermute(own, FY, near_y)

    fluid, part = kernel_call(
        fluid_body,
        (f32(*state.shape), f32(2, 8, LANES)),
        [SM] + [VM] * 8,
        scratch=[
            pltpu.VMEM((NV, 4, ROWS, LANES), jnp.float32),
            pltpu.VMEM((NV, 4, ROWS, LANES), jnp.float32),
            pltpu.VMEM((ROWS, LANES), jnp.float32),
            pltpu.VMEM((32, LANES), jnp.float32),
        ],
        cost=LONG,
    )(mixing, near, state, far, beyond, to_near, to_far, from_near, from_far)
    new_state, new_disp, new_vel = finish(walls, weight, part, own, other, fluid)
    return (new_state, new_disp.reshape(1, -1), new_vel.reshape(1, -1))


def solution(mesh):
    nfx, nfy, nsec = mesh.devices.shape
    mesh = jax.sharding.Mesh(
        mesh.devices.reshape(nfx, nfy // 2, 2, nsec), ("fx", "z", "core", "sec")
    )
    return jax.shard_map(
        shards,
        mesh=mesh,
        in_specs=(
            P(None, "fx", FY, "sec"),
            P(),
            P("fx", FY, "sec"),
            P("fx", FY, "sec", None),
            P("fx", FY, "sec", None),
            P("fx", None),
            P("fx", None),
            P("fx", None, None),
            P("fx", None, None),
        ),
        out_specs=(P(None, "fx", FY, "sec"), P("fx", None), P("fx", None)),
        check_vma=False,
    )
```

```python
import jax
import jax.numpy as jnp
from jax import lax
from jax.experimental import pallas as pl
from jax.experimental.pallas import tpu as pltpu
from jax.sharding import PartitionSpec as P

NV = 5
NB = 32
SUBCYCLES = 4
LANES = 128
HALF = 64
FY = ("z", "core")

DIFFUSION = 0.25
TRANSPORT = 0.5
TIME_STEP = 0.2
SHELL_STEP = 0.25
DAMPING = 0.1

TOP = 8
ROWS = 48

LONG = 3_800_000_000

VM = pl.BlockSpec(memory_space=pltpu.VMEM)
SM = pl.BlockSpec(memory_space=pltpu.SMEM)
ANY = pl.BlockSpec(memory_space=pl.ANY)
HBM = pl.BlockSpec(memory_space=pltpu.HBM)
SMALL = pltpu.CompilerParams(vmem_limit_bytes=8 * 1024 * 1024)


def kernel_call(body, outs, ins, scratch=(), cost=20000, params=SMALL):
    return pl.pallas_call(
        body,
        out_shape=outs,
        in_specs=ins,
        out_specs=jax.tree.map(lambda _: VM, outs),
        scratch_shapes=scratch,
        compiler_params=params,
        cost_estimate=pl.CostEstimate(flops=cost, bytes_accessed=cost, transcendentals=0),
    )


def f32(*shape):
    return jax.ShapeDtypeStruct(shape, jnp.float32)


def terms(x):
    found = []
    for _ in range(3):
        term = x.astype(jnp.bfloat16)
        x = x - term.astype(jnp.float32)
        found.append(term)
    return found


def product(select, x, axis=0):
    select = select.astype(jnp.bfloat16)
    total = None
    for term in terms(x):
        part = lax.dot_general(
            select, term, (((1,), (axis,)), ((), ())), preferred_element_type=jnp.float32
        )
        total = part if total is None else total + part
    return total


def offer_body(
    patch_hbm,
    block_hbm,
    weight_hbm,
    state_hbm,
    out_ref,
    patch_ref,
    block_ref,
    weight_ref,
    state_ref,
    arrived,
):
    copies = [
        pltpu.make_async_copy(source, target, arrived.at[place])
        for place, (source, target) in enumerate(
            (
                (state_hbm, state_ref),
                (patch_hbm, patch_ref),
                (block_hbm, block_ref),
                (weight_hbm, weight_ref),
            )
        )
    ]
    for copy in copies:
        copy.start()
    for copy in copies:
        copy.wait()
    sec = lax.axis_index("sec")
    column = lax.broadcasted_iota(jnp.int32, (8, LANES), 0)
    lane = lax.broadcasted_iota(jnp.int32, (8, LANES), 1)
    wanted = (lane == column + (LANES - 2) * (1 - sec)).astype(jnp.float32)
    columns = product(wanted, state_ref[...].reshape(-1, LANES), axis=1)
    rows = [weight_ref[tile] * state_ref[NV - 1, tile, 0:1, :] for tile in range(2)]
    for tile in range(2):
        target = patch_ref[tile] * NB + block_ref[tile]
        target = jnp.full((1, LANES // 2), target.astype(jnp.float32))
        values = columns[tile : tile + 1, :]
        rows += [values[:, :LANES], values[:, LANES : 2 * LANES]]
        rows.append(jnp.concatenate([values[:, 2 * LANES :], target], axis=1))
    rows = jnp.concatenate(rows, axis=0)
    for receiver in range(out_ref.shape[0]):
        out_ref[receiver] = rows


def offer(patch_map, block_map, weight, state, receivers):
    return kernel_call(
        offer_body,
        f32(receivers, 8, LANES),
        [HBM] * 4,
        scratch=[
            pltpu.SMEM((2,), jnp.int32),
            pltpu.SMEM((2,), jnp.int32),
            pltpu.VMEM(weight.shape, jnp.float32),
            pltpu.VMEM(state.shape, jnp.float32),
            pltpu.SemaphoreType.DMA((4,)),
        ],
        params=None,
    )(patch_map, block_map, weight, state)


def targets_of(rows):
    lane = lax.broadcasted_iota(jnp.int32, (8, LANES), 1)
    return jnp.where(lane < LANES // 2, pltpu.roll(rows, LANES // 2, axis=1), rows)


def halved(x, core):
    keep = jnp.where(core == 0, x[: NB // 2], x[NB // 2 :])
    move = jnp.where(core == 0, x[NB // 2 :], x[: NB // 2])
    lane = lax.broadcasted_iota(jnp.int32, keep.shape, 1)
    return jnp.where((lane < HALF) == (core == 0), keep, pltpu.roll(move, HALF, axis=1))


def doubled(rows):
    lane = lax.broadcasted_iota(jnp.int32, rows.shape, 1)
    moved = pltpu.roll(rows, HALF, axis=1)
    return jnp.where(lane < HALF, rows, moved), jnp.where(lane < HALF, moved, rows)


def joined(first, second):
    lane = lax.broadcasted_iota(jnp.int32, first.shape, 1)
    low = jnp.where(lane < HALF, first, pltpu.roll(second, HALF, axis=1))
    high = jnp.where(lane < HALF, pltpu.roll(first, HALF, axis=1), second)
    return low, high


def collect_body(offered_ref, out_ref):
    base = (lax.axis_index("fx") * NB).astype(jnp.float32)
    block = lax.broadcasted_iota(jnp.int32, (NB, LANES), 0).astype(jnp.float32) + base
    sums = [jnp.zeros((NB, LANES), jnp.float32) for _ in range(4)]
    for sender in range(offered_ref.shape[0]):
        rows = offered_ref[sender]
        targets = targets_of(rows)
        for tile in range(2):
            load = rows[tile : tile + 1, :]
            target = targets[4 + 3 * tile : 5 + 3 * tile, :]
            slot = (2 * sender + tile) % 4
            sums[slot] = sums[slot] + jnp.where(block == target, load, 0.0)
    total = (sums[0] + sums[1]) + (sums[2] + sums[3])
    halves = [halved(total, core) for core in range(2)]
    for receiver in range(out_ref.shape[0]):
        out_ref[receiver] = halves[receiver // (out_ref.shape[0] // 2)]


def couple_body(
    connect_ref, stiff_ref, disp_ref, vel_ref, weight_ref, out_ref, disp_out, vel_out, weight_out
):
    core = lax.axis_index("core")
    elements = stiff_ref.shape[0]
    block = lax.broadcasted_iota(jnp.int32, (NB, elements), 0)
    first = connect_ref[0:1, :]
    second = connect_ref[1:2, :]
    ends = (block == first).astype(jnp.float32) - (block == second).astype(jnp.float32)
    pairs = [(ends * ends[a : a + 1, :]).astype(jnp.bfloat16) for a in range(NB)]
    pairs = jnp.concatenate(pairs, axis=0)
    low, high = doubled(stiff_ref[...])
    out_ref[...] = product(pairs, jnp.where(core == 0, low, high)).reshape(NB, NB, LANES)
    for source, out in ((disp_ref, disp_out), (vel_ref, vel_out)):
        low, high = doubled(source[...])
        out[...] = jnp.where(core == 0, low, high)
    weight_out[...] = weight_ref[...]


def shell_body(
    loads_ref, wanted_ref, from_near_ref, couple_ref, disp_ref, vel_ref, last_out, wall_out
):
    disp = disp_ref[...]
    vel = vel_ref[...]
    parts = [loads_ref[sender] for sender in range(loads_ref.shape[0])]
    while len(parts) > 1:
        parts = [sum(parts[i + 1 : i + 2], parts[i]) for i in range(0, len(parts), 2)]
    load = jnp.concatenate(doubled(parts[0]), axis=0)
    total = jnp.zeros_like(disp)
    for _ in range(SUBCYCLES):
        inner = [jnp.zeros_like(disp) for _ in range(4)]
        for a in range(NB):
            inner[a % 4] = inner[a % 4] + couple_ref[a] * disp[a : a + 1, :]
        inner = (inner[0] + inner[1]) + (inner[2] + inner[3])
        vel = vel + SHELL_STEP * (load - inner - DAMPING * vel)
        disp = disp + SHELL_STEP * vel
        total = total + disp
    slots = wall_out.shape[0]
    wanted = wanted_ref[...] + from_near_ref[8 * NV + 8 :, :]
    found = jnp.dot(
        wanted[:, : 3 * NB].astype(jnp.bfloat16),
        jnp.concatenate(terms(total * (1.0 / SUBCYCLES)), axis=0),
        preferred_element_type=jnp.float32,
    )
    lane = lax.broadcasted_iota(jnp.int32, (slots, LANES), 1)
    wall_out[...] = jnp.where(lane < HALF, found[:slots], found[slots:])
    lane = lax.broadcasted_iota(jnp.int32, (NB // 2, LANES), 1)
    last_out[: NB // 2, :] = jnp.where(lane < HALF, disp[: NB // 2], disp[NB // 2 :])
    last_out[NB // 2 :, :] = jnp.where(lane < HALF, vel[: NB // 2], vel[NB // 2 :])


def finish_body(
    walls_ref, weight_ref, part_ref, own_ref, other_ref, _, out_ref, disp_out, vel_out
):
    wall = walls_ref[0:8, :]
    for first in range(8, walls_ref.shape[0], 8):
        wall = wall + walls_ref[first : first + 8, :]
    wall = wall + pltpu.roll(wall, 4, axis=0)
    wall = wall + pltpu.roll(wall, 2, axis=0)
    walls = joined(wall[0:1, :], wall[1:2, :])
    row = lax.broadcasted_iota(jnp.int32, (8, LANES), 0)
    for tile in range(2):
        gain = weight_ref[tile] * walls[tile]
        out_ref[0, tile] = part_ref[tile] + jnp.where(row == 0, gain, 0.0)
    core = lax.axis_index("core")
    first = jnp.where(core == 0, own_ref[...], other_ref[...])
    second = jnp.where(core == 0, other_ref[...], own_ref[...])
    for rows, out in ((slice(0, NB // 2), disp_out), (slice(NB // 2, NB), vel_out)):
        low, high = joined(first[rows], second[rows])
        out[: NB // 2, :] = low
        out[NB // 2 :, :] = high


def finish(walls, weight, part, own, other, state):
    block = pl.BlockSpec((NB, LANES), lambda i: (0, 0))
    return pl.pallas_call(
        finish_body,
        grid=(1,),
        out_shape=(f32(*state.shape), f32(NB, LANES), f32(NB, LANES)),
        in_specs=[VM] * 5 + [ANY],
        out_specs=(pl.BlockSpec((1, 2, 8, LANES), lambda i: (2, 0, 0, 0)), block, block),
        input_output_aliases={5: 0},
        compiler_params=SMALL,
        cost_estimate=pl.CostEstimate(flops=4096, bytes_accessed=65536, transcendentals=0),
    )(walls, weight, part, own, other, state)


def sides(axis, near, far):
    even = lax.rem(lax.axis_index("core" if axis == "fy" else axis), 2) == 0
    return jnp.where(even, far, near), jnp.where(even, near, far)


def slab(near_ref, state_ref, far_ref, v, xi, rows=slice(None)):
    if xi < 1:
        return sides("fx", near_ref[v, 1 + xi, rows, :], far_ref[v, 1 + xi, rows, :])[0]
    if xi > 2:
        return sides("fx", near_ref[v, xi - 3, rows, :], far_ref[v, xi - 3, rows, :])[1]
    return state_ref[v, xi - 1, rows, :]


def pack_columns(slabs, out_ref):
    lane = lax.broadcasted_iota(jnp.int32, (32, LANES), 1)

    def pack(shift):
        packed = jnp.zeros((32, LANES), jnp.float32)
        for (v, xi), cells_ref in slabs.items():
            first = 8 * v + 2 * xi
            cells = cells_ref[...]
            moved = pltpu.roll(cells, first + shift, axis=1) if first + shift else cells
            packed = jnp.where((lane == first) | (lane == first + 1), moved, packed)
        out_ref[...] = packed

    sec = lax.axis_index("sec")
    pl.when(sec == 0)(lambda: pack(2))
    pl.when(sec == 1)(lambda: pack(0))


def unpack_columns(offered_ref):
    sec = lax.axis_index("sec")
    fx = lax.axis_index("fx")
    last = lax.axis_size("fx") - 1
    rows = [
        offered_ref[2 * jnp.maximum(fx - 1, 0) + 1 - sec] * (fx > 0).astype(jnp.float32),
        offered_ref[2 * fx + 1 - sec],
        offered_ref[2 * jnp.minimum(fx + 1, last) + 1 - sec] * (fx < last).astype(jnp.float32),
        jnp.zeros((8, LANES), jnp.float32),
    ]
    rows = jnp.concatenate(rows, axis=0)

    def place(shape):
        l = lax.broadcasted_iota(jnp.int32, shape, 0)
        xi = (l & 7) >> 1
        neighbour = jnp.where(xi == 0, 0, jnp.where(xi == 3, 2, 1))
        return neighbour, l & 1, 2 * (l >> 3) + 1 - (xi & 1)

    neighbour, column, source = place((LANES, 32))
    row = 8 * neighbour + 2 + 3 * column + (source >> 2)
    here = lax.broadcasted_iota(jnp.int32, (LANES, 32), 1) == row
    here &= lax.broadcasted_iota(jnp.int32, (LANES, 32), 0) < 8 * NV
    lines = product(here.astype(jnp.float32), rows)
    _, _, source = place((LANES, LANES))
    position = lax.broadcasted_iota(jnp.int32, (LANES, LANES), 1)
    lines = jnp.where((position >> 5) == (source & 3), lines, 0.0)
    position = lax.broadcasted_iota(jnp.int32, (32, LANES), 1)
    y = lax.broadcasted_iota(jnp.int32, (32, LANES), 0)
    return product(((position & 31) == y).astype(jnp.float32), lines, axis=1)


def wanted_blocks(offered_ref, peers):
    base = (lax.axis_index("fx") * NB).astype(jnp.float32)
    sec = lax.axis_index("sec")
    targets = [targets_of(offered_ref[2 * peer + sec]) for peer in range(peers)]
    rows = [found[row : row + 1, :] for row in (4, 7) for found in targets for _ in range(2)]
    rows = jnp.concatenate(rows, axis=0)
    lane = lax.broadcasted_iota(jnp.int32, rows.shape, 1)
    here = (lax.broadcasted_iota(jnp.int32, rows.shape, 0) & 1) == lax.axis_index("core")
    asked = (lane & (NB - 1)).astype(jnp.float32) + base == rows
    return (asked & here & (lane < 3 * NB)).astype(jnp.float32)


def second_round_body(
    near_ref, state_ref, far_ref, offered_ref, to_near_ref, to_far_ref, beyond_ref, wanted_ref
):
    beyond_ref[...] = unpack_columns(offered_ref)
    wanted = wanted_blocks(offered_ref, wanted_ref.shape[0] // 4)
    wanted_ref[...] = wanted
    to_near_ref[8 * NV + 8 :, :] = wanted
    last = state_ref.shape[2] - 1

    def put(spot, low, high):
        to_far, to_near = sides("fy", high, low)
        to_near_ref[spot : spot + 1, :] = to_near
        to_far_ref[spot : spot + 1, :] = to_far

    for place in range(2):
        low = slice(place, place + 1)
        high = slice(last - place, last - place + 1)
        for v in range(NV):
            for xi in range(4):
                put(
                    8 * v + 4 * place + xi,
                    slab(near_ref, state_ref, far_ref, v, xi, low),
                    slab(near_ref, state_ref, far_ref, v, xi, high),
                )
        put(8 * NV + place, beyond_ref[low, :], beyond_ref[high, :])
    for out in (to_near_ref, to_far_ref):
        out[8 * NV + 2 : 8 * NV + 8, :] = jnp.zeros((6, LANES), jnp.float32)


def stencil(center, ahead, behind, others, mixed):
    beside = ahead + behind + others
    return DIFFUSION * (beside - 6.0 * center) - TRANSPORT * 0.5 * (ahead - behind) + mixed


def fluid_body(
    mixing_ref,
    near_ref,
    state_ref,
    far_ref,
    beyond_ref,
    to_near_ref,
    to_far_ref,
    from_near_ref,
    from_far_ref,
    out_ref,
    part_ref,
    field,
    section,
    packed,
    edge_ref,
):
    rows = 8 * NV + 8
    top, bottom = sides("fy", to_near_ref[:rows, :], to_far_ref[...])
    before, after = sides("fy", from_near_ref[:rows, :], from_far_ref[...])
    beyond = beyond_ref[...]
    pack_columns({(v, xi): state_ref.at[v, xi - 1] for v in range(NV) for xi in (1, 2)}, edge_ref)
    size = state_ref.shape[2]
    end = TOP + size
    sec = lax.axis_index("sec")
    fx = lax.axis_index("fx")
    fy = 2 * lax.axis_index("z") + lax.axis_index("core")
    inside_low = (fx > 0).astype(jnp.float32)
    inside_high = (fx < lax.axis_size("fx") - 1).astype(jnp.float32)
    inside_before = (fy > 0).astype(jnp.float32)
    inside_after = (fy < 2 * lax.axis_size("z") - 1).astype(jnp.float32)
    mix = [[mixing_ref[v, w] for w in range(NV)] for v in range(NV)]

    lane = lax.broadcasted_iota(jnp.int32, (1, LANES), 1)
    open_lane = (LANES - 1) * (1 - sec)
    keep_low = (lane != 0).astype(jnp.float32)
    keep_high = (lane != LANES - 1).astype(jnp.float32)
    at_open = (lane == open_lane).astype(jnp.float32)

    def along_z(cells, columns, v, xi):
        moved = pltpu.roll(columns, LANES - 1 - (8 * v + 2 * xi), axis=1)
        return (
            keep_low * pltpu.roll(cells, 1, axis=1)
            + keep_high * pltpu.roll(cells, LANES - 1, axis=1)
            + at_open * moved
        )

    def mixed(cells, v):
        total = mix[v][0] * cells[0]
        for w in range(1, NV):
            total = total + mix[v][w] * cells[w]
        return total

    packed[TOP:end, :] = beyond
    packed[TOP - 1 : TOP, :] = before[8 * NV : 8 * NV + 1, :]
    packed[end : end + 1, :] = after[8 * NV : 8 * NV + 1, :]
    group = lane // 8
    mixed_columns = jnp.zeros((size, LANES), jnp.float32)
    for shift in range(1 - NV, NV):
        factor = jnp.zeros((1, LANES), jnp.float32)
        for v in range(NV):
            if 0 <= v - shift < NV:
                factor = jnp.where(group == v, mix[v][v - shift], factor)
        source = beyond if shift == 0 else pltpu.roll(beyond, (8 * shift) % LANES, axis=1)
        mixed_columns = mixed_columns + factor * source
    column_rate = stencil(
        beyond,
        pltpu.roll(beyond, LANES - 2, axis=1),
        pltpu.roll(beyond, 2, axis=1),
        packed[TOP - 1 : end - 1, :]
        + packed[TOP + 1 : end + 1, :]
        + pltpu.roll(beyond + edge_ref[...], 1 + (LANES - 2) * (1 - sec), axis=1),
        mixed_columns,
    )
    column_section = beyond + TIME_STEP * column_rate

    row = lax.broadcasted_iota(jnp.int32, (8, LANES), 0)
    inside_rows = jnp.where(row < 4, inside_before, inside_after)
    row_cells = []
    row_others = []
    row_columns = jnp.where(
        row < 4, before[8 * NV : 8 * NV + 1, :], after[8 * NV : 8 * NV + 1, :]
    )
    for v in range(NV):
        cells = jnp.concatenate(
            [before[8 * v : 8 * v + 4, :], after[8 * v : 8 * v + 4, :]], axis=0
        )
        outer = jnp.concatenate(
            [before[8 * v + 4 : 8 * v + 8, :], after[8 * v + 4 : 8 * v + 8, :]], axis=0
        )
        inner = jnp.concatenate(
            [top[8 * v : 8 * v + 4, :], bottom[8 * v : 8 * v + 4, :]], axis=0
        )
        columns = jnp.zeros((8, LANES), jnp.float32)
        for xi in (1, 2):
            moved = pltpu.roll(row_columns, LANES - 1 - (8 * v + 2 * xi), axis=1)
            columns = jnp.where((row == xi) | (row == 4 + xi), moved, columns)
        across = (
            keep_low * pltpu.roll(cells, 1, axis=1)
            + keep_high * pltpu.roll(cells, LANES - 1, axis=1)
            + at_open * columns
        )
        row_cells.append(cells)
        row_others.append(outer + inner + across)
    for v in range(NV):
        cells = row_cells[v]
        rate = stencil(
            cells,
            pltpu.roll(cells, 7, axis=0),
            pltpu.roll(cells, 1, axis=0),
            row_others[v],
            mixed(row_cells, v),
        )
        later = inside_rows * (cells + TIME_STEP * rate)
        for xi in (1, 2):
            section[v, xi, TOP - 1 : TOP, :] = later[xi : xi + 1, :]
            section[v, xi, end : end + 1, :] = later[4 + xi : 5 + xi, :]

    for v in range(NV):
        for xi in range(4):
            field[v, xi, TOP:end, :] = slab(near_ref, state_ref, far_ref, v, xi)
            field[v, xi, TOP - 1 : TOP, :] = before[8 * v + xi : 8 * v + xi + 1, :]
            field[v, xi, end : end + 1, :] = after[8 * v + xi : 8 * v + xi + 1, :]

    def center(v, x):
        if x < 0 or x > 3:
            return slab(near_ref, state_ref, far_ref, v, x)
        return field[v, x, TOP:end, :]

    for xi in range(4):
        cells = [center(w, xi) for w in range(NV)]
        for v in range(NV):
            others = (
                field[v, xi, TOP - 1 : end - 1, :]
                + field[v, xi, TOP + 1 : end + 1, :]
                + along_z(cells[v], beyond, v, xi)
            )
            rate = stencil(
                cells[v], center(v, xi + 1), center(v, xi - 1), others, mixed(cells, v)
            )
            later = cells[v] + TIME_STEP * rate
            if xi == 0:
                later = inside_low * later
            if xi == 3:
                later = inside_high * later
            section[v, xi, TOP:end, :] = later
            if xi in (1, 2):
                out_ref[v, xi - 1] = cells[v] + 0.5 * TIME_STEP * rate

    for xi in (1, 2):
        cells = [section[w, xi, TOP:end, :] for w in range(NV)]
        for v in range(NV):
            others = (
                section[v, xi, TOP - 1 : end - 1, :]
                + section[v, xi, TOP + 1 : end + 1, :]
                + along_z(cells[v], column_section, v, xi)
            )
            rate = stencil(
                cells[v],
                section[v, xi + 1, TOP:end, :],
                section[v, xi - 1, TOP:end, :],
                others,
                mixed(cells, v),
            )
            final = out_ref[v, xi - 1] + 0.5 * TIME_STEP * rate
            out_ref[v, xi - 1] = final
            if v == 2:
                part_ref[xi - 1] = final[:8, :]


def shards(
    state, mixing, wall_weight, patch_map, block_map, shell_disp, shell_vel, connect, stiffness
):
    nfx, nfy, nsec = (lax.axis_size(axis) for axis in ("fx", FY, "sec"))
    near_x, far_x, near_y, far_y = (
        [pair for i in range(first, n - 1, 2) for pair in ((i, i + 1), (i + 1, i))]
        for n in (nfx, nfy)
        for first in (0, 1)
    )

    offered = offer(
        patch_map.reshape(2), block_map.reshape(2), wall_weight, state, nfx * nsec
    )
    offered = lax.all_to_all(offered, ("fx", "sec"), 0, 0, tiled=True)
    near = lax.ppermute(state, "fx", near_x)
    far = lax.ppermute(state, "fx", far_x)

    partial = kernel_call(collect_body, f32(nfy, NB // 2, LANES), [VM])(offered)
    loads = lax.all_to_all(partial, ("core", "z"), 0, 0, tiled=True)

    block = f32(NB, LANES)
    couple, disp, vel, weight = kernel_call(
        couple_body,
        (f32(NB, NB, LANES), block, block, f32(*wall_weight.shape)),
        [VM] * 5,
    )(
        connect[0].T,
        stiffness[0],
        shell_disp.reshape(NB, LANES),
        shell_vel.reshape(NB, LANES),
        wall_weight,
    )
    span = f32(8 * NV + 8, LANES)
    to_near, to_far, beyond, wanted = kernel_call(
        second_round_body,
        (f32(8 * NV + 8 + 4 * nfx, LANES), span, f32(32, LANES), f32(4 * nfx, LANES)),
        [VM] * 4,
        cost=LONG,
    )(near, state, far, offered)
    from_near = lax.ppermute(to_near, FY, near_y)
    from_far = lax.ppermute(to_far, FY, far_y)

    own, walls = kernel_call(
        shell_body, (f32(NB, LANES), f32(2 * nfx, LANES)), [VM] * 6
    )(loads, wanted, from_near, couple, disp, vel)
    walls = lax.all_to_all(walls, ("fx", "core"), 0, 0, tiled=True)
    other = lax.ppermute(own, FY, near_y)

    fluid, part = kernel_call(
        fluid_body,
        (f32(*state.shape), f32(2, 8, LANES)),
        [SM] + [VM] * 8,
        scratch=[
            pltpu.VMEM((NV, 4, ROWS, LANES), jnp.float32),
            pltpu.VMEM((NV, 4, ROWS, LANES), jnp.float32),
            pltpu.VMEM((ROWS, LANES), jnp.float32),
            pltpu.VMEM((32, LANES), jnp.float32),
        ],
        cost=LONG,
    )(mixing, near, state, far, beyond, to_near, to_far, from_near, from_far)
    new_state, new_disp, new_vel = finish(walls, weight, part, own, other, fluid)
    return (new_state, new_disp.reshape(1, -1), new_vel.reshape(1, -1))


def solution(mesh):
    nfx, nfy, nsec = mesh.devices.shape
    mesh = jax.sharding.Mesh(
        mesh.devices.reshape(nfx, nfy // 2, 2, nsec), ("fx", "z", "core", "sec")
    )
    return jax.shard_map(
        shards,
        mesh=mesh,
        in_specs=(
            P(None, "fx", FY, "sec"),
            P(),
            P("fx", FY, "sec"),
            P("fx", FY, "sec", None),
            P("fx", FY, "sec", None),
            P("fx", None),
            P("fx", None),
            P("fx", None, None),
            P("fx", None, None),
        ),
        out_specs=(P(None, "fx", FY, "sec"), P("fx", None), P("fx", None)),
        check_vma=False,
    )
```

```python
import jax
import jax.numpy as jnp
from jax import lax
from jax.experimental import pallas as pl
from jax.experimental.pallas import tpu as pltpu
from jax.sharding import PartitionSpec as P

NV = 5
NB = 32
SUBCYCLES = 4
LANES = 128
HALF = 64
FY = ("z", "core")

DIFFUSION = 0.25
TRANSPORT = 0.5
TIME_STEP = 0.2
SHELL_STEP = 0.25
DAMPING = 0.1

TOP = 8
ROWS = 48

LONG = 3_800_000_000

VM = pl.BlockSpec(memory_space=pltpu.VMEM)
SM = pl.BlockSpec(memory_space=pltpu.SMEM)
ANY = pl.BlockSpec(memory_space=pl.ANY)
HBM = pl.BlockSpec(memory_space=pltpu.HBM)
SMALL = pltpu.CompilerParams(vmem_limit_bytes=8 * 1024 * 1024)


def kernel_call(body, outs, ins, scratch=(), cost=20000, params=SMALL):
    return pl.pallas_call(
        body,
        out_shape=outs,
        in_specs=ins,
        out_specs=jax.tree.map(lambda _: VM, outs),
        scratch_shapes=scratch,
        compiler_params=params,
        cost_estimate=pl.CostEstimate(flops=cost, bytes_accessed=cost, transcendentals=0),
    )


def f32(*shape):
    return jax.ShapeDtypeStruct(shape, jnp.float32)


def terms(x):
    found = []
    for _ in range(3):
        term = x.astype(jnp.bfloat16)
        x = x - term.astype(jnp.float32)
        found.append(term)
    return found


def product(select, x, axis=0):
    select = select.astype(jnp.bfloat16)
    total = None
    for term in terms(x):
        part = lax.dot_general(
            select, term, (((1,), (axis,)), ((), ())), preferred_element_type=jnp.float32
        )
        total = part if total is None else total + part
    return total


def offer_body(
    patch_hbm,
    block_hbm,
    weight_hbm,
    state_hbm,
    out_ref,
    patch_ref,
    block_ref,
    weight_ref,
    state_ref,
    arrived,
):
    copies = [
        pltpu.make_async_copy(source, target, arrived.at[place])
        for place, (source, target) in enumerate(
            (
                (state_hbm, state_ref),
                (patch_hbm, patch_ref),
                (block_hbm, block_ref),
                (weight_hbm, weight_ref),
            )
        )
    ]
    for copy in copies:
        copy.start()
    for copy in copies:
        copy.wait()
    sec = lax.axis_index("sec")
    column = lax.broadcasted_iota(jnp.int32, (8, LANES), 0)
    lane = lax.broadcasted_iota(jnp.int32, (8, LANES), 1)
    wanted = (lane == column + (LANES - 2) * (1 - sec)).astype(jnp.float32)
    columns = product(wanted, state_ref[...].reshape(-1, LANES), axis=1)
    rows = [weight_ref[tile] * state_ref[NV - 1, tile, 0:1, :] for tile in range(2)]
    for tile in range(2):
        target = patch_ref[tile] * NB + block_ref[tile]
        target = jnp.full((1, LANES // 2), target.astype(jnp.float32))
        values = columns[tile : tile + 1, :]
        rows += [values[:, :LANES], values[:, LANES : 2 * LANES]]
        rows.append(jnp.concatenate([values[:, 2 * LANES :], target], axis=1))
    rows = jnp.concatenate(rows, axis=0)
    for receiver in range(out_ref.shape[0]):
        out_ref[receiver] = rows


def offer(patch_map, block_map, weight, state, receivers):
    return kernel_call(
        offer_body,
        f32(receivers, 8, LANES),
        [HBM] * 4,
        scratch=[
            pltpu.SMEM((2,), jnp.int32),
            pltpu.SMEM((2,), jnp.int32),
            pltpu.VMEM(weight.shape, jnp.float32),
            pltpu.VMEM(state.shape, jnp.float32),
            pltpu.SemaphoreType.DMA((4,)),
        ],
        params=None,
    )(patch_map, block_map, weight, state)


def targets_of(rows):
    lane = lax.broadcasted_iota(jnp.int32, (8, LANES), 1)
    return jnp.where(lane < LANES // 2, pltpu.roll(rows, LANES // 2, axis=1), rows)


def halved(x, core):
    keep = jnp.where(core == 0, x[: NB // 2], x[NB // 2 :])
    move = jnp.where(core == 0, x[NB // 2 :], x[: NB // 2])
    lane = lax.broadcasted_iota(jnp.int32, keep.shape, 1)
    return jnp.where((lane < HALF) == (core == 0), keep, pltpu.roll(move, HALF, axis=1))


def doubled(rows):
    lane = lax.broadcasted_iota(jnp.int32, rows.shape, 1)
    moved = pltpu.roll(rows, HALF, axis=1)
    return jnp.where(lane < HALF, rows, moved), jnp.where(lane < HALF, moved, rows)


def joined(first, second):
    lane = lax.broadcasted_iota(jnp.int32, first.shape, 1)
    low = jnp.where(lane < HALF, first, pltpu.roll(second, HALF, axis=1))
    high = jnp.where(lane < HALF, pltpu.roll(first, HALF, axis=1), second)
    return low, high


def collect_body(offered_ref, out_ref):
    base = (lax.axis_index("fx") * NB).astype(jnp.float32)
    block = lax.broadcasted_iota(jnp.int32, (NB, LANES), 0).astype(jnp.float32) + base
    sums = [jnp.zeros((NB, LANES), jnp.float32) for _ in range(4)]
    for sender in range(offered_ref.shape[0]):
        rows = offered_ref[sender]
        targets = targets_of(rows)
        for tile in range(2):
            load = rows[tile : tile + 1, :]
            target = targets[4 + 3 * tile : 5 + 3 * tile, :]
            slot = (2 * sender + tile) % 4
            sums[slot] = sums[slot] + jnp.where(block == target, load, 0.0)
    total = (sums[0] + sums[1]) + (sums[2] + sums[3])
    halves = [halved(total, core) for core in range(2)]
    for receiver in range(out_ref.shape[0]):
        out_ref[receiver] = halves[receiver // (out_ref.shape[0] // 2)]


def couple_body(
    connect_ref, stiff_ref, disp_ref, vel_ref, weight_ref, out_ref, disp_out, vel_out, weight_out
):
    core = lax.axis_index("core")
    elements = stiff_ref.shape[0]
    block = lax.broadcasted_iota(jnp.int32, (NB, elements), 0)
    first = connect_ref[0:1, :]
    second = connect_ref[1:2, :]
    ends = (block == first).astype(jnp.float32) - (block == second).astype(jnp.float32)
    pairs = [(ends * ends[a : a + 1, :]).astype(jnp.bfloat16) for a in range(NB)]
    pairs = jnp.concatenate(pairs, axis=0)
    low, high = doubled(stiff_ref[...])
    out_ref[...] = product(pairs, jnp.where(core == 0, low, high)).reshape(NB, NB, LANES)
    for source, out in ((disp_ref, disp_out), (vel_ref, vel_out)):
        low, high = doubled(source[...])
        out[...] = jnp.where(core == 0, low, high)
    weight_out[...] = weight_ref[...]


def shell_body(
    loads_ref, wanted_ref, from_near_ref, couple_ref, disp_ref, vel_ref, last_out, wall_out
):
    disp = disp_ref[...]
    vel = vel_ref[...]
    parts = [loads_ref[sender] for sender in range(loads_ref.shape[0])]
    while len(parts) > 1:
        parts = [sum(parts[i + 1 : i + 2], parts[i]) for i in range(0, len(parts), 2)]
    load = jnp.concatenate(doubled(parts[0]), axis=0)
    total = jnp.zeros_like(disp)
    for _ in range(SUBCYCLES):
        inner = [jnp.zeros_like(disp) for _ in range(4)]
        for a in range(NB):
            inner[a % 4] = inner[a % 4] + couple_ref[a] * disp[a : a + 1, :]
        inner = (inner[0] + inner[1]) + (inner[2] + inner[3])
        vel = vel + SHELL_STEP * (load - inner - DAMPING * vel)
        disp = disp + SHELL_STEP * vel
        total = total + disp
    slots = wall_out.shape[0]
    wanted = wanted_ref[...] + from_near_ref[8 * NV + 8 :, :]
    found = jnp.dot(
        wanted[:, : 3 * NB].astype(jnp.bfloat16),
        jnp.concatenate(terms(total * (1.0 / SUBCYCLES)), axis=0),
        preferred_element_type=jnp.float32,
    )
    lane = lax.broadcasted_iota(jnp.int32, (slots, LANES), 1)
    wall_out[...] = jnp.where(lane < HALF, found[:slots], found[slots:])
    lane = lax.broadcasted_iota(jnp.int32, (NB // 2, LANES), 1)
    last_out[: NB // 2, :] = jnp.where(lane < HALF, disp[: NB // 2], disp[NB // 2 :])
    last_out[NB // 2 :, :] = jnp.where(lane < HALF, vel[: NB // 2], vel[NB // 2 :])


def finish_body(
    walls_ref, weight_ref, part_ref, _, out_ref
):
    wall = walls_ref[0:8, :]
    for first in range(8, walls_ref.shape[0], 8):
        wall = wall + walls_ref[first : first + 8, :]
    wall = wall + pltpu.roll(wall, 4, axis=0)
    wall = wall + pltpu.roll(wall, 2, axis=0)
    walls = joined(wall[0:1, :], wall[1:2, :])
    row = lax.broadcasted_iota(jnp.int32, (8, LANES), 0)
    for tile in range(2):
        gain = weight_ref[tile] * walls[tile]
        out_ref[0, tile] = part_ref[tile] + jnp.where(row == 0, gain, 0.0)


def finish(walls, weight, part, state):
    return pl.pallas_call(
        finish_body,
        grid=(1,),
        out_shape=f32(*state.shape),
        in_specs=[VM] * 3 + [ANY],
        out_specs=pl.BlockSpec((1, 2, 8, LANES), lambda i: (2, 0, 0, 0)),
        input_output_aliases={3: 0},
        compiler_params=SMALL,
        cost_estimate=pl.CostEstimate(flops=4096, bytes_accessed=65536, transcendentals=0),
    )(walls, weight, part, state)


def sides(axis, near, far):
    even = lax.rem(lax.axis_index("core" if axis == "fy" else axis), 2) == 0
    return jnp.where(even, far, near), jnp.where(even, near, far)


def slab(near_ref, state_ref, far_ref, v, xi, rows=slice(None)):
    if xi < 1:
        return sides("fx", near_ref[v, 1 + xi, rows, :], far_ref[v, 1 + xi, rows, :])[0]
    if xi > 2:
        return sides("fx", near_ref[v, xi - 3, rows, :], far_ref[v, xi - 3, rows, :])[1]
    return state_ref[v, xi - 1, rows, :]


def pack_columns(slabs, out_ref):
    lane = lax.broadcasted_iota(jnp.int32, (32, LANES), 1)

    def pack(shift):
        packed = jnp.zeros((32, LANES), jnp.float32)
        for (v, xi), cells_ref in slabs.items():
            first = 8 * v + 2 * xi
            cells = cells_ref[...]
            moved = pltpu.roll(cells, first + shift, axis=1) if first + shift else cells
            packed = jnp.where((lane == first) | (lane == first + 1), moved, packed)
        out_ref[...] = packed

    sec = lax.axis_index("sec")
    pl.when(sec == 0)(lambda: pack(2))
    pl.when(sec == 1)(lambda: pack(0))


def unpack_columns(offered_ref):
    sec = lax.axis_index("sec")
    fx = lax.axis_index("fx")
    last = lax.axis_size("fx") - 1
    rows = [
        offered_ref[2 * jnp.maximum(fx - 1, 0) + 1 - sec] * (fx > 0).astype(jnp.float32),
        offered_ref[2 * fx + 1 - sec],
        offered_ref[2 * jnp.minimum(fx + 1, last) + 1 - sec] * (fx < last).astype(jnp.float32),
        jnp.zeros((8, LANES), jnp.float32),
    ]
    rows = jnp.concatenate(rows, axis=0)

    def place(shape):
        l = lax.broadcasted_iota(jnp.int32, shape, 0)
        xi = (l & 7) >> 1
        neighbour = jnp.where(xi == 0, 0, jnp.where(xi == 3, 2, 1))
        return neighbour, l & 1, 2 * (l >> 3) + 1 - (xi & 1)

    neighbour, column, source = place((LANES, 32))
    row = 8 * neighbour + 2 + 3 * column + (source >> 2)
    here = lax.broadcasted_iota(jnp.int32, (LANES, 32), 1) == row
    here &= lax.broadcasted_iota(jnp.int32, (LANES, 32), 0) < 8 * NV
    lines = product(here.astype(jnp.float32), rows)
    _, _, source = place((LANES, LANES))
    position = lax.broadcasted_iota(jnp.int32, (LANES, LANES), 1)
    lines = jnp.where((position >> 5) == (source & 3), lines, 0.0)
    position = lax.broadcasted_iota(jnp.int32, (32, LANES), 1)
    y = lax.broadcasted_iota(jnp.int32, (32, LANES), 0)
    return product(((position & 31) == y).astype(jnp.float32), lines, axis=1)


def wanted_blocks(offered_ref, peers):
    base = (lax.axis_index("fx") * NB).astype(jnp.float32)
    sec = lax.axis_index("sec")
    targets = [targets_of(offered_ref[2 * peer + sec]) for peer in range(peers)]
    rows = [found[row : row + 1, :] for row in (4, 7) for found in targets for _ in range(2)]
    rows = jnp.concatenate(rows, axis=0)
    lane = lax.broadcasted_iota(jnp.int32, rows.shape, 1)
    here = (lax.broadcasted_iota(jnp.int32, rows.shape, 0) & 1) == lax.axis_index("core")
    asked = (lane & (NB - 1)).astype(jnp.float32) + base == rows
    return (asked & here & (lane < 3 * NB)).astype(jnp.float32)


def second_round_body(
    near_ref, state_ref, far_ref, offered_ref, to_near_ref, to_far_ref, beyond_ref, wanted_ref
):
    beyond_ref[...] = unpack_columns(offered_ref)
    wanted = wanted_blocks(offered_ref, wanted_ref.shape[0] // 4)
    wanted_ref[...] = wanted
    to_near_ref[8 * NV + 8 :, :] = wanted
    last = state_ref.shape[2] - 1

    def put(spot, low, high):
        to_far, to_near = sides("fy", high, low)
        to_near_ref[spot : spot + 1, :] = to_near
        to_far_ref[spot : spot + 1, :] = to_far

    for place in range(2):
        low = slice(place, place + 1)
        high = slice(last - place, last - place + 1)
        for v in range(NV):
            for xi in range(4):
                put(
                    8 * v + 4 * place + xi,
                    slab(near_ref, state_ref, far_ref, v, xi, low),
                    slab(near_ref, state_ref, far_ref, v, xi, high),
                )
        put(8 * NV + place, beyond_ref[low, :], beyond_ref[high, :])
    for out in (to_near_ref, to_far_ref):
        out[8 * NV + 2 : 8 * NV + 8, :] = jnp.zeros((6, LANES), jnp.float32)


def stencil(center, ahead, behind, others, mixed):
    beside = ahead + behind + others
    return DIFFUSION * (beside - 6.0 * center) - TRANSPORT * 0.5 * (ahead - behind) + mixed


def join_halves(own_ref, other_ref, disp_out, vel_out):
    core = lax.axis_index("core")
    first = jnp.where(core == 0, own_ref[...], other_ref[...])
    second = jnp.where(core == 0, other_ref[...], own_ref[...])
    for rows, out in ((slice(0, NB // 2), disp_out), (slice(NB // 2, NB), vel_out)):
        low, high = joined(first[rows], second[rows])
        out[: NB // 2, :] = low
        out[NB // 2 :, :] = high


def fluid_body(
    mixing_ref,
    near_ref,
    state_ref,
    far_ref,
    beyond_ref,
    to_near_ref,
    to_far_ref,
    from_near_ref,
    from_far_ref,
    own_ref,
    other_ref,
    out_ref,
    part_ref,
    disp_out,
    vel_out,
    field,
    section,
    packed,
    edge_ref,
):
    join_halves(own_ref, other_ref, disp_out, vel_out)
    rows = 8 * NV + 8
    top, bottom = sides("fy", to_near_ref[:rows, :], to_far_ref[...])
    before, after = sides("fy", from_near_ref[:rows, :], from_far_ref[...])
    beyond = beyond_ref[...]
    pack_columns({(v, xi): state_ref.at[v, xi - 1] for v in range(NV) for xi in (1, 2)}, edge_ref)
    size = state_ref.shape[2]
    end = TOP + size
    sec = lax.axis_index("sec")
    fx = lax.axis_index("fx")
    fy = 2 * lax.axis_index("z") + lax.axis_index("core")
    inside_low = (fx > 0).astype(jnp.float32)
    inside_high = (fx < lax.axis_size("fx") - 1).astype(jnp.float32)
    inside_before = (fy > 0).astype(jnp.float32)
    inside_after = (fy < 2 * lax.axis_size("z") - 1).astype(jnp.float32)
    mix = [[mixing_ref[v, w] for w in range(NV)] for v in range(NV)]

    lane = lax.broadcasted_iota(jnp.int32, (1, LANES), 1)
    open_lane = (LANES - 1) * (1 - sec)
    keep_low = (lane != 0).astype(jnp.float32)
    keep_high = (lane != LANES - 1).astype(jnp.float32)
    at_open = (lane == open_lane).astype(jnp.float32)

    def along_z(cells, columns, v, xi):
        moved = pltpu.roll(columns, LANES - 1 - (8 * v + 2 * xi), axis=1)
        return (
            keep_low * pltpu.roll(cells, 1, axis=1)
            + keep_high * pltpu.roll(cells, LANES - 1, axis=1)
            + at_open * moved
        )

    def mixed(cells, v):
        total = mix[v][0] * cells[0]
        for w in range(1, NV):
            total = total + mix[v][w] * cells[w]
        return total

    packed[TOP:end, :] = beyond
    packed[TOP - 1 : TOP, :] = before[8 * NV : 8 * NV + 1, :]
    packed[end : end + 1, :] = after[8 * NV : 8 * NV + 1, :]
    group = lane // 8
    mixed_columns = jnp.zeros((size, LANES), jnp.float32)
    for shift in range(1 - NV, NV):
        factor = jnp.zeros((1, LANES), jnp.float32)
        for v in range(NV):
            if 0 <= v - shift < NV:
                factor = jnp.where(group == v, mix[v][v - shift], factor)
        source = beyond if shift == 0 else pltpu.roll(beyond, (8 * shift) % LANES, axis=1)
        mixed_columns = mixed_columns + factor * source
    column_rate = stencil(
        beyond,
        pltpu.roll(beyond, LANES - 2, axis=1),
        pltpu.roll(beyond, 2, axis=1),
        packed[TOP - 1 : end - 1, :]
        + packed[TOP + 1 : end + 1, :]
        + pltpu.roll(beyond + edge_ref[...], 1 + (LANES - 2) * (1 - sec), axis=1),
        mixed_columns,
    )
    column_section = beyond + TIME_STEP * column_rate

    row = lax.broadcasted_iota(jnp.int32, (8, LANES), 0)
    inside_rows = jnp.where(row < 4, inside_before, inside_after)
    row_cells = []
    row_others = []
    row_columns = jnp.where(
        row < 4, before[8 * NV : 8 * NV + 1, :], after[8 * NV : 8 * NV + 1, :]
    )
    for v in range(NV):
        cells = jnp.concatenate(
            [before[8 * v : 8 * v + 4, :], after[8 * v : 8 * v + 4, :]], axis=0
        )
        outer = jnp.concatenate(
            [before[8 * v + 4 : 8 * v + 8, :], after[8 * v + 4 : 8 * v + 8, :]], axis=0
        )
        inner = jnp.concatenate(
            [top[8 * v : 8 * v + 4, :], bottom[8 * v : 8 * v + 4, :]], axis=0
        )
        columns = jnp.zeros((8, LANES), jnp.float32)
        for xi in (1, 2):
            moved = pltpu.roll(row_columns, LANES - 1 - (8 * v + 2 * xi), axis=1)
            columns = jnp.where((row == xi) | (row == 4 + xi), moved, columns)
        across = (
            keep_low * pltpu.roll(cells, 1, axis=1)
            + keep_high * pltpu.roll(cells, LANES - 1, axis=1)
            + at_open * columns
        )
        row_cells.append(cells)
        row_others.append(outer + inner + across)
    for v in range(NV):
        cells = row_cells[v]
        rate = stencil(
            cells,
            pltpu.roll(cells, 7, axis=0),
            pltpu.roll(cells, 1, axis=0),
            row_others[v],
            mixed(row_cells, v),
        )
        later = inside_rows * (cells + TIME_STEP * rate)
        for xi in (1, 2):
            section[v, xi, TOP - 1 : TOP, :] = later[xi : xi + 1, :]
            section[v, xi, end : end + 1, :] = later[4 + xi : 5 + xi, :]

    for v in range(NV):
        for xi in range(4):
            field[v, xi, TOP:end, :] = slab(near_ref, state_ref, far_ref, v, xi)
            field[v, xi, TOP - 1 : TOP, :] = before[8 * v + xi : 8 * v + xi + 1, :]
            field[v, xi, end : end + 1, :] = after[8 * v + xi : 8 * v + xi + 1, :]

    def center(v, x):
        if x < 0 or x > 3:
            return slab(near_ref, state_ref, far_ref, v, x)
        return field[v, x, TOP:end, :]

    for xi in range(4):
        cells = [center(w, xi) for w in range(NV)]
        for v in range(NV):
            others = (
                field[v, xi, TOP - 1 : end - 1, :]
                + field[v, xi, TOP + 1 : end + 1, :]
                + along_z(cells[v], beyond, v, xi)
            )
            rate = stencil(
                cells[v], center(v, xi + 1), center(v, xi - 1), others, mixed(cells, v)
            )
            later = cells[v] + TIME_STEP * rate
            if xi == 0:
                later = inside_low * later
            if xi == 3:
                later = inside_high * later
            section[v, xi, TOP:end, :] = later
            if xi in (1, 2):
                out_ref[v, xi - 1] = cells[v] + 0.5 * TIME_STEP * rate

    for xi in (1, 2):
        cells = [section[w, xi, TOP:end, :] for w in range(NV)]
        for v in range(NV):
            others = (
                section[v, xi, TOP - 1 : end - 1, :]
                + section[v, xi, TOP + 1 : end + 1, :]
                + along_z(cells[v], column_section, v, xi)
            )
            rate = stencil(
                cells[v],
                section[v, xi + 1, TOP:end, :],
                section[v, xi - 1, TOP:end, :],
                others,
                mixed(cells, v),
            )
            final = out_ref[v, xi - 1] + 0.5 * TIME_STEP * rate
            out_ref[v, xi - 1] = final
            if v == 2:
                part_ref[xi - 1] = final[:8, :]


def shards(
    state, mixing, wall_weight, patch_map, block_map, shell_disp, shell_vel, connect, stiffness
):
    nfx, nfy, nsec = (lax.axis_size(axis) for axis in ("fx", FY, "sec"))
    near_x, far_x, near_y, far_y = (
        [pair for i in range(first, n - 1, 2) for pair in ((i, i + 1), (i + 1, i))]
        for n in (nfx, nfy)
        for first in (0, 1)
    )

    offered = offer(
        patch_map.reshape(2), block_map.reshape(2), wall_weight, state, nfx * nsec
    )
    offered = lax.all_to_all(offered, ("fx", "sec"), 0, 0, tiled=True)
    near = lax.ppermute(state, "fx", near_x)
    far = lax.ppermute(state, "fx", far_x)

    partial = kernel_call(collect_body, f32(nfy, NB // 2, LANES), [VM])(offered)
    loads = lax.all_to_all(partial, ("core", "z"), 0, 0, tiled=True)

    block = f32(NB, LANES)
    couple, disp, vel, weight = kernel_call(
        couple_body,
        (f32(NB, NB, LANES), block, block, f32(*wall_weight.shape)),
        [VM] * 5,
    )(
        connect[0].T,
        stiffness[0],
        shell_disp.reshape(NB, LANES),
        shell_vel.reshape(NB, LANES),
        wall_weight,
    )
    span = f32(8 * NV + 8, LANES)
    to_near, to_far, beyond, wanted = kernel_call(
        second_round_body,
        (f32(8 * NV + 8 + 4 * nfx, LANES), span, f32(32, LANES), f32(4 * nfx, LANES)),
        [VM] * 4,
        cost=LONG,
    )(near, state, far, offered)
    from_near = lax.ppermute(to_near, FY, near_y)
    from_far = lax.ppermute(to_far, FY, far_y)

    own, walls = kernel_call(
        shell_body, (f32(NB, LANES), f32(2 * nfx, LANES)), [VM] * 6
    )(loads, wanted, from_near, couple, disp, vel)
    walls = lax.all_to_all(walls, ("fx", "core"), 0, 0, tiled=True)
    other = lax.ppermute(own, FY, near_y)

    fluid, part, new_disp, new_vel = kernel_call(
        fluid_body,
        (f32(*state.shape), f32(2, 8, LANES), block, block),
        [SM] + [VM] * 10,
        scratch=[
            pltpu.VMEM((NV, 4, ROWS, LANES), jnp.float32),
            pltpu.VMEM((NV, 4, ROWS, LANES), jnp.float32),
            pltpu.VMEM((ROWS, LANES), jnp.float32),
            pltpu.VMEM((32, LANES), jnp.float32),
        ],
        cost=LONG,
    )(mixing, near, state, far, beyond, to_near, to_far, from_near, from_far, own, other)
    new_state = finish(walls, weight, part, fluid)
    return (new_state, new_disp.reshape(1, -1), new_vel.reshape(1, -1))


def solution(mesh):
    nfx, nfy, nsec = mesh.devices.shape
    mesh = jax.sharding.Mesh(
        mesh.devices.reshape(nfx, nfy // 2, 2, nsec), ("fx", "z", "core", "sec")
    )
    return jax.shard_map(
        shards,
        mesh=mesh,
        in_specs=(
            P(None, "fx", FY, "sec"),
            P(),
            P("fx", FY, "sec"),
            P("fx", FY, "sec", None),
            P("fx", FY, "sec", None),
            P("fx", None),
            P("fx", None),
            P("fx", None, None),
            P("fx", None, None),
        ),
        out_specs=(P(None, "fx", FY, "sec"), P("fx", None), P("fx", None)),
        check_vma=False,
    )
```
